32 devices in a mesh: expert: 8 (over z, y), tensor: 4 (over x, core).
Axes of the slice: x: 2, y: 2, z: 4, core: 2. Of those that a mesh axis runs over, the one named last changes fastest.
Arguments:
- tokens: bfloat16 [16384, 768], P('expert'), may hold values from -6 to 6
- lengths: int32 [8, 8], P('expert'), may hold values from 1 to 512, 2048 in all within a row
- routes: int32 [16384, 2], P(('expert', 'tensor')), may hold values from 0 to 7, all different within a row; in each aligned block of 512 rows (0 to 511, 512 to 1023, ...) at most 256 rows name the same one
- norm1_gain: float32 [768], replicated, may hold values from 0.25 to 1.75
- attn_qkv: bfloat16 [768, 3, 768], P(None, None, 'tensor'), may hold values from -0.21875 to 0.21875
- attn_out: bfloat16 [768, 768], P('tensor'), may hold values from -0.875 to 0.875
- rel_bias: float32 [12, 128], P('tensor'), may hold values from -3 to 3
- norm2_gain: float32 [768], replicated, may hold values from 0.25 to 1.75
- router: bfloat16 [768, 8], replicated, may hold values from -0.15625 to 0.15625
- expert_in: bfloat16 [8, 768, 3072], P('expert', None, 'tensor'), may hold values from -0.21875 to 0.21875
- expert_out: bfloat16 [8, 3072, 768], P('expert', 'tensor'), may hold values from -0.109375 to 0.109375
- out_grad: bfloat16 [16384, 768], P(('expert', 'tensor')), may hold values from -6 to 6
Outputs:
- output: float32 [16384, 768], P(('expert', 'tensor'))
- grad_tokens: float32 [16384, 768], P(('expert', 'tensor'))
- grad_norm1_gain: float32 [768], P('tensor')
- grad_attn_qkv: float32 [768, 3, 768], P(None, None, 'tensor')
- grad_attn_out: float32 [768, 768], P('tensor')
- grad_rel_bias: float32 [12, 128], P('tensor')
- grad_norm2_gain: float32 [768], P('tensor')
- grad_router: float32 [768, 8], P('tensor')
- grad_expert_in: float32 [8, 768, 3072], P('expert', None, 'tensor')
- grad_expert_out: float32 [8, 3072, 768], P('expert', 'tensor')
The draws below stay inside these ranges and needn't reach their ends.
Inputs may be any that keep to these rules, and one draw needn't show every extreme that they name: Row g gives in order the lengths of the sequences that fill group g; each row sums to 2048 and its longest is exactly 512. `routes`: each token names two different experts. Within each aligned block of 512 tokens no expert is named more than 256 times, and in some block one expert is named exactly 256 times.
All inputs are finite; a program needn't handle non-finite values.
Results may differ from the reference program's by a relative error of at most 0.025.
Values may be sent and summed in bfloat16 or wider, within the bound.
No kernel may reach another device: no remote copies, remote signals or barrier semaphores. Data moves between devices by JAX's collectives and lax.ppermute only.
A program may use at most 320 MiB of HBM per device.

```python
import math
import jax
import jax.numpy as jnp
import numpy as np
from jax import lax

D = 768
H = 12
HD = 64
FF = 3072
EXPERTS = 8
ROWS_DEV = 512
TOK_GRP = 2048
TOKENS = 16384
SEQ_MOST = 512
SEQ_SLOTS = 8
NB = 128
CAP = 256
N_EXPERT = 8


def shard_levels(own_key, dims, pieces, smallest, high):
    loudness = 1.0
    for dim, shards_of in pieces:
        steps = jax.random.uniform(jax.random.fold_in(jax.random.fold_in(own_key, 6), dim), (shards_of,), jnp.float32, smallest / len(pieces), high / len(pieces))
        loudness = loudness * jnp.repeat(jnp.exp(steps), dims[dim] // shards_of).reshape((-1,) + (1,) * (len(dims) - 1 - dim))
    return loudness


def profile(count, total, bound, slope):
    loads = [(1 << 20) // math.isqrt(grade ** slope) + 1 for grade in range(2, count + 1)]
    rest, given = total - bound - (count - 1), [1] * (count - 1)
    while rest > 0:
        free = [i for i in range(count - 1) if given[i] < bound]
        mass, left = sum([loads[i] for i in free]), rest
        for i in free:
            more = min(bound - given[i], max(1, left * loads[i] // mass), rest)
            given[i] = given[i] + more
            rest = rest - more
    return np.array([bound] + given)


def ragged(rng, number_of, total, reach, lean):
    if number_of == 2:
        one = jax.random.randint(rng, (), max(1, total - reach), min(reach, total - 1) + 1)
        return jnp.stack([one, total - one])
    sizes = jnp.asarray(profile(number_of, total, reach, lean), jnp.int32)
    pairs = (number_of - 1) // 2
    donor, taker = sizes[1:1 + 2 * pairs:2], sizes[2:2 + 2 * pairs:2]
    margin = jnp.minimum(donor - 1, reach - taker)
    passed = jax.random.randint(jax.random.fold_in(rng, 1), (pairs,), 0, 1 << 20) % (margin + 1)
    sizes = sizes.at[1:1 + 2 * pairs:2].set(donor - passed).at[2:2 + 2 * pairs:2].set(taker + passed)
    return sizes[jax.random.permutation(jax.random.fold_in(rng, 2), number_of)]


def routed_block(rng, own, number, rows, number_of, top, most, skew):
    sequence = jax.random.permutation(rng, number_of)
    heavy_load, common = shares(number_of, rows * top, most, skew, True), shares(number_of, rows * top, most, skew, False)
    places = jnp.arange(number_of)

    def named(sizes, rotation):
        used = int((sizes > 0).sum())
        fixed = max(1, used // 4)
        moved = fixed + (places - fixed + rotation * (used - fixed)) % max(1, number_of - fixed)
        return jnp.zeros((number_of,), jnp.int32).at[sequence[jnp.where(places < fixed, places, moved)]].set(jnp.asarray(sizes, jnp.int32))

    sizes = jnp.where(number % 4 == 0, named(heavy_load, number // 4), named(common, number - number // 4 - 1))
    mixed = jax.random.permutation(jax.random.fold_in(own, 3), number_of)
    source_of, taker = mixed[0:number_of // 2 * 2:2], mixed[1:number_of // 2 * 2:2]
    room = jnp.minimum(sizes[source_of] - 1, most - sizes[taker]) // 2
    room = jnp.where((source_of == sequence[0]) | (taker == sequence[0]) | (sizes[taker] == 0), 0, jnp.maximum(room, 0))
    moved = jax.random.randint(jax.random.fold_in(own, 4), (number_of // 2,), 0, 1 << 20) % (room + 1)
    sizes = sizes.at[source_of].add(-moved).at[taker].add(moved)
    items = jnp.searchsorted(jnp.cumsum(sizes), jnp.arange(rows * top), side="right").astype(jnp.int32)
    grid = items.reshape(top, rows).T
    grid = grid[jax.random.permutation(jax.random.fold_in(own, 1), rows)]
    rotation = jax.random.randint(jax.random.fold_in(own, 2), (rows, 1), 0, top)
    return jnp.take_along_axis(grid, (jnp.arange(top)[None, :] + rotation) % top, axis=1)


def shares(count, total, bound, lean, full):
    portions = [(1 << 20) // math.isqrt(rank ** lean) + 1 for rank in range(1, count + 1)]
    largest = bound if full else min(bound, max(-(-total // count), total * portions[0] // sum(portions)))
    least = 1 if total - largest >= count - 1 else 0
    holding, surplus = [largest] + [least] * (count - 1), total - largest - least * (count - 1)
    while surplus > 0:
        candidates = [i for i in range(1, count) if holding[i] < largest] or [i for i in range(1, count) if holding[i] < bound]
        mass, budget = sum([portions[i] for i in candidates]), surplus
        for i in candidates:
            extra = min(bound - holding[i], max(1, budget * portions[i] // mass), surplus)
            holding[i] = holding[i] + extra
            surplus = surplus - extra
    return np.array(holding)


def normal_values(rng, dims, width, most, shards=(), kind=jnp.bfloat16):
    drawn = jax.random.normal(rng, dims, jnp.float32) * width
    if len(shards) > 0:
        drawn = shard_levels(rng, dims, shards, -0.22, 0.18) * drawn
    return jnp.clip(drawn, min=-most, max=most).astype(kind)


def setup_inputs(seed: int = 0) -> dict:
    streams_of = jax.random.split(jax.random.key(seed), 13)
    tokens = normal_values(streams_of[0], (TOKENS, D), 1.0, 6.0, ((0, 8),))
    lengths = jax.vmap(lambda own: ragged(own, SEQ_SLOTS, TOK_GRP, SEQ_MOST, 2))(jax.random.split(streams_of[1], N_EXPERT)).reshape((N_EXPERT, SEQ_SLOTS)).astype(jnp.int32)
    routes_keys = jax.random.split(jax.random.fold_in(streams_of[2], 1), TOKENS // ROWS_DEV)
    routes_turns = jax.random.permutation(jax.random.fold_in(streams_of[2], 3), TOKENS // ROWS_DEV)
    routes = jax.vmap(lambda own, number: routed_block(jax.random.fold_in(streams_of[2], 2), own, number, ROWS_DEV, EXPERTS, 2, CAP, 2))(routes_keys, routes_turns).reshape((TOKENS, 2))
    norm1_gain = jnp.clip(1.0 + 0.15 * jax.random.normal(streams_of[3], (D,), jnp.float32), 0.25, 1.75)
    attn_qkv = normal_values(streams_of[4], (D, 3, H * HD), D ** -0.5, 0.21875, ((2, 4),))
    attn_out = normal_values(streams_of[5], (H * HD, D), (H * HD // 16) ** -0.5, 0.875, ((0, 4),))
    rel_bias = normal_values(streams_of[6], (H, NB), 0.5, 3.0, ((0, 4),), jnp.float32)
    norm2_gain = jnp.clip(1.0 + 0.15 * jax.random.normal(streams_of[7], (D,), jnp.float32), 0.25, 1.75)
    router = normal_values(streams_of[8], (D, EXPERTS), (2 * D) ** -0.5, 0.15625)
    expert_in = normal_values(streams_of[9], (EXPERTS, D, FF), D ** -0.5, 0.21875, ((0, 8), (2, 4)))
    expert_out = normal_values(streams_of[10], (EXPERTS, FF, D), FF ** -0.5, 0.109375, ((0, 8), (1, 4)))
    out_grad = normal_values(streams_of[11], (TOKENS, D), 1.0, 6.0, ((0, 32),))
    return {"tokens": tokens, "lengths": lengths, "routes": routes, "norm1_gain": norm1_gain, "attn_qkv": attn_qkv, "attn_out": attn_out, "rel_bias": rel_bias, "norm2_gain": norm2_gain, "router": router, "expert_in": expert_in, "expert_out": expert_out, "out_grad": out_grad}


EPSILON = 1e-06
PRECISE = lax.Precision.HIGHEST

@jax.custom_vjp
def low(v):
    return lax.optimization_barrier(v.astype(jnp.bfloat16)).astype(jnp.float32)

@jax.custom_vjp
def low_back(v):
    return v

def low_keep(v):
    return (low(v), None)

def low_pass(kept, grad):
    return (grad,)

def back_keep(v):
    return (v, None)

def back_low(kept, grad):
    return (low(grad),)
low.defvjp(low_keep, low_pass)
low_back.defvjp(back_keep, back_low)

def rms_norm(values, gain):
    return values * lax.rsqrt(lax.optimization_barrier(jnp.mean(values * values, axis=-1, keepdims=True)) + EPSILON) * gain

def gelu_tanh(values):
    return 0.5 * values * (1.0 + jnp.tanh(0.7978845608028654 * (values + 0.044715 * values * values * values)))

def matmul(left, right):
    return jnp.dot(left, right, precision=PRECISE, preferred_element_type=jnp.float32)

def reference(tokens, lengths, routes, norm1_gain, attn_qkv, attn_out, rel_bias, norm2_gain, router, expert_in, expert_out, out_grad):
    ends = jnp.cumsum(lengths, axis=1).astype(jnp.int32)
    positions = jnp.arange(TOK_GRP, dtype=jnp.int32)
    segment = lax.optimization_barrier(jnp.sum((positions[None, :, None] >= ends[:, None, :]).astype(jnp.int32), axis=2)).astype(jnp.int32)
    distance = positions[:, None] - positions[None, :]
    causal = distance >= 0
    bucket = jnp.clip(distance, 0, NB - 1).astype(jnp.int32)
    block_total = TOKENS // ROWS_DEV
    blocked_routes = routes.reshape(block_total, ROWS_DEV, 2)
    route_hot = (blocked_routes[..., None] == jnp.arange(EXPERTS, dtype=jnp.int32)).astype(jnp.int32)
    counts = lax.optimization_barrier(jnp.sum(route_hot, axis=2))
    before = jnp.cumsum(counts, axis=1).astype(jnp.int32) - counts
    slot_rank = lax.optimization_barrier(jnp.sum(route_hot * before[:, :, None, :], axis=3)).astype(jnp.int32)
    block_base = jnp.arange(block_total, dtype=jnp.int32)[:, None, None] * EXPERTS
    slot_index = ((block_base + blocked_routes) * CAP + slot_rank).reshape(TOKENS, 2).astype(jnp.int32)
    token_ids = jnp.broadcast_to(jnp.arange(TOKENS, dtype=jnp.int32)[:, None], (TOKENS, 2))
    slot_owner = jnp.full((block_total * EXPERTS * CAP,), TOKENS, jnp.int32).at[slot_index.reshape(-1)].set(token_ids.reshape(-1))
    token_hot = (routes[..., None] == jnp.arange(EXPERTS, dtype=jnp.int32)).astype(jnp.float32)
    scale = HD ** (-0.5)

    def forward(widened, gain_one, weight_qkv, weight_out, bias_table, gain_two, weight_router, weight_in, weight_down):
        hidden_one = low(rms_norm(widened, gain_one))
        projected = low_back(low(matmul(hidden_one, weight_qkv.reshape(D, 3 * H * HD))))
        projected = projected.reshape(N_EXPERT, TOK_GRP, 3, H, HD)

        def group_attend(packed):
            group_proj, group_seg = packed
            queries = group_proj[:, 0]
            keys = group_proj[:, 1]
            values = group_proj[:, 2]
            scores = jnp.einsum('ihd,jhd->hij', queries, keys, precision=PRECISE) * scale + bias_table[:, bucket]
            scores = low_back(scores)
            allowed = causal & (group_seg[:, None] == group_seg[None, :])
            probs = jax.nn.softmax(jnp.where(allowed[None], scores, -1e+30), axis=-1)
            mixed = jnp.einsum('hij,jhd->ihd', low(probs), values, precision=PRECISE)
            return low_back(low(mixed)).reshape(TOK_GRP, H * HD)
        attention = lax.map(jax.checkpoint(group_attend), (projected, segment)).reshape(TOKENS, H * HD)
        branch = low_back(matmul(attention, weight_out))
        resid = widened + branch
        hidden_two = low(rms_norm(resid, gain_two))
        logits = low_back(matmul(hidden_two, weight_router))
        chosen_logit = lax.optimization_barrier(jnp.sum(token_hot * logits[:, None, :], axis=-1))
        gate_vals = jax.nn.softmax(chosen_logit, axis=-1)
        padded = jnp.concatenate([hidden_two, jnp.zeros((1, D), jnp.float32)], axis=0)
        sent = low_back(padded[slot_owner])
        expert_rows = sent.reshape(block_total, EXPERTS, CAP, D).transpose(1, 0, 2, 3).reshape(EXPERTS, block_total * CAP, D)

        def expert_ffn(packed):
            rows_here, first_weight, second_weight = packed
            pre = low_back(matmul(rows_here, first_weight))
            act = low(gelu_tanh(pre))
            return low_back(low(matmul(act, second_weight)))
        returned = lax.map(jax.checkpoint(expert_ffn), (expert_rows, weight_in, weight_down))
        flat_returned = returned.reshape(EXPERTS, block_total, CAP, D).transpose(1, 0, 2, 3).reshape(-1, D)
        picked = flat_returned[slot_index]
        return resid + lax.optimization_barrier(jnp.sum(gate_vals[:, :, None] * picked, axis=1))
    output, pull = jax.vjp(forward, tokens.astype(jnp.float32), norm1_gain.astype(jnp.float32), attn_qkv.astype(jnp.float32), attn_out.astype(jnp.float32), rel_bias.astype(jnp.float32), norm2_gain.astype(jnp.float32), router.astype(jnp.float32), expert_in.astype(jnp.float32), expert_out.astype(jnp.float32))
    grads = pull(out_grad.astype(jnp.float32))
    return (output, grads[0], grads[1], grads[2], grads[3], grads[4], grads[5], grads[6], grads[7], grads[8])
```

```python
import jax
import jax.numpy as jnp
from jax import lax
from jax.sharding import PartitionSpec as P

QBLK = 512


EPSILON = 1e-06
BLOCKED = -1e30
PRECISE = lax.Precision.HIGHEST


def rms_norm(values, gain):
    return values * lax.rsqrt(jnp.mean(values * values, axis=-1, keepdims=True) + EPSILON) * gain


def gelu_tanh(values):
    return (
        0.5
        * values
        * (1.0 + jnp.tanh(0.7978845608028654 * (values + 0.044715 * values * values * values)))
    )


def contract_rows(left, right):
    return lax.dot_general(
        left, right, (((0,), (0,)), ((), ())), preferred_element_type=jnp.float32
    )


def contract_cols(left, right):
    return lax.dot_general(
        left, right, (((1,), (1,)), ((), ())), preferred_element_type=jnp.float32
    )


def fold_keys(pieces, block):
    later = pieces[:, block:]
    earlier = pieces[:, :block]
    shifted = jnp.concatenate([earlier[1:], jnp.zeros_like(earlier[:1])], axis=0)
    return (later + shifted).reshape(-1, pieces.shape[2] * pieces.shape[3])


def spread_diag(vector, block):
    head_count, diag_span = vector.shape
    repeated = jnp.tile(vector, (1, block))
    trimmed = repeated[:, block : block + block * (diag_span - 1)].reshape(
        head_count, block, diag_span - 1
    )
    return trimmed[:, :, : 2 * block]


def fold_diag(matrix, block, diag_span):
    head_count = matrix.shape[0]
    padded_mat = jnp.pad(matrix, ((0, 0), (0, 0), (0, diag_span - 1 - 2 * block)))
    flattened = jnp.pad(padded_mat.reshape(head_count, -1), ((0, 0), (block, 0)))
    return jnp.sum(flattened.reshape(head_count, block, diag_span), axis=1)


def local(
    tokens,
    lengths,
    routes,
    norm1_gain,
    attn_qkv,
    attn_out,
    rel_bias,
    norm2_gain,
    router,
    expert_in,
    expert_out,
    out_grad,
):
    n_expert = lax.axis_size("expert")
    group_rows, width = tokens.shape
    groups_here, seq_slots = lengths.shape
    group_len = group_rows // groups_here
    own_rows = routes.shape[0]
    inner_width = attn_out.shape[0]
    head_count, bucket_count = rel_bias.shape
    head_dim = inner_width // head_count
    expert_count = router.shape[1]
    capacity = max(2, 4 * own_rows // expert_count)
    block = QBLK
    block_count = group_rows // block
    scale = head_dim ** (-0.5)
    own_first = lax.axis_index("tensor") * own_rows
    def exchange(rows):
        return lax.all_to_all(
            rows.reshape(n_expert, -1, rows.shape[-1]), "expert", split_axis=0, concat_axis=0, tiled=True
        ).reshape(rows.shape)

    route_hot = (routes[:, :, None] == jnp.arange(expert_count, dtype=jnp.int32)).astype(jnp.int32)
    counts = jnp.sum(route_hot, axis=1)
    before = jnp.cumsum(counts, axis=0) - counts
    slot_rank = jnp.sum(route_hot * before[:, None, :], axis=-1)
    slot_index = routes * capacity + slot_rank
    slot_ids = jnp.arange(expert_count * capacity, dtype=jnp.int32)
    slot_hot = (slot_index[:, :, None] == slot_ids[None, None, :]).astype(jnp.bfloat16)
    dispatch = slot_hot[:, 0] + slot_hot[:, 1]
    other_ids = jnp.sum(
        jnp.where(slot_index[:, :, None] == slot_ids[None, None, :], routes[:, ::-1, None] + 1, 0),
        axis=(0, 1),
    )
    other_here = lax.all_to_all(
        other_ids.reshape(n_expert, -1), "expert", split_axis=0, concat_axis=0, tiled=True
    ).reshape(-1)
    grad_rows = exchange(contract_rows(dispatch, out_grad).astype(jnp.bfloat16))
    weights_in = lax.all_gather(expert_in[0], "tensor")
    weights_out = lax.all_gather(expert_out[0], "tensor")
    widened = tokens.astype(jnp.float32)
    normed_one, norm1_pull = jax.vjp(rms_norm, widened, norm1_gain)
    hidden_one = normed_one.astype(jnp.bfloat16)
    projected = jnp.einsum(
        "td,dcf->tcf", hidden_one, attn_qkv, preferred_element_type=jnp.float32
    ).astype(jnp.bfloat16)
    queries = projected[:, 0].reshape(group_rows, head_count, head_dim)
    zero_rows = jnp.zeros((block, head_count, head_dim), jnp.bfloat16)
    keys_pad = jnp.concatenate(
        [zero_rows, projected[:, 1].reshape(group_rows, head_count, head_dim)], axis=0
    )
    values_pad = jnp.concatenate(
        [zero_rows, projected[:, 2].reshape(group_rows, head_count, head_dim)], axis=0
    )
    ends = jnp.cumsum(lengths, axis=1)
    positions = jnp.arange(group_rows, dtype=jnp.int32)
    group_of = positions // group_len
    local_pos = positions - group_of * group_len
    group_hot = (group_of[:, None] == jnp.arange(groups_here, dtype=jnp.int32)[None, :]).astype(
        jnp.int32
    )
    row_ends = jnp.sum(group_hot[:, :, None] * ends[None, :, :], axis=1)
    segment = group_of * seq_slots + jnp.sum(
        (local_pos[:, None] >= row_ends).astype(jnp.int32), axis=1
    )
    segment_pad = jnp.concatenate([jnp.full((block,), -1, jnp.int32), segment], axis=0)
    distance = (
        jnp.arange(block, dtype=jnp.int32)[:, None]
        - jnp.arange(2 * block, dtype=jnp.int32)[None, :]
        + block
    )
    causal = distance >= 0
    diag_span = 3 * block
    offsets = jnp.arange(diag_span, dtype=jnp.int32)
    spot_hot = (
        jnp.clip(2 * block - offsets, 0, bucket_count - 1)[:, None]
        == jnp.arange(bucket_count, dtype=jnp.int32)[None, :]
    ).astype(jnp.float32)
    diag_bias = jnp.dot(rel_bias, spot_hot.T, precision=PRECISE, preferred_element_type=jnp.float32)
    bias_block = spread_diag(diag_bias, block)

    def block_scores(index):
        first_row = index * block
        query_blk = lax.dynamic_slice_in_dim(queries, first_row, block, 0)
        key_blk = lax.dynamic_slice_in_dim(keys_pad, first_row, 2 * block, 0)
        value_blk = lax.dynamic_slice_in_dim(values_pad, first_row, 2 * block, 0)
        seg_query = lax.dynamic_slice_in_dim(segment, first_row, block, 0)
        seg_key = lax.dynamic_slice_in_dim(segment_pad, first_row, 2 * block, 0)
        allowed = causal & (seg_query[:, None] == seg_key[None, :])
        scores = (
            jnp.einsum("ahd,chd->hac", query_blk, key_blk, preferred_element_type=jnp.float32)
            * scale
            + bias_block
        )
        return (query_blk, key_blk, value_blk, allowed, scores)

    def attend(index):
        query_blk, key_blk, value_blk, allowed, scores = block_scores(index)
        masked = jnp.where(allowed[None], scores, BLOCKED)
        peak = jnp.max(masked, axis=-1, keepdims=True)
        raised = jnp.exp(masked - peak)
        total = jnp.sum(raised, axis=-1, keepdims=True)
        weights = (raised / total).astype(jnp.bfloat16)
        mixed = jnp.einsum(
            "hac,chd->ahd", weights, value_blk, preferred_element_type=jnp.float32
        ).astype(jnp.bfloat16)
        return (mixed, (peak + jnp.log(total))[:, :, 0])

    mixed_blocks, log_totals = lax.map(attend, jnp.arange(block_count, dtype=jnp.int32))
    attention = mixed_blocks.reshape(group_rows, inner_width)
    branch = lax.psum_scatter(
        jnp.dot(attention, attn_out, preferred_element_type=jnp.float32).astype(jnp.bfloat16),
        "tensor",
        scatter_dimension=0,
        tiled=True,
    ).astype(jnp.float32)
    resid = lax.dynamic_slice_in_dim(widened, own_first, own_rows, 0) + branch
    normed_two, norm2_pull = jax.vjp(rms_norm, resid, norm2_gain)
    hidden_two = normed_two.astype(jnp.bfloat16)
    outgoing = contract_rows(dispatch, hidden_two).astype(jnp.bfloat16)
    expert_rows = exchange(outgoing)
    pre = jnp.einsum("sd,jdf->jsf", expert_rows, weights_in, preferred_element_type=jnp.float32)
    act_value, gelu_pull = jax.vjp(gelu_tanh, pre)
    act = act_value.astype(jnp.bfloat16)
    slot_logits = jnp.dot(expert_rows, router, preferred_element_type=jnp.float32)
    own_hot = (jnp.arange(expert_count, dtype=jnp.int32) == lax.axis_index("expert")).astype(
        jnp.float32
    )
    other_hot = (other_here[:, None] == jnp.arange(1, expert_count + 1, dtype=jnp.int32)).astype(
        jnp.float32
    )
    hot_gap = own_hot[None, :] - other_hot
    logit_gap = jnp.sum(hot_gap * slot_logits, axis=-1, keepdims=True)
    gate = 1.0 / (1.0 + jnp.exp(-logit_gap))
    other_gate = 1.0 / (1.0 + jnp.exp(logit_gap))
    act_grads = jnp.einsum("sd,jfd->jsf", grad_rows, weights_out, preferred_element_type=jnp.float32)
    gate_grads = jnp.sum(act_value * act_grads, axis=(0, 2))[:, None]
    grad_logits = (gate * other_gate * gate_grads * hot_gap).astype(jnp.bfloat16)
    grad_pre = gelu_pull(gate[None] * act_grads)[0].astype(jnp.bfloat16)
    grad_sent = exchange(
        (
            jnp.einsum("jsf,jdf->sd", grad_pre, weights_in, preferred_element_type=jnp.float32)
            + contract_cols(grad_logits, router)
        ).astype(jnp.bfloat16)
    )
    result = (
        gate * jnp.einsum("jsf,jfd->sd", act, weights_out, preferred_element_type=jnp.float32)
    ).astype(jnp.bfloat16)
    came_back = exchange(result)
    output = resid + jnp.dot(dispatch, came_back, preferred_element_type=jnp.float32)
    router_part = contract_rows(expert_rows, grad_logits)
    gated_rows = (gate * grad_rows.astype(jnp.float32)).astype(jnp.bfloat16)
    grad_w_out = jnp.einsum("jsf,sd->jfd", act, gated_rows, preferred_element_type=jnp.float32)
    grad_w_in = jnp.einsum("sd,jsf->jdf", expert_rows, grad_pre, preferred_element_type=jnp.float32)
    grad_w_out = lax.psum_scatter(
        grad_w_out.astype(jnp.bfloat16), "tensor", scatter_dimension=0
    ).astype(jnp.float32)[None]
    grad_w_in = lax.psum_scatter(
        grad_w_in.astype(jnp.bfloat16), "tensor", scatter_dimension=0
    ).astype(jnp.float32)[None]
    grad_in = out_grad.astype(jnp.float32)
    grad_hidden_two = jnp.dot(dispatch, grad_sent, preferred_element_type=jnp.float32)
    grad_resid_norm, gain_two_part = norm2_pull(grad_hidden_two)
    grad_resid = grad_in + grad_resid_norm
    grad_branch = lax.all_gather(grad_resid.astype(jnp.bfloat16), "tensor", axis=0, tiled=True)
    grad_attention = contract_cols(grad_branch, attn_out).astype(jnp.bfloat16)
    grad_attn_out = contract_rows(attention, grad_branch)
    grad_mixed = grad_attention.reshape(group_rows, head_count, head_dim)

    def attend_back(bias_acc, packed):
        index, log_block = packed
        query_blk, key_blk, value_blk, allowed, scores = block_scores(index)
        grad_blk = lax.dynamic_slice_in_dim(grad_mixed, index * block, block, 0)
        probs = jnp.where(allowed[None], jnp.exp(scores - log_block[:, :, None]), 0.0)
        grad_probs = jnp.einsum(
            "ahd,chd->hac", grad_blk, value_blk, preferred_element_type=jnp.float32
        )
        row_inner = jnp.sum(probs * grad_probs, axis=-1, keepdims=True)
        grad_scores = (probs * (grad_probs - row_inner)).astype(jnp.bfloat16)
        grad_query = (
            jnp.einsum("hac,chd->ahd", grad_scores, key_blk, preferred_element_type=jnp.float32)
            * scale
        )
        grad_key = (
            jnp.einsum("hac,ahd->chd", grad_scores, query_blk, preferred_element_type=jnp.float32)
            * scale
        )
        grad_value = jnp.einsum(
            "hac,ahd->chd", probs.astype(jnp.bfloat16), grad_blk, preferred_element_type=jnp.float32
        )
        return (bias_acc + grad_scores.astype(jnp.float32), (grad_query, grad_key, grad_value))

    bias_start = jnp.zeros((head_count, block, 2 * block), jnp.float32)
    bias_acc, (grad_query, grad_key, grad_value) = lax.scan(
        attend_back, bias_start, (jnp.arange(block_count, dtype=jnp.int32), log_totals)
    )
    grad_projected = jnp.stack(
        [
            grad_query.reshape(group_rows, inner_width),
            fold_keys(grad_key, block),
            fold_keys(grad_value, block),
        ],
        axis=1,
    ).astype(jnp.bfloat16)
    grad_attn_qkv = jnp.einsum(
        "td,tcf->dcf", hidden_one, grad_projected, preferred_element_type=jnp.float32
    )
    grad_hidden_one = jnp.einsum(
        "tcf,dcf->td", grad_projected, attn_qkv, preferred_element_type=jnp.float32
    )
    bias_part = jnp.dot(
        fold_diag(bias_acc, block, diag_span),
        spot_hot,
        precision=PRECISE,
        preferred_element_type=jnp.float32,
    )
    tokens_part, gain_one_part = norm1_pull(grad_hidden_one)
    tokens_shared, gain_one_share, gain_two_share, router_share = (
        lax.psum_scatter(
            tokens_part.astype(jnp.bfloat16), "tensor", scatter_dimension=0, tiled=True
        ).astype(jnp.float32),
        lax.psum_scatter(
            gain_one_part.astype(jnp.bfloat16), "tensor", scatter_dimension=0, tiled=True
        ).astype(jnp.float32),
        lax.psum_scatter(
            gain_two_part.astype(jnp.bfloat16), "tensor", scatter_dimension=0, tiled=True
        ).astype(jnp.float32),
        lax.psum_scatter(
            router_part.astype(jnp.bfloat16), "tensor", scatter_dimension=0, tiled=True
        ).astype(jnp.float32),
    )
    totals = lax.psum(
        (grad_attn_qkv, grad_attn_out, bias_part, gain_one_share, gain_two_share, router_share),
        "expert",
    )
    grad_tokens = grad_resid + tokens_shared
    return (
        output,
        grad_tokens,
        totals[3],
        totals[0],
        totals[1],
        totals[2],
        totals[4],
        totals[5],
        grad_w_in,
        grad_w_out,
    )


def solution(mesh):
    return jax.shard_map(
        local,
        mesh=mesh,
        in_specs=(
            P("expert", None),
            P("expert", None),
            P(("expert", "tensor"), None),
            P(),
            P(None, None, "tensor"),
            P("tensor", None),
            P("tensor", None),
            P(),
            P(),
            P("expert", None, "tensor"),
            P("expert", "tensor", None),
            P(("expert", "tensor"), None),
        ),
        out_specs=(
            P(("expert", "tensor"), None),
            P(("expert", "tensor"), None),
            P("tensor"),
            P(None, None, "tensor"),
            P("tensor", None),
            P("tensor", None),
            P("tensor"),
            P("tensor", None),
            P("expert", None, "tensor"),
            P("expert", "tensor", None),
        ),
        check_vma=False,
    )
```

```python
import functools

import jax
import jax.numpy as jnp
from jax import lax
from jax.experimental import pallas as pl
from jax.experimental.pallas import tpu as pltpu
from jax.sharding import PartitionSpec as P

BLOCK = 512
HALF = 256
EPSILON = 1e-06
BLOCKED = -1e30
VMEM_LIMIT = 48 * 2**20


def mul(left, right, left_dim, right_dim):
    return lax.dot_general(
        left,
        right,
        (((left_dim,), (right_dim,)), ((), ())),
        preferred_element_type=jnp.float32,
    )


def spread_bias(bias_ref, spread_ref, head_count):
    for head in range(head_count):
        line = jnp.broadcast_to(bias_ref[head : head + 1, :], (2 * HALF, 2 * HALF))
        rolled = pltpu.roll(line, 0, 1, stride=1, stride_axis=0)
        spread_ref[head] = rolled[:, :HALF]


def fold_bias(total):
    line = jnp.concatenate([total, jnp.zeros_like(total)], axis=1)
    rows = lax.broadcasted_iota(jnp.int32, line.shape, 0)
    step = 1
    while step < 2 * HALF:
        line = jnp.where((rows & step) != 0, pltpu.roll(line, 2 * HALF - step, 1), line)
        step *= 2
    return jnp.sum(line, axis=0, keepdims=True)


def window_masks(lengths_ref, block_index, half, slots):
    query_pos = (
        lax.broadcasted_iota(jnp.int32, (1, HALF), 1) + block_index * BLOCK + half * HALF
    )
    start = jnp.zeros_like(query_pos)
    end = jnp.int32(0)
    for slot in range(slots):
        end = end + lengths_ref[0, slot]
        start = jnp.where(query_pos >= end, end, start)
    first_key = (block_index - 1) * BLOCK + half * HALF
    far_pos = lax.broadcasted_iota(jnp.int32, (HALF, 1), 0) + first_key
    near_pos = lax.broadcasted_iota(jnp.int32, (2 * HALF, 1), 0) + first_key + HALF
    return far_pos >= start, (near_pos >= start) & (near_pos <= query_pos)


def forward_kernel(
    lengths_ref, tokens_ref, gain_ref, qkv_ref, out_ref, bias_ref,
    branch_ref, proj_ref, mixed_ref, log_ref,
    keys_ref, values_ref, spread_ref,
    *, head_count, head_dim, slots,
):
    block_index = pl.program_id(0)
    inner = head_count * head_dim

    @pl.when(block_index == 0)
    def _():
        keys_ref[:, :BLOCK] = jnp.zeros_like(keys_ref[:, :BLOCK])
        values_ref[:, :BLOCK] = jnp.zeros_like(values_ref[:, :BLOCK])
        spread_bias(bias_ref, spread_ref, head_count)

    @pl.when(block_index > 0)
    def _():
        keys_ref[:, :BLOCK] = keys_ref[:, BLOCK:]
        values_ref[:, :BLOCK] = values_ref[:, BLOCK:]

    widened = tokens_ref[...].astype(jnp.float32)
    inverse = lax.rsqrt(jnp.mean(widened * widened, axis=-1, keepdims=True) + EPSILON)
    hidden = (widened * inverse * gain_ref[...]).astype(jnp.bfloat16)
    projected = mul(qkv_ref[...], hidden, 1, 1)
    proj_ref[...] = projected.astype(jnp.bfloat16)
    for head in range(head_count):
        low = inner + head * head_dim
        keys_ref[head, BLOCK:, :] = projected[low : low + head_dim].T.astype(jnp.bfloat16)
    values_ref[:, BLOCK:] = proj_ref[2 * inner :, :]
    scale = head_dim**-0.5
    for half in range(BLOCK // HALF):
        far_mask, near_mask = window_masks(lengths_ref, block_index, half, slots)
        cols = slice(half * HALF, (half + 1) * HALF)
        window = slice(half * HALF, (half + 3) * HALF)
        for head in range(head_count):
            rows = slice(head * head_dim, (head + 1) * head_dim)
            query = proj_ref[rows, cols] * jnp.bfloat16(scale)
            scores = mul(keys_ref[head, window, :], query, 1, 0)
            far = jnp.where(far_mask, scores[:HALF], BLOCKED)
            near = jnp.where(near_mask, scores[HALF:] + spread_ref[head], BLOCKED)
            peak = jnp.maximum(
                jnp.max(far, axis=0, keepdims=True), jnp.max(near, axis=0, keepdims=True)
            )
            far = jnp.exp(far - peak)
            near = jnp.exp(near - peak)
            total = jnp.sum(far, axis=0, keepdims=True) + jnp.sum(near, axis=0, keepdims=True)
            share = 1.0 / total
            weights = jnp.concatenate(
                [(far * share).astype(jnp.bfloat16), (near * share).astype(jnp.bfloat16)], axis=0
            )
            mixed_ref[rows, cols] = mul(values_ref[rows, window], weights, 1, 0).astype(
                jnp.bfloat16
            )
            log_ref[head : head + 1, cols] = peak + jnp.log(total)
    branch_ref[...] = mul(mixed_ref[...], out_ref[...], 0, 0).astype(jnp.bfloat16)


def backward_kernel(
    lengths_ref, tokens_ref, gain_ref, qkv_ref, out_ref, bias_ref,
    proj_ref, before_ref, mixed_ref, log_ref, grad_ref,
    part_ref, qkv_grad_ref, out_grad_ref, gain_grad_ref, bias_grad_ref, far_grad_ref,
    spread_ref, near_ref, far_ref, carry_ref, pieces_ref,
    *, head_count, head_dim, slots, block_count,
):
    step = pl.program_id(0)
    block_index = block_count - 1 - step
    inner = head_count * head_dim

    @pl.when(step == 0)
    def _():
        spread_bias(bias_ref, spread_ref, head_count)
        near_ref[...] = jnp.zeros_like(near_ref)
        far_ref[...] = jnp.zeros_like(far_ref)
        carry_ref[...] = jnp.zeros_like(carry_ref)
        qkv_grad_ref[...] = jnp.zeros_like(qkv_grad_ref)
        out_grad_ref[...] = jnp.zeros_like(out_grad_ref)
        gain_grad_ref[...] = jnp.zeros_like(gain_grad_ref)
        bias_grad_ref[...] = jnp.zeros_like(bias_grad_ref)

    @pl.when(step > 0)
    def _():
        carry_ref[:, BLOCK:] = carry_ref[:, :BLOCK]
        carry_ref[:, :BLOCK] = jnp.zeros_like(carry_ref[:, :BLOCK])

    grad_branch = grad_ref[...]
    out_grad_ref[...] += mul(mixed_ref[...], grad_branch, 1, 0)
    grad_mixed = mul(out_ref[...], grad_branch, 1, 1).astype(jnp.bfloat16)
    scale = head_dim**-0.5
    for head in range(head_count):
        rows = slice(head * head_dim, (head + 1) * head_dim)
        key_rows = slice(inner + head * head_dim, inner + (head + 1) * head_dim)
        value_rows = slice(2 * inner + head * head_dim, 2 * inner + (head + 1) * head_dim)
        keys_flat = jnp.concatenate([before_ref[key_rows, :], proj_ref[key_rows, :]], axis=1)
        values_flat = jnp.concatenate([before_ref[value_rows, :], proj_ref[value_rows, :]], axis=1)
        keys = keys_flat.astype(jnp.float32).T.astype(jnp.bfloat16)
        values = values_flat.astype(jnp.float32).T.astype(jnp.bfloat16)
        for half in range(BLOCK // HALF):
            far_mask, near_mask = window_masks(lengths_ref, block_index, half, slots)
            cols = slice(half * HALF, (half + 1) * HALF)
            window = slice(half * HALF, (half + 3) * HALF)
            query = proj_ref[rows, cols] * jnp.bfloat16(scale)
            scores = mul(keys[window], query, 1, 0)
            log_total = log_ref[head : head + 1, cols]
            far = jnp.where(far_mask, jnp.exp(scores[:HALF] - log_total), 0.0)
            near = jnp.where(
                near_mask, jnp.exp(scores[HALF:] + spread_ref[head] - log_total), 0.0
            )
            probs = jnp.concatenate([far, near], axis=0)
            grad_out = grad_mixed[rows, cols]
            grad_probs = mul(values[window], grad_out, 1, 0)
            row_inner = jnp.sum(probs * grad_probs, axis=0, keepdims=True)
            grad_scores = (probs * (grad_probs - row_inner)).astype(jnp.bfloat16)
            rounded = grad_scores.astype(jnp.float32)
            near_ref[head] += rounded[HALF:]
            far_ref[head : head + 1] += jnp.sum(rounded[:HALF], axis=0, keepdims=True)
            pieces_ref[rows, cols] = (
                mul(keys_flat[:, window], grad_scores, 1, 0) * scale
            ).astype(jnp.bfloat16)
            carry_ref[rows, window] += mul(query, grad_scores, 1, 1)
            carry_ref[key_rows, window] += mul(grad_out, probs.astype(jnp.bfloat16), 1, 1)
    pieces_ref[inner:, :] = carry_ref[:, BLOCK:].astype(jnp.bfloat16)
    widened = tokens_ref[...].astype(jnp.float32)
    inverse = lax.rsqrt(jnp.mean(widened * widened, axis=-1, keepdims=True) + EPSILON)
    normed = widened * inverse
    hidden = (normed * gain_ref[...]).astype(jnp.bfloat16)
    pieces = pieces_ref[...]
    qkv_grad_ref[...] += mul(pieces, hidden, 1, 0)
    grad_hidden = mul(pieces, qkv_ref[...], 0, 0)
    gain_grad_ref[...] += jnp.sum(
        (grad_hidden * normed).reshape(BLOCK // 8, 8, normed.shape[1]), axis=0
    )
    gained = grad_hidden * gain_ref[...]
    part_ref[...] = (
        inverse * (gained - normed * jnp.mean(gained * normed, axis=-1, keepdims=True))
    ).astype(jnp.bfloat16)

    @pl.when(step == block_count - 1)
    def _():
        for head in range(head_count):
            bias_grad_ref[head : head + 1, :] = fold_bias(near_ref[head])
        far_grad_ref[...] = far_ref[...]


def whole(shape):
    return pl.BlockSpec(shape, lambda step: (0,) * len(shape))


def bias_line(rel_bias):
    head_count, bucket_count = rel_bias.shape
    line = rel_bias - rel_bias[:, bucket_count - 1 :]
    line = jnp.concatenate(
        [
            jnp.zeros((head_count, HALF), jnp.float32),
            line,
            jnp.zeros((head_count, HALF - bucket_count), jnp.float32),
        ],
        axis=1,
    )
    return jnp.concatenate([line, jnp.zeros((8 - head_count, 2 * HALF), jnp.float32)], axis=0)


def attend(tokens, lengths, gain, qkv_flat, attn_out, rel_bias):
    rows, width = tokens.shape
    inner = attn_out.shape[0]
    head_count = rel_bias.shape[0]
    head_dim = inner // head_count
    block_count = rows // BLOCK
    return pl.pallas_call(
        functools.partial(
            forward_kernel, head_count=head_count, head_dim=head_dim, slots=lengths.shape[1]
        ),
        grid=(block_count,),
        in_specs=[
            pl.BlockSpec(memory_space=pltpu.SMEM),
            pl.BlockSpec((BLOCK, width), lambda step: (step, 0)),
            whole((1, width)),
            whole(qkv_flat.shape),
            whole(attn_out.shape),
            whole((8, 2 * HALF)),
        ],
        out_specs=[
            pl.BlockSpec((BLOCK, width), lambda step: (step, 0)),
            pl.BlockSpec((3 * inner, BLOCK), lambda step: (0, step)),
            pl.BlockSpec((inner, BLOCK), lambda step: (0, step)),
            pl.BlockSpec((8, BLOCK), lambda step: (0, step)),
        ],
        out_shape=[
            jax.ShapeDtypeStruct((rows, width), jnp.bfloat16),
            jax.ShapeDtypeStruct((3 * inner, rows), jnp.bfloat16),
            jax.ShapeDtypeStruct((inner, rows), jnp.bfloat16),
            jax.ShapeDtypeStruct((8, rows), jnp.float32),
        ],
        scratch_shapes=[
            pltpu.VMEM((head_count, 2 * BLOCK, head_dim), jnp.bfloat16),
            pltpu.VMEM((inner, 2 * BLOCK), jnp.bfloat16),
            pltpu.VMEM((head_count, 2 * HALF, HALF), jnp.float32),
        ],
        compiler_params=pltpu.CompilerParams(vmem_limit_bytes=VMEM_LIMIT),
        cost_estimate=pl.CostEstimate(
            flops=2 * rows * width * inner * 4 + 4 * rows * 768 * inner,
            bytes_accessed=10 * rows * width,
            transcendentals=rows * 768 * head_count,
        ),
        name="attend_forward",
    )(lengths, tokens, gain[None, :], qkv_flat, attn_out, bias_line(rel_bias))


def attend_back(
    tokens, lengths, gain, qkv_flat, attn_out, rel_bias, projected, mixed, log_total, grad_branch
):
    rows, width = tokens.shape
    inner = attn_out.shape[0]
    head_count, bucket_count = rel_bias.shape
    head_dim = inner // head_count
    block_count = rows // BLOCK
    last = block_count - 1
    part, qkv_grad, out_grad, gain_grad, bias_grad, far_grad = pl.pallas_call(
        functools.partial(
            backward_kernel,
            head_count=head_count,
            head_dim=head_dim,
            slots=lengths.shape[1],
            block_count=block_count,
        ),
        grid=(block_count,),
        in_specs=[
            pl.BlockSpec(memory_space=pltpu.SMEM),
            pl.BlockSpec((BLOCK, width), lambda step: (last - step, 0)),
            whole((1, width)),
            whole(qkv_flat.shape),
            whole(attn_out.shape),
            whole((8, 2 * HALF)),
            pl.BlockSpec((3 * inner, BLOCK), lambda step: (0, last - step)),
            pl.BlockSpec((3 * inner, BLOCK), lambda step: (0, jnp.maximum(last - step - 1, 0))),
            pl.BlockSpec((inner, BLOCK), lambda step: (0, last - step)),
            pl.BlockSpec((8, BLOCK), lambda step: (0, last - step)),
            pl.BlockSpec((BLOCK, width), lambda step: (last - step, 0)),
        ],
        out_specs=[
            pl.BlockSpec((BLOCK, width), lambda step: (last - step, 0)),
            whole((3 * inner, width)),
            whole((inner, width)),
            whole((8, width)),
            whole((8, 2 * HALF)),
            whole((8, HALF)),
        ],
        out_shape=[
            jax.ShapeDtypeStruct((rows, width), jnp.bfloat16),
            jax.ShapeDtypeStruct((3 * inner, width), jnp.float32),
            jax.ShapeDtypeStruct((inner, width), jnp.float32),
            jax.ShapeDtypeStruct((8, width), jnp.float32),
            jax.ShapeDtypeStruct((8, 2 * HALF), jnp.float32),
            jax.ShapeDtypeStruct((8, HALF), jnp.float32),
        ],
        scratch_shapes=[
            pltpu.VMEM((head_count, 2 * HALF, HALF), jnp.float32),
            pltpu.VMEM((head_count, 2 * HALF, HALF), jnp.float32),
            pltpu.VMEM((8, HALF), jnp.float32),
            pltpu.VMEM((2 * inner, 2 * BLOCK), jnp.float32),
            pltpu.VMEM((3 * inner, BLOCK), jnp.bfloat16),
        ],
        compiler_params=pltpu.CompilerParams(vmem_limit_bytes=VMEM_LIMIT),
        cost_estimate=pl.CostEstimate(
            flops=2 * rows * width * inner * 8 + 10 * rows * 768 * inner,
            bytes_accessed=14 * rows * width,
            transcendentals=rows * 768 * head_count,
        ),
        name="attend_backward",
    )(
        lengths, tokens, gain[None, :], qkv_flat, attn_out, bias_line(rel_bias),
        projected, projected, mixed, log_total, grad_branch,
    )
    near_grad = bias_grad[:head_count, HALF : HALF + bucket_count - 1]
    rest = jnp.sum(bias_grad[:head_count], axis=1) - jnp.sum(near_grad, axis=1)
    rest = rest + jnp.sum(far_grad[:head_count], axis=1)
    bias_part = jnp.concatenate([near_grad, rest[:, None]], axis=1)
    return part, qkv_grad, out_grad, jnp.sum(gain_grad, axis=0), bias_part


def rms_norm(values, gain):
    return values * lax.rsqrt(jnp.mean(values * values, axis=-1, keepdims=True) + EPSILON) * gain


def gelu_tanh(values):
    return (
        0.5
        * values
        * (1.0 + jnp.tanh(0.7978845608028654 * (values + 0.044715 * values * values * values)))
    )


def exchange(rows):
    parts = lax.axis_size("expert")
    return lax.all_to_all(
        rows.reshape((parts, -1) + rows.shape[1:]), "expert", split_axis=0, concat_axis=0, tiled=True
    ).reshape(rows.shape)


def local(
    tokens,
    lengths,
    routes,
    norm1_gain,
    attn_qkv,
    attn_out,
    rel_bias,
    norm2_gain,
    router,
    expert_in,
    expert_out,
    out_grad,
):
    n_tensor = lax.axis_size("tensor")
    tensor_index = lax.axis_index("tensor")
    width = tokens.shape[1]
    own_rows = routes.shape[0]
    inner = attn_out.shape[0]
    head_count, bucket_count = rel_bias.shape
    expert_count = router.shape[1]
    capacity = max(2, 4 * own_rows // expert_count)

    route_hot = (routes[:, :, None] == jnp.arange(expert_count, dtype=jnp.int32)).astype(jnp.int32)
    counts = jnp.sum(route_hot, axis=1)
    before = jnp.cumsum(counts, axis=0) - counts
    slot_rank = jnp.sum(route_hot * before[:, None, :], axis=-1)
    slot_index = routes * capacity + slot_rank
    slot_ids = jnp.arange(expert_count * capacity, dtype=jnp.int32)
    slot_match = slot_index[:, :, None] == slot_ids[None, None, :]
    dispatch = (slot_match[:, 0] | slot_match[:, 1]).astype(jnp.bfloat16)
    other_ids = jnp.sum(jnp.where(slot_match, routes[:, ::-1, None] + 1, 0), axis=(0, 1))
    other_here = exchange(other_ids)
    grad_rows = exchange(mul(dispatch, out_grad, 0, 0).astype(jnp.bfloat16))

    qkv_flat = attn_qkv.transpose(1, 2, 0).reshape(3 * inner, width)
    branch, projected, mixed, log_total = attend(
        tokens, lengths, norm1_gain, qkv_flat, attn_out, rel_bias
    )
    branch = lax.psum_scatter(branch, "tensor", scatter_dimension=0, tiled=True)
    branch, grad_rows, other_here = lax.optimization_barrier((branch, grad_rows, other_here))
    own_tokens = lax.dynamic_slice_in_dim(tokens, tensor_index * own_rows, own_rows, 0)
    resid = own_tokens.astype(jnp.float32) + branch.astype(jnp.float32)
    normed_two, norm2_pull = jax.vjp(rms_norm, resid, norm2_gain)
    hidden_two = normed_two.astype(jnp.bfloat16)
    expert_rows = exchange(mul(dispatch, hidden_two, 0, 0).astype(jnp.bfloat16))
    weights_in = lax.all_gather(expert_in[0], "tensor")
    weights_out = lax.all_gather(expert_out[0], "tensor")

    pre = jnp.einsum("sd,jdf->jsf", expert_rows, weights_in, preferred_element_type=jnp.float32)
    act_value, gelu_pull = jax.vjp(gelu_tanh, pre)
    act = act_value.astype(jnp.bfloat16)
    slot_logits = jnp.dot(expert_rows, router, preferred_element_type=jnp.float32)
    own_hot = (jnp.arange(expert_count, dtype=jnp.int32) == lax.axis_index("expert")).astype(
        jnp.float32
    )
    other_hot = (other_here[:, None] == jnp.arange(1, expert_count + 1, dtype=jnp.int32)).astype(
        jnp.float32
    )
    hot_gap = own_hot[None, :] - other_hot
    logit_gap = jnp.sum(hot_gap * slot_logits, axis=-1, keepdims=True)
    gate = 1.0 / (1.0 + jnp.exp(-logit_gap))
    other_gate = 1.0 / (1.0 + jnp.exp(logit_gap))
    act_grads = jnp.einsum("sd,jfd->jsf", grad_rows, weights_out, preferred_element_type=jnp.float32)
    gate_grads = jnp.sum(act_value * act_grads, axis=(0, 2))[:, None]
    grad_logits = (gate * other_gate * gate_grads * hot_gap).astype(jnp.bfloat16)
    grad_pre = gelu_pull(gate[None] * act_grads)[0].astype(jnp.bfloat16)
    grad_sent = exchange(
        (
            jnp.einsum("jsf,jdf->sd", grad_pre, weights_in, preferred_element_type=jnp.float32)
            + mul(grad_logits, router, 1, 1)
        ).astype(jnp.bfloat16)
    )
    result = (
        gate * jnp.einsum("jsf,jfd->sd", act, weights_out, preferred_element_type=jnp.float32)
    ).astype(jnp.bfloat16)
    router_part = mul(expert_rows, grad_logits, 0, 0)
    gated_rows = (gate * grad_rows.astype(jnp.float32)).astype(jnp.bfloat16)
    grad_w_out = jnp.einsum(
        "jsf,sd->jfd", act, gated_rows, preferred_element_type=jnp.float32
    ).astype(jnp.bfloat16)
    grad_w_in = jnp.einsum(
        "sd,jsf->jdf", expert_rows, grad_pre, preferred_element_type=jnp.float32
    ).astype(jnp.bfloat16)
    grad_sent, result, grad_w_in, grad_w_out = lax.optimization_barrier(
        (grad_sent, result, grad_w_in, grad_w_out)
    )
    came_back = exchange(result)
    grad_in = out_grad.astype(jnp.float32)
    grad_hidden_two = jnp.dot(dispatch, grad_sent, preferred_element_type=jnp.float32)
    grad_resid_norm, gain_two_part = norm2_pull(grad_hidden_two)
    grad_resid = grad_in + grad_resid_norm
    grad_branch = lax.all_gather(grad_resid.astype(jnp.bfloat16), "tensor", axis=0, tiled=True)
    grad_w_out = lax.psum_scatter(grad_w_out, "tensor", scatter_dimension=0)
    grad_w_in = lax.psum_scatter(grad_w_in, "tensor", scatter_dimension=0)

    tokens_part, qkv_part, out_part, gain_one_part, bias_part = attend_back(
        tokens, lengths, norm1_gain, qkv_flat, attn_out, rel_bias,
        projected, mixed, log_total, grad_branch,
    )
    tokens_part, came_back = lax.optimization_barrier((tokens_part, came_back))
    output = resid + jnp.dot(dispatch, came_back, preferred_element_type=jnp.float32)
    tokens_shared = lax.psum_scatter(tokens_part, "tensor", scatter_dimension=0, tiled=True)
    grad_tokens = grad_resid + tokens_shared.astype(jnp.float32)
    weights_part = jnp.concatenate([qkv_part, out_part], axis=0).astype(jnp.bfloat16)
    weights_total = lax.psum(weights_part, "expert").astype(jnp.float32)
    bias_slots = lax.dynamic_update_slice_in_dim(
        jnp.zeros((n_tensor * head_count, bucket_count), jnp.float32),
        bias_part,
        tensor_index * head_count,
        0,
    )
    small = jnp.concatenate(
        [gain_one_part, gain_two_part, router_part.T.reshape(-1), bias_slots.reshape(-1)]
    )
    small = lax.psum(small, ("expert", "tensor"))
    count = 2 + expert_count
    columns = lax.dynamic_slice_in_dim(
        small[: count * width].reshape(count, width),
        tensor_index * (width // n_tensor),
        width // n_tensor,
        1,
    )
    bias_total = lax.dynamic_slice_in_dim(
        small[count * width :].reshape(n_tensor * head_count, bucket_count),
        tensor_index * head_count,
        head_count,
        0,
    )
    return (
        output,
        grad_tokens,
        columns[0],
        weights_total[: 3 * inner].reshape(3, inner, width).transpose(2, 0, 1),
        weights_total[3 * inner :],
        bias_total,
        columns[1],
        columns[2:].T,
        grad_w_in.astype(jnp.float32)[None],
        grad_w_out.astype(jnp.float32)[None],
    )


def solution(mesh):
    return jax.shard_map(
        local,
        mesh=mesh,
        in_specs=(
            P("expert", None),
            P("expert", None),
            P(("expert", "tensor"), None),
            P(),
            P(None, None, "tensor"),
            P("tensor", None),
            P("tensor", None),
            P(),
            P(),
            P("expert", None, "tensor"),
            P("expert", "tensor", None),
            P(("expert", "tensor"), None),
        ),
        out_specs=(
            P(("expert", "tensor"), None),
            P(("expert", "tensor"), None),
            P("tensor"),
            P(None, None, "tensor"),
            P("tensor", None),
            P("tensor", None),
            P("tensor"),
            P("tensor", None),
            P("expert", None, "tensor"),
            P("expert", "tensor", None),
        ),
        check_vma=False,
    )
```

```python
import functools

import jax
import jax.numpy as jnp
from jax import lax
from jax.experimental import pallas as pl
from jax.experimental.pallas import tpu as pltpu
from jax.sharding import PartitionSpec as P

BLOCK = 512
HALF = 256
EPSILON = 1e-06
BLOCKED = -1e30
VMEM_LIMIT = 48 * 2**20


def mul(left, right, left_dim, right_dim):
    return lax.dot_general(
        left,
        right,
        (((left_dim,), (right_dim,)), ((), ())),
        preferred_element_type=jnp.float32,
    )


def spread_bias(bias_ref, spread_ref, head_count):
    for head in range(head_count):
        line = jnp.broadcast_to(bias_ref[head : head + 1, :], (2 * HALF, 2 * HALF))
        rolled = pltpu.roll(line, 0, 1, stride=1, stride_axis=0)
        spread_ref[head] = rolled[:, :HALF]


def fold_bias(total):
    line = jnp.concatenate([total, jnp.zeros_like(total)], axis=1)
    rows = lax.broadcasted_iota(jnp.int32, line.shape, 0)
    step = 1
    while step < 2 * HALF:
        line = jnp.where((rows & step) != 0, pltpu.roll(line, 2 * HALF - step, 1), line)
        step *= 2
    return jnp.sum(line, axis=0, keepdims=True)


def window_masks(lengths_ref, block_index, half, slots):
    query_pos = (
        lax.broadcasted_iota(jnp.int32, (1, HALF), 1) + block_index * BLOCK + half * HALF
    )
    start = jnp.zeros_like(query_pos)
    end = jnp.int32(0)
    for slot in range(slots):
        end = end + lengths_ref[0, slot]
        start = jnp.where(query_pos >= end, end, start)
    first_key = (block_index - 1) * BLOCK + half * HALF
    far_pos = lax.broadcasted_iota(jnp.int32, (HALF, 1), 0) + first_key
    near_pos = lax.broadcasted_iota(jnp.int32, (2 * HALF, 1), 0) + first_key + HALF
    return far_pos >= start, (near_pos >= start) & (near_pos <= query_pos)


def forward_kernel(
    lengths_ref, tokens_ref, gain_ref, qkv_ref, out_ref, bias_ref,
    branch_ref, proj_ref, mixed_ref, log_ref,
    keys_ref, values_ref, spread_ref,
    *, head_count, head_dim, slots,
):
    block_index = pl.program_id(0)
    inner = head_count * head_dim

    @pl.when(block_index == 0)
    def _():
        keys_ref[:, :BLOCK] = jnp.zeros_like(keys_ref[:, :BLOCK])
        values_ref[:, :BLOCK] = jnp.zeros_like(values_ref[:, :BLOCK])
        spread_bias(bias_ref, spread_ref, head_count)

    @pl.when(block_index > 0)
    def _():
        keys_ref[:, :BLOCK] = keys_ref[:, BLOCK:]
        values_ref[:, :BLOCK] = values_ref[:, BLOCK:]

    widened = tokens_ref[...].astype(jnp.float32)
    inverse = lax.rsqrt(jnp.mean(widened * widened, axis=-1, keepdims=True) + EPSILON)
    hidden = (widened * inverse * gain_ref[...]).astype(jnp.bfloat16)
    projected = mul(qkv_ref[...], hidden, 1, 1)
    proj_ref[...] = projected.astype(jnp.bfloat16)
    for head in range(head_count):
        low = inner + head * head_dim
        keys_ref[head, BLOCK:, :] = projected[low : low + head_dim].T.astype(jnp.bfloat16)
    values_ref[:, BLOCK:] = proj_ref[2 * inner :, :]
    scale = head_dim**-0.5
    for half in range(BLOCK // HALF):
        far_mask, near_mask = window_masks(lengths_ref, block_index, half, slots)
        cols = slice(half * HALF, (half + 1) * HALF)
        window = slice(half * HALF, (half + 3) * HALF)
        for head in range(head_count):
            rows = slice(head * head_dim, (head + 1) * head_dim)
            query = proj_ref[rows, cols] * jnp.bfloat16(scale)
            scores = mul(keys_ref[head, window, :], query, 1, 0)
            far = jnp.where(far_mask, scores[:HALF], BLOCKED)
            near = jnp.where(near_mask, scores[HALF:] + spread_ref[head], BLOCKED)
            peak = jnp.maximum(
                jnp.max(far, axis=0, keepdims=True), jnp.max(near, axis=0, keepdims=True)
            )
            far = jnp.exp(far - peak)
            near = jnp.exp(near - peak)
            total = jnp.sum(far, axis=0, keepdims=True) + jnp.sum(near, axis=0, keepdims=True)
            share = 1.0 / total
            weights = jnp.concatenate(
                [(far * share).astype(jnp.bfloat16), (near * share).astype(jnp.bfloat16)], axis=0
            )
            mixed_ref[rows, cols] = mul(values_ref[rows, window], weights, 1, 0).astype(
                jnp.bfloat16
            )
            log_ref[head : head + 1, cols] = peak + jnp.log(total)
    branch_ref[...] = mul(mixed_ref[...], out_ref[...], 0, 0).astype(jnp.bfloat16)


def backward_kernel(
    lengths_ref, tokens_ref, gain_ref, qkv_ref, out_ref, bias_ref,
    proj_ref, before_ref, mixed_ref, log_ref, grad_ref,
    part_ref, qkv_grad_ref, out_grad_ref, gain_grad_ref, bias_grad_ref, far_grad_ref,
    spread_ref, near_ref, far_ref, carry_ref, pieces_ref,
    *, head_count, head_dim, slots, block_count,
):
    step = pl.program_id(0)
    block_index = block_count - 1 - step
    inner = head_count * head_dim

    @pl.when(step == 0)
    def _():
        spread_bias(bias_ref, spread_ref, head_count)
        near_ref[...] = jnp.zeros_like(near_ref)
        far_ref[...] = jnp.zeros_like(far_ref)
        carry_ref[...] = jnp.zeros_like(carry_ref)
        qkv_grad_ref[...] = jnp.zeros_like(qkv_grad_ref)
        out_grad_ref[...] = jnp.zeros_like(out_grad_ref)
        gain_grad_ref[...] = jnp.zeros_like(gain_grad_ref)
        bias_grad_ref[...] = jnp.zeros_like(bias_grad_ref)

    @pl.when(step > 0)
    def _():
        carry_ref[:, BLOCK:] = carry_ref[:, :BLOCK]
        carry_ref[:, :BLOCK] = jnp.zeros_like(carry_ref[:, :BLOCK])

    grad_branch = grad_ref[...]
    out_grad_ref[...] += mul(mixed_ref[...], grad_branch, 1, 0)
    grad_mixed = mul(out_ref[...], grad_branch, 1, 1).astype(jnp.bfloat16)
    scale = head_dim**-0.5
    for head in range(head_count):
        rows = slice(head * head_dim, (head + 1) * head_dim)
        key_rows = slice(inner + head * head_dim, inner + (head + 1) * head_dim)
        value_rows = slice(2 * inner + head * head_dim, 2 * inner + (head + 1) * head_dim)
        keys_flat = jnp.concatenate([before_ref[key_rows, :], proj_ref[key_rows, :]], axis=1)
        values_flat = jnp.concatenate([before_ref[value_rows, :], proj_ref[value_rows, :]], axis=1)
        keys = keys_flat.astype(jnp.float32).T.astype(jnp.bfloat16)
        values = values_flat.astype(jnp.float32).T.astype(jnp.bfloat16)
        for half in range(BLOCK // HALF):
            far_mask, near_mask = window_masks(lengths_ref, block_index, half, slots)
            cols = slice(half * HALF, (half + 1) * HALF)
            window = slice(half * HALF, (half + 3) * HALF)
            query = proj_ref[rows, cols] * jnp.bfloat16(scale)
            scores = mul(keys[window], query, 1, 0)
            log_total = log_ref[head : head + 1, cols]
            far = jnp.where(far_mask, jnp.exp(scores[:HALF] - log_total), 0.0)
            near = jnp.where(
                near_mask, jnp.exp(scores[HALF:] + spread_ref[head] - log_total), 0.0
            )
            probs = jnp.concatenate([far, near], axis=0)
            grad_out = grad_mixed[rows, cols]
            grad_probs = mul(values[window], grad_out, 1, 0)
            row_inner = jnp.sum(probs * grad_probs, axis=0, keepdims=True)
            grad_scores = (probs * (grad_probs - row_inner)).astype(jnp.bfloat16)
            rounded = grad_scores.astype(jnp.float32)
            near_ref[head] += rounded[HALF:]
            far_ref[head : head + 1] += jnp.sum(rounded[:HALF], axis=0, keepdims=True)
            pieces_ref[rows, cols] = (
                mul(keys_flat[:, window], grad_scores, 1, 0) * scale
            ).astype(jnp.bfloat16)
            carry_ref[rows, window] += mul(query, grad_scores, 1, 1)
            carry_ref[key_rows, window] += mul(grad_out, probs.astype(jnp.bfloat16), 1, 1)
    pieces_ref[inner:, :] = carry_ref[:, BLOCK:].astype(jnp.bfloat16)
    widened = tokens_ref[...].astype(jnp.float32)
    inverse = lax.rsqrt(jnp.mean(widened * widened, axis=-1, keepdims=True) + EPSILON)
    normed = widened * inverse
    hidden = (normed * gain_ref[...]).astype(jnp.bfloat16)
    pieces = pieces_ref[...]
    qkv_grad_ref[...] += mul(pieces, hidden, 1, 0)
    grad_hidden = mul(pieces, qkv_ref[...], 0, 0)
    gain_grad_ref[...] += jnp.sum(
        (grad_hidden * normed).reshape(BLOCK // 8, 8, normed.shape[1]), axis=0
    )
    gained = grad_hidden * gain_ref[...]
    part_ref[...] = (
        inverse * (gained - normed * jnp.mean(gained * normed, axis=-1, keepdims=True))
    ).astype(jnp.bfloat16)

    @pl.when(step == block_count - 1)
    def _():
        for head in range(head_count):
            bias_grad_ref[head : head + 1, :] = fold_bias(near_ref[head])
        far_grad_ref[...] = far_ref[...]


def whole(shape):
    return pl.BlockSpec(shape, lambda step: (0,) * len(shape))


def bias_line(rel_bias):
    head_count, bucket_count = rel_bias.shape
    line = rel_bias - rel_bias[:, bucket_count - 1 :]
    line = jnp.concatenate(
        [
            jnp.zeros((head_count, HALF), jnp.float32),
            line,
            jnp.zeros((head_count, HALF - bucket_count), jnp.float32),
        ],
        axis=1,
    )
    return jnp.concatenate([line, jnp.zeros((8 - head_count, 2 * HALF), jnp.float32)], axis=0)


def attend(tokens, lengths, gain, qkv_flat, attn_out, rel_bias):
    rows, width = tokens.shape
    inner = attn_out.shape[0]
    head_count = rel_bias.shape[0]
    head_dim = inner // head_count
    block_count = rows // BLOCK
    return pl.pallas_call(
        functools.partial(
            forward_kernel, head_count=head_count, head_dim=head_dim, slots=lengths.shape[1]
        ),
        grid=(block_count,),
        in_specs=[
            pl.BlockSpec(memory_space=pltpu.SMEM),
            pl.BlockSpec((BLOCK, width), lambda step: (step, 0)),
            whole((1, width)),
            whole(qkv_flat.shape),
            whole(attn_out.shape),
            whole((8, 2 * HALF)),
        ],
        out_specs=[
            pl.BlockSpec((BLOCK, width), lambda step: (step, 0)),
            pl.BlockSpec((3 * inner, BLOCK), lambda step: (0, step)),
            pl.BlockSpec((inner, BLOCK), lambda step: (0, step)),
            pl.BlockSpec((8, BLOCK), lambda step: (0, step)),
        ],
        out_shape=[
            jax.ShapeDtypeStruct((rows, width), jnp.bfloat16),
            jax.ShapeDtypeStruct((3 * inner, rows), jnp.bfloat16),
            jax.ShapeDtypeStruct((inner, rows), jnp.bfloat16),
            jax.ShapeDtypeStruct((8, rows), jnp.float32),
        ],
        scratch_shapes=[
            pltpu.VMEM((head_count, 2 * BLOCK, head_dim), jnp.bfloat16),
            pltpu.VMEM((inner, 2 * BLOCK), jnp.bfloat16),
            pltpu.VMEM((head_count, 2 * HALF, HALF), jnp.float32),
        ],
        compiler_params=pltpu.CompilerParams(vmem_limit_bytes=VMEM_LIMIT),
        cost_estimate=pl.CostEstimate(
            flops=2 * rows * width * inner * 4 + 4 * rows * 768 * inner,
            bytes_accessed=10 * rows * width,
            transcendentals=rows * 768 * head_count,
        ),
        name="attend_forward",
    )(lengths, tokens, gain[None, :], qkv_flat, attn_out, bias_line(rel_bias))


def attend_back(
    tokens, lengths, gain, qkv_flat, attn_out, rel_bias, projected, mixed, log_total, grad_branch
):
    rows, width = tokens.shape
    inner = attn_out.shape[0]
    head_count, bucket_count = rel_bias.shape
    head_dim = inner // head_count
    block_count = rows // BLOCK
    last = block_count - 1
    part, qkv_grad, out_grad, gain_grad, bias_grad, far_grad = pl.pallas_call(
        functools.partial(
            backward_kernel,
            head_count=head_count,
            head_dim=head_dim,
            slots=lengths.shape[1],
            block_count=block_count,
        ),
        grid=(block_count,),
        in_specs=[
            pl.BlockSpec(memory_space=pltpu.SMEM),
            pl.BlockSpec((BLOCK, width), lambda step: (last - step, 0)),
            whole((1, width)),
            whole(qkv_flat.shape),
            whole(attn_out.shape),
            whole((8, 2 * HALF)),
            pl.BlockSpec((3 * inner, BLOCK), lambda step: (0, last - step)),
            pl.BlockSpec((3 * inner, BLOCK), lambda step: (0, jnp.maximum(last - step - 1, 0))),
            pl.BlockSpec((inner, BLOCK), lambda step: (0, last - step)),
            pl.BlockSpec((8, BLOCK), lambda step: (0, last - step)),
            pl.BlockSpec((BLOCK, width), lambda step: (last - step, 0)),
        ],
        out_specs=[
            pl.BlockSpec((BLOCK, width), lambda step: (last - step, 0)),
            whole((3 * inner, width)),
            whole((inner, width)),
            whole((8, width)),
            whole((8, 2 * HALF)),
            whole((8, HALF)),
        ],
        out_shape=[
            jax.ShapeDtypeStruct((rows, width), jnp.bfloat16),
            jax.ShapeDtypeStruct((3 * inner, width), jnp.float32),
            jax.ShapeDtypeStruct((inner, width), jnp.float32),
            jax.ShapeDtypeStruct((8, width), jnp.float32),
            jax.ShapeDtypeStruct((8, 2 * HALF), jnp.float32),
            jax.ShapeDtypeStruct((8, HALF), jnp.float32),
        ],
        scratch_shapes=[
            pltpu.VMEM((head_count, 2 * HALF, HALF), jnp.float32),
            pltpu.VMEM((head_count, 2 * HALF, HALF), jnp.float32),
            pltpu.VMEM((8, HALF), jnp.float32),
            pltpu.VMEM((2 * inner, 2 * BLOCK), jnp.float32),
            pltpu.VMEM((3 * inner, BLOCK), jnp.bfloat16),
        ],
        compiler_params=pltpu.CompilerParams(vmem_limit_bytes=VMEM_LIMIT),
        cost_estimate=pl.CostEstimate(
            flops=2 * rows * width * inner * 8 + 10 * rows * 768 * inner,
            bytes_accessed=14 * rows * width,
            transcendentals=rows * 768 * head_count,
        ),
        name="attend_backward",
    )(
        lengths, tokens, gain[None, :], qkv_flat, attn_out, bias_line(rel_bias),
        projected, projected, mixed, log_total, grad_branch,
    )
    near_grad = bias_grad[:head_count, HALF : HALF + bucket_count - 1]
    rest = jnp.sum(bias_grad[:head_count], axis=1) - jnp.sum(near_grad, axis=1)
    rest = rest + jnp.sum(far_grad[:head_count], axis=1)
    bias_part = jnp.concatenate([near_grad, rest[:, None]], axis=1)
    return part, qkv_grad, out_grad, jnp.sum(gain_grad, axis=0), bias_part


def rms_norm(values, gain):
    return values * lax.rsqrt(jnp.mean(values * values, axis=-1, keepdims=True) + EPSILON) * gain


def gelu_tanh(values):
    return (
        0.5
        * values
        * (1.0 + jnp.tanh(0.7978845608028654 * (values + 0.044715 * values * values * values)))
    )


def exchange(rows):
    parts = lax.axis_size("expert")
    return lax.all_to_all(
        rows.reshape((parts, -1) + rows.shape[1:]), "expert", split_axis=0, concat_axis=0, tiled=True
    ).reshape(rows.shape)


def swap(value, axis_name, bit):
    count = lax.axis_size(axis_name)
    return lax.ppermute(value, axis_name, [(i, i ^ (1 << bit)) for i in range(count)])


def own_bit(axis_name, bit):
    return (lax.axis_index(axis_name) >> bit) & 1


def scatter_sum(pieces, axis_name, order):
    bits = sorted(order, reverse=True)
    total = pieces.reshape((2,) * len(bits) + pieces.shape[1:])
    for bit in order:
        dim = bits.index(bit)
        bits.remove(bit)
        mine = own_bit(axis_name, bit)
        keep = lax.dynamic_index_in_dim(total, mine, dim, keepdims=False)
        send = lax.dynamic_index_in_dim(total, 1 - mine, dim, keepdims=False)
        got = swap(send.astype(jnp.bfloat16), axis_name, bit)
        total = keep.astype(jnp.float32) + got.astype(jnp.float32)
    return total


def gather(piece, axis_name, order):
    bits = []
    whole_value = piece
    for bit in order:
        bits = sorted(bits + [bit], reverse=True)
        dim = bits.index(bit)
        got = swap(whole_value, axis_name, bit)
        first = own_bit(axis_name, bit) == 0
        whole_value = jnp.stack(
            [jnp.where(first, whole_value, got), jnp.where(first, got, whole_value)], axis=dim
        )
    return whole_value.reshape((-1,) + piece.shape[1:])


def butterfly(value, axis_name):
    for bit in range(bit_count(axis_name)):
        value = value + swap(value, axis_name, bit)
    return value


def bit_count(axis_name):
    return (lax.axis_size(axis_name) - 1).bit_length()


def sum_rows(rows, axis_name):
    bits = list(range(bit_count(axis_name)))
    parts = lax.axis_size(axis_name)
    results = []
    for half, turn in zip(jnp.split(rows, 2, axis=0), (0, 1)):
        order = bits[turn:] + bits[:turn]
        pieces = half.reshape((parts, -1) + rows.shape[1:])
        own = scatter_sum(pieces, axis_name, order).astype(jnp.bfloat16)
        results.append(gather(own, axis_name, order[::-1]))
    return jnp.concatenate(results, axis=0)


def local(
    tokens,
    lengths,
    routes,
    norm1_gain,
    attn_qkv,
    attn_out,
    rel_bias,
    norm2_gain,
    router,
    expert_in,
    expert_out,
    out_grad,
):
    n_tensor = lax.axis_size("tensor")
    tensor_index = lax.axis_index("tensor")
    width = tokens.shape[1]
    own_rows = routes.shape[0]
    inner = attn_out.shape[0]
    head_count, bucket_count = rel_bias.shape
    expert_count = router.shape[1]
    capacity = max(2, 4 * own_rows // expert_count)

    route_hot = (routes[:, :, None] == jnp.arange(expert_count, dtype=jnp.int32)).astype(jnp.int32)
    counts = jnp.sum(route_hot, axis=1)
    before = jnp.cumsum(counts, axis=0) - counts
    slot_rank = jnp.sum(route_hot * before[:, None, :], axis=-1)
    slot_index = routes * capacity + slot_rank
    slot_ids = jnp.arange(expert_count * capacity, dtype=jnp.int32)
    slot_match = slot_index[:, :, None] == slot_ids[None, None, :]
    dispatch = (slot_match[:, 0] | slot_match[:, 1]).astype(jnp.bfloat16)
    other_ids = jnp.sum(jnp.where(slot_match, routes[:, ::-1, None] + 1, 0), axis=(0, 1))
    grad_slots = mul(dispatch, out_grad, 0, 0).astype(jnp.bfloat16)
    grad_rows = exchange(grad_slots)
    tokens, _ = lax.optimization_barrier((tokens, grad_slots))
    tensor_bits = list(range(bit_count("tensor")))

    qkv_flat = attn_qkv.transpose(1, 2, 0).reshape(3 * inner, width)
    branch, projected, mixed, log_total = attend(
        tokens, lengths, norm1_gain, qkv_flat, attn_out, rel_bias
    )
    branch = scatter_sum(branch.reshape(n_tensor, own_rows, width), "tensor", tensor_bits)
    own_tokens = lax.dynamic_slice_in_dim(tokens, tensor_index * own_rows, own_rows, 0)
    resid = own_tokens.astype(jnp.float32) + branch
    normed_two, norm2_pull = jax.vjp(rms_norm, resid, norm2_gain)
    hidden_two = normed_two.astype(jnp.bfloat16)
    outgoing = mul(dispatch, hidden_two, 0, 0).astype(jnp.bfloat16)
    outgoing, other_ids, grad_rows = lax.optimization_barrier((outgoing, other_ids, grad_rows))
    expert_rows = exchange(outgoing)
    other_here = exchange(other_ids)
    weights_in = lax.all_gather(expert_in[0], "tensor")
    weights_out = lax.all_gather(expert_out[0], "tensor")

    pre = jnp.einsum("sd,jdf->jsf", expert_rows, weights_in, preferred_element_type=jnp.float32)
    act_value, gelu_pull = jax.vjp(gelu_tanh, pre)
    act = act_value.astype(jnp.bfloat16)
    slot_logits = jnp.dot(expert_rows, router, preferred_element_type=jnp.float32)
    own_hot = (jnp.arange(expert_count, dtype=jnp.int32) == lax.axis_index("expert")).astype(
        jnp.float32
    )
    other_hot = (other_here[:, None] == jnp.arange(1, expert_count + 1, dtype=jnp.int32)).astype(
        jnp.float32
    )
    hot_gap = own_hot[None, :] - other_hot
    logit_gap = jnp.sum(hot_gap * slot_logits, axis=-1, keepdims=True)
    gate = 1.0 / (1.0 + jnp.exp(-logit_gap))
    other_gate = 1.0 / (1.0 + jnp.exp(logit_gap))
    act_grads = jnp.einsum("sd,jfd->jsf", grad_rows, weights_out, preferred_element_type=jnp.float32)
    gate_grads = jnp.sum(act_value * act_grads, axis=(0, 2))[:, None]
    grad_logits = (gate * other_gate * gate_grads * hot_gap).astype(jnp.bfloat16)
    grad_pre = gelu_pull(gate[None] * act_grads)[0].astype(jnp.bfloat16)
    grad_sent = exchange(
        (
            jnp.einsum("jsf,jdf->sd", grad_pre, weights_in, preferred_element_type=jnp.float32)
            + mul(grad_logits, router, 1, 1)
        ).astype(jnp.bfloat16)
    )
    result = (
        gate * jnp.einsum("jsf,jfd->sd", act, weights_out, preferred_element_type=jnp.float32)
    ).astype(jnp.bfloat16)
    router_part = mul(expert_rows, grad_logits, 0, 0)
    gated_rows = (gate * grad_rows.astype(jnp.float32)).astype(jnp.bfloat16)
    grad_w_out = jnp.einsum(
        "jsf,sd->jfd", act, gated_rows, preferred_element_type=jnp.float32
    ).astype(jnp.bfloat16)
    grad_w_in = jnp.einsum(
        "sd,jsf->jdf", expert_rows, grad_pre, preferred_element_type=jnp.float32
    ).astype(jnp.bfloat16)
    grad_sent, result, grad_w_in, grad_w_out = lax.optimization_barrier(
        (grad_sent, result, grad_w_in, grad_w_out)
    )
    came_back = exchange(result)
    grad_in = out_grad.astype(jnp.float32)
    grad_hidden_two = jnp.dot(dispatch, grad_sent, preferred_element_type=jnp.float32)
    grad_resid_norm, gain_two_part = norm2_pull(grad_hidden_two)
    grad_resid = grad_in + grad_resid_norm
    grad_branch = gather(grad_resid.astype(jnp.bfloat16), "tensor", tensor_bits[::-1])
    grad_w_out = lax.psum_scatter(grad_w_out, "tensor", scatter_dimension=0)
    grad_w_in = lax.psum_scatter(grad_w_in, "tensor", scatter_dimension=0)

    tokens_part, qkv_part, out_part, gain_one_part, bias_part = attend_back(
        tokens, lengths, norm1_gain, qkv_flat, attn_out, rel_bias,
        projected, mixed, log_total, grad_branch,
    )
    (tokens_part, qkv_part, out_part, gain_one_part, bias_part, came_back, grad_w_in, grad_w_out) = (
        lax.optimization_barrier(
            (tokens_part, qkv_part, out_part, gain_one_part, bias_part, came_back, grad_w_in, grad_w_out)
        )
    )
    output = resid + jnp.dot(dispatch, came_back, preferred_element_type=jnp.float32)
    tokens_shared = scatter_sum(
        tokens_part.reshape(n_tensor, own_rows, width), "tensor", tensor_bits
    )
    grad_tokens = grad_resid + tokens_shared
    weights_part = jnp.concatenate([qkv_part, out_part], axis=0).astype(jnp.bfloat16)
    weights_total = sum_rows(weights_part, "expert").astype(jnp.float32)
    bias_slots = lax.dynamic_update_slice_in_dim(
        jnp.zeros((n_tensor * head_count, bucket_count), jnp.float32),
        bias_part,
        tensor_index * head_count,
        0,
    )
    small = jnp.concatenate(
        [gain_one_part, gain_two_part, router_part.T.reshape(-1), bias_slots.reshape(-1)]
    )
    small = butterfly(butterfly(small, "tensor"), "expert")
    count = 2 + expert_count
    columns = lax.dynamic_slice_in_dim(
        small[: count * width].reshape(count, width),
        tensor_index * (width // n_tensor),
        width // n_tensor,
        1,
    )
    bias_total = lax.dynamic_slice_in_dim(
        small[count * width :].reshape(n_tensor * head_count, bucket_count),
        tensor_index * head_count,
        head_count,
        0,
    )
    return (
        output,
        grad_tokens,
        columns[0],
        weights_total[: 3 * inner].reshape(3, inner, width).transpose(2, 0, 1),
        weights_total[3 * inner :],
        bias_total,
        columns[1],
        columns[2:].T,
        grad_w_in.astype(jnp.float32)[None],
        grad_w_out.astype(jnp.float32)[None],
    )


def solution(mesh):
    return jax.shard_map(
        local,
        mesh=mesh,
        in_specs=(
            P("expert", None),
            P("expert", None),
            P(("expert", "tensor"), None),
            P(),
            P(None, None, "tensor"),
            P("tensor", None),
            P("tensor", None),
            P(),
            P(),
            P("expert", None, "tensor"),
            P("expert", "tensor", None),
            P(("expert", "tensor"), None),
        ),
        out_specs=(
            P(("expert", "tensor"), None),
            P(("expert", "tensor"), None),
            P("tensor"),
            P(None, None, "tensor"),
            P("tensor", None),
            P("tensor", None),
            P("tensor"),
            P("tensor", None),
            P("expert", None, "tensor"),
            P("expert", "tensor", None),
        ),
        check_vma=False,
    )
```

```python
import functools

import jax
import jax.numpy as jnp
from jax import lax
from jax.experimental import pallas as pl
from jax.experimental.pallas import tpu as pltpu
from jax.sharding import PartitionSpec as P

BLOCK = 512
HALF = 256
EPSILON = 1e-06
BLOCKED = -1e30
VMEM_LIMIT = 48 * 2**20
LANES = 128
SPARE = 16


def mul(left, right, left_dim, right_dim):
    return lax.dot_general(
        left,
        right,
        (((left_dim,), (right_dim,)), ((), ())),
        preferred_element_type=jnp.float32,
    )


def spread_bias(bias_ref, spread_ref, head_count):
    for head in range(head_count):
        line = jnp.broadcast_to(bias_ref[head : head + 1, :], (2 * HALF, 2 * HALF))
        rolled = pltpu.roll(line, 0, 1, stride=1, stride_axis=0)
        spread_ref[head] = rolled[:, :HALF]


def fold_bias(total):
    line = jnp.concatenate([total, jnp.zeros_like(total)], axis=1)
    rows = lax.broadcasted_iota(jnp.int32, line.shape, 0)
    step = 1
    while step < 2 * HALF:
        line = jnp.where((rows & step) != 0, pltpu.roll(line, 2 * HALF - step, 1), line)
        step *= 2
    return jnp.sum(line, axis=0, keepdims=True)


def window_masks(lengths_ref, block_index, half, slots):
    query_pos = (
        lax.broadcasted_iota(jnp.int32, (1, HALF), 1) + block_index * BLOCK + half * HALF
    )
    start = jnp.zeros_like(query_pos)
    end = jnp.int32(0)
    for slot in range(slots):
        end = end + lengths_ref[0, slot]
        start = jnp.where(query_pos >= end, end, start)
    first_key = (block_index - 1) * BLOCK + half * HALF
    far_pos = lax.broadcasted_iota(jnp.int32, (HALF, 1), 0) + first_key
    near_pos = lax.broadcasted_iota(jnp.int32, (2 * HALF, 1), 0) + first_key + HALF
    return far_pos >= start, (near_pos >= start) & (near_pos <= query_pos)


def forward_kernel(
    place_ref, lengths_ref, tokens_ref, gain_ref, qkv_ref, out_ref, bias_ref,
    branch_ref, proj_ref, mixed_ref, log_ref,
    keys_ref, values_ref, spread_ref,
    *, head_count, head_dim, slots,
):
    block_index = pl.program_id(0)
    inner = head_count * head_dim

    @pl.when(block_index == 0)
    def _():
        keys_ref[:, :BLOCK] = jnp.zeros_like(keys_ref[:, :BLOCK])
        values_ref[:, :BLOCK] = jnp.zeros_like(values_ref[:, :BLOCK])
        spread_bias(bias_ref, spread_ref, head_count)

    @pl.when(block_index > 0)
    def _():
        keys_ref[:, :BLOCK] = keys_ref[:, BLOCK:]
        values_ref[:, :BLOCK] = values_ref[:, BLOCK:]

    widened = tokens_ref[...].astype(jnp.float32)
    inverse = lax.rsqrt(jnp.mean(widened * widened, axis=-1, keepdims=True) + EPSILON)
    hidden = (widened * inverse * gain_ref[...]).astype(jnp.bfloat16)
    projected = mul(qkv_ref[...], hidden, 1, 1)
    proj_ref[...] = projected.astype(jnp.bfloat16)
    for head in range(head_count):
        low = inner + head * head_dim
        keys_ref[head, BLOCK:, :] = projected[low : low + head_dim].T.astype(jnp.bfloat16)
    values_ref[:, BLOCK:] = proj_ref[2 * inner :, :]
    scale = head_dim**-0.5
    for half in range(BLOCK // HALF):
        far_mask, near_mask = window_masks(lengths_ref, block_index, half, slots)
        cols = slice(half * HALF, (half + 1) * HALF)
        window = slice(half * HALF, (half + 3) * HALF)
        for head in range(head_count):
            rows = slice(head * head_dim, (head + 1) * head_dim)
            query = proj_ref[rows, cols] * jnp.bfloat16(scale)
            scores = mul(keys_ref[head, window, :], query, 1, 0)
            far = jnp.where(far_mask, scores[:HALF], BLOCKED)
            near = jnp.where(near_mask, scores[HALF:] + spread_ref[head], BLOCKED)
            peak = jnp.maximum(
                jnp.max(far, axis=0, keepdims=True), jnp.max(near, axis=0, keepdims=True)
            )
            far = jnp.exp(far - peak)
            near = jnp.exp(near - peak)
            total = jnp.sum(far, axis=0, keepdims=True) + jnp.sum(near, axis=0, keepdims=True)
            share = 1.0 / total
            weights = jnp.concatenate(
                [(far * share).astype(jnp.bfloat16), (near * share).astype(jnp.bfloat16)], axis=0
            )
            mixed_ref[rows, cols] = mul(values_ref[rows, window], weights, 1, 0).astype(
                jnp.bfloat16
            )
            log_ref[head : head + 1, cols] = peak + jnp.log(total)
    branch_ref[...] = mul(mixed_ref[...], out_ref[...], 0, 0).astype(jnp.bfloat16)


def backward_kernel(
    place_ref, lengths_ref, tokens_ref, gain_ref, qkv_ref, out_ref, bias_ref,
    proj_ref, before_ref, mixed_ref, log_ref, near_grad_ref, away_grad_ref,
    part_ref, qkv_grad_ref, out_grad_ref, gain_grad_ref, bias_grad_ref, far_grad_ref,
    spread_ref, near_ref, far_ref, carry_ref, pieces_ref,
    *, head_count, head_dim, slots, block_count, placed,
):
    step = pl.program_id(0)
    block_index = block_count - 1 - step
    inner = head_count * head_dim

    @pl.when(step == 0)
    def _():
        spread_bias(bias_ref, spread_ref, head_count)
        near_ref[...] = jnp.zeros_like(near_ref)
        far_ref[...] = jnp.zeros_like(far_ref)
        carry_ref[...] = jnp.zeros_like(carry_ref)
        qkv_grad_ref[...] = jnp.zeros_like(qkv_grad_ref)
        out_grad_ref[...] = jnp.zeros_like(out_grad_ref)
        gain_grad_ref[...] = jnp.zeros_like(gain_grad_ref)
        bias_grad_ref[...] = jnp.zeros_like(bias_grad_ref)

    @pl.when(step > 0)
    def _():
        carry_ref[:, BLOCK:] = carry_ref[:, :BLOCK]
        carry_ref[:, :BLOCK] = jnp.zeros_like(carry_ref[:, :BLOCK])

    close = placed(block_index, place_ref) < block_count // 2
    grad_branch = jnp.where(close, near_grad_ref[0], away_grad_ref[0])
    out_grad_ref[...] += mul(mixed_ref[...], grad_branch, 1, 0)
    grad_mixed = mul(out_ref[...], grad_branch, 1, 1).astype(jnp.bfloat16)
    scale = head_dim**-0.5
    for head in range(head_count):
        rows = slice(head * head_dim, (head + 1) * head_dim)
        key_rows = slice(inner + head * head_dim, inner + (head + 1) * head_dim)
        value_rows = slice(2 * inner + head * head_dim, 2 * inner + (head + 1) * head_dim)
        keys_flat = jnp.concatenate([before_ref[key_rows, :], proj_ref[key_rows, :]], axis=1)
        values_flat = jnp.concatenate([before_ref[value_rows, :], proj_ref[value_rows, :]], axis=1)
        keys = keys_flat.astype(jnp.float32).T.astype(jnp.bfloat16)
        values = values_flat.astype(jnp.float32).T.astype(jnp.bfloat16)
        for half in range(BLOCK // HALF):
            far_mask, near_mask = window_masks(lengths_ref, block_index, half, slots)
            cols = slice(half * HALF, (half + 1) * HALF)
            window = slice(half * HALF, (half + 3) * HALF)
            query = proj_ref[rows, cols] * jnp.bfloat16(scale)
            scores = mul(keys[window], query, 1, 0)
            log_total = log_ref[head : head + 1, cols]
            far = jnp.where(far_mask, jnp.exp(scores[:HALF] - log_total), 0.0)
            near = jnp.where(
                near_mask, jnp.exp(scores[HALF:] + spread_ref[head] - log_total), 0.0
            )
            probs = jnp.concatenate([far, near], axis=0)
            grad_out = grad_mixed[rows, cols]
            grad_probs = mul(values[window], grad_out, 1, 0)
            row_inner = jnp.sum(probs * grad_probs, axis=0, keepdims=True)
            grad_scores = (probs * (grad_probs - row_inner)).astype(jnp.bfloat16)
            rounded = grad_scores.astype(jnp.float32)
            near_ref[head] += rounded[HALF:]
            far_ref[head : head + 1] += jnp.sum(rounded[:HALF], axis=0, keepdims=True)
            pieces_ref[rows, cols] = (
                mul(keys_flat[:, window], grad_scores, 1, 0) * scale
            ).astype(jnp.bfloat16)
            carry_ref[rows, window] += mul(query, grad_scores, 1, 1)
            carry_ref[key_rows, window] += mul(grad_out, probs.astype(jnp.bfloat16), 1, 1)
    pieces_ref[inner:, :] = carry_ref[:, BLOCK:].astype(jnp.bfloat16)
    widened = tokens_ref[...].astype(jnp.float32)
    inverse = lax.rsqrt(jnp.mean(widened * widened, axis=-1, keepdims=True) + EPSILON)
    normed = widened * inverse
    hidden = (normed * gain_ref[...]).astype(jnp.bfloat16)
    pieces = pieces_ref[...]
    qkv_grad_ref[...] += mul(pieces, hidden, 1, 0)
    grad_hidden = mul(pieces, qkv_ref[...], 0, 0)
    gain_grad_ref[...] += jnp.sum(
        (grad_hidden * normed).reshape(BLOCK // 8, 8, normed.shape[1]), axis=0
    )
    gained = grad_hidden * gain_ref[...]
    part_ref[...] = (
        inverse * (gained - normed * jnp.mean(gained * normed, axis=-1, keepdims=True))
    ).astype(jnp.bfloat16)

    @pl.when(step == block_count - 1)
    def _():
        for head in range(head_count):
            bias_grad_ref[head : head + 1, :] = fold_bias(near_ref[head])
        far_grad_ref[...] = far_ref[...]


def whole(shape):
    return pl.BlockSpec(shape, lambda *steps: (0,) * len(shape))


def reversed_bits(value, count):
    result = value * 0
    for bit in range(count):
        result = result + ((value >> bit) & 1) * 2 ** (count - 1 - bit)
    return result


def bias_line(rel_bias):
    head_count, bucket_count = rel_bias.shape
    line = rel_bias - rel_bias[:, bucket_count - 1 :]
    line = jnp.concatenate(
        [
            jnp.zeros((head_count, HALF), jnp.float32),
            line,
            jnp.zeros((head_count, HALF - bucket_count), jnp.float32),
        ],
        axis=1,
    )
    return jnp.concatenate([line, jnp.zeros((8 - head_count, 2 * HALF), jnp.float32)], axis=0)


def attend(place, tokens, lengths, gain, qkv_flat, attn_out, rel_bias):
    rows, width = tokens.shape
    inner = attn_out.shape[0]
    head_count = rel_bias.shape[0]
    head_dim = inner // head_count
    block_count = rows // BLOCK
    bits = (block_count - 1).bit_length()

    def placed(block, at):
        return reversed_bits(block ^ at[0], bits)

    return pl.pallas_call(
        functools.partial(
            forward_kernel, head_count=head_count, head_dim=head_dim, slots=lengths.shape[1]
        ),
        grid_spec=pltpu.PrefetchScalarGridSpec(
            num_scalar_prefetch=1,
            grid=(block_count,),
            in_specs=[
                pl.BlockSpec(memory_space=pltpu.SMEM),
                pl.BlockSpec((BLOCK, width), lambda step, at: (step, 0)),
                whole((1, width)),
                whole(qkv_flat.shape),
                whole(attn_out.shape),
                whole((8, 2 * HALF)),
            ],
            out_specs=[
                pl.BlockSpec((BLOCK, width), lambda step, at: (placed(step, at), 0)),
                pl.BlockSpec((3 * inner, BLOCK), lambda step, at: (0, step)),
                pl.BlockSpec((inner, BLOCK), lambda step, at: (0, step)),
                pl.BlockSpec((8, BLOCK), lambda step, at: (0, step)),
            ],
            scratch_shapes=[
                pltpu.VMEM((head_count, 2 * BLOCK, head_dim), jnp.bfloat16),
                pltpu.VMEM((inner, 2 * BLOCK), jnp.bfloat16),
                pltpu.VMEM((head_count, 2 * HALF, HALF), jnp.float32),
            ],
        ),
        out_shape=[
            jax.ShapeDtypeStruct((rows, width), jnp.bfloat16),
            jax.ShapeDtypeStruct((3 * inner, rows), jnp.bfloat16),
            jax.ShapeDtypeStruct((inner, rows), jnp.bfloat16),
            jax.ShapeDtypeStruct((8, rows), jnp.float32),
        ],
        compiler_params=pltpu.CompilerParams(vmem_limit_bytes=VMEM_LIMIT),
        cost_estimate=pl.CostEstimate(
            flops=2 * rows * width * inner * 4 + 4 * rows * 768 * inner,
            bytes_accessed=10 * rows * width,
            transcendentals=rows * 768 * head_count,
        ),
        name="attend_forward",
    )(place, lengths, tokens, gain[None, :], qkv_flat, attn_out, bias_line(rel_bias))


def attend_back(
    place, tokens, lengths, gain, qkv_flat, attn_out, rel_bias, projected, mixed, log_total, near_grad,
    away_grad,
):
    rows, width = tokens.shape
    inner = attn_out.shape[0]
    head_count, bucket_count = rel_bias.shape
    head_dim = inner // head_count
    block_count = rows // BLOCK
    last = block_count - 1
    bits = last.bit_length()

    def placed(block, at):
        return reversed_bits(block ^ at[0], bits)

    part, qkv_grad, out_grad, gain_grad, bias_grad, far_grad = pl.pallas_call(
        functools.partial(
            backward_kernel,
            head_count=head_count,
            head_dim=head_dim,
            slots=lengths.shape[1],
            block_count=block_count,
            placed=placed,
        ),
        grid_spec=pltpu.PrefetchScalarGridSpec(
            num_scalar_prefetch=1,
            grid=(block_count,),
            in_specs=[
                pl.BlockSpec(memory_space=pltpu.SMEM),
                pl.BlockSpec((BLOCK, width), lambda step, at: (last - step, 0)),
                whole((1, width)),
                whole(qkv_flat.shape),
                whole(attn_out.shape),
                whole((8, 2 * HALF)),
                pl.BlockSpec((3 * inner, BLOCK), lambda step, at: (0, last - step)),
                pl.BlockSpec(
                    (3 * inner, BLOCK), lambda step, at: (0, jnp.maximum(last - step - 1, 0))
                ),
                pl.BlockSpec((inner, BLOCK), lambda step, at: (0, last - step)),
                pl.BlockSpec((8, BLOCK), lambda step, at: (0, last - step)),
                pl.BlockSpec(
                    (1, BLOCK, width),
                    lambda step, at: (
                        jnp.minimum(placed(last - step, at), block_count // 2 - 1), 0, 0
                    ),
                ),
                pl.BlockSpec(
                    (1, BLOCK, width),
                    lambda step, at: (
                        jnp.maximum(placed(last - step, at) - block_count // 2, 0), 0, 0
                    ),
                ),
            ],
            out_specs=[
                pl.BlockSpec((BLOCK, width), lambda step, at: (last - step, 0)),
                whole((3 * inner, width)),
                whole((inner, width)),
                whole((8, width)),
                whole((8, 2 * HALF)),
                whole((8, HALF)),
            ],
            scratch_shapes=[
                pltpu.VMEM((head_count, 2 * HALF, HALF), jnp.float32),
                pltpu.VMEM((head_count, 2 * HALF, HALF), jnp.float32),
                pltpu.VMEM((8, HALF), jnp.float32),
                pltpu.VMEM((2 * inner, 2 * BLOCK), jnp.float32),
                pltpu.VMEM((3 * inner, BLOCK), jnp.bfloat16),
            ],
        ),
        out_shape=[
            jax.ShapeDtypeStruct((rows, width), jnp.bfloat16),
            jax.ShapeDtypeStruct((3 * inner, width), jnp.float32),
            jax.ShapeDtypeStruct((inner, width), jnp.float32),
            jax.ShapeDtypeStruct((8, width), jnp.float32),
            jax.ShapeDtypeStruct((8, 2 * HALF), jnp.float32),
            jax.ShapeDtypeStruct((8, HALF), jnp.float32),
        ],
        compiler_params=pltpu.CompilerParams(vmem_limit_bytes=VMEM_LIMIT),
        cost_estimate=pl.CostEstimate(
            flops=2 * rows * width * inner * 8 + 10 * rows * 768 * inner,
            bytes_accessed=14 * rows * width,
            transcendentals=rows * 768 * head_count,
        ),
        name="attend_backward",
    )(
        place, lengths, tokens, gain[None, :], qkv_flat, attn_out, bias_line(rel_bias),
        projected, projected, mixed, log_total, near_grad, away_grad,
    )
    near_grad = bias_grad[:head_count, HALF : HALF + bucket_count - 1]
    rest = jnp.sum(bias_grad[:head_count], axis=1) - jnp.sum(near_grad, axis=1)
    rest = rest + jnp.sum(far_grad[:head_count], axis=1)
    bias_part = jnp.concatenate([near_grad, rest[:, None]], axis=1)
    return part, qkv_grad, out_grad, jnp.sum(gain_grad, axis=0), bias_part


GELU_ONE = 0.7978845608028654
GELU_TWO = 0.044715


def shard_at(place_ref, position, shards):
    offset = 0
    bits = (shards - 1).bit_length()
    for bit in range(bits):
        offset += ((position >> bit) & 1) * 2 ** (bits - 1 - bit)
    return place_ref[0] ^ offset


def expert_kernel(
    place_ref, rows_ref, grads_ref, gap_ref, weights_ref, router_ref, *rest, sub
):
    sent_ref, act_ref, pre_ref, logit_ref = rest[-4:]
    shards = weights_ref.shape[0]
    sources, slots, width = rows_ref.shape
    step = max(1, sub // slots)

    @pl.loop(0, sources // step)
    def _(index):
        part = pl.ds(index * step, step)
        rows = rows_ref[part].reshape(step * slots, width)
        gap = gap_ref[part, 0].reshape(step * slots, gap_ref.shape[3]).astype(jnp.float32)
        logits = mul(rows, router_ref[...], 1, 0)
        logit_gap = jnp.sum(gap * logits, axis=-1, keepdims=True)
        gate = 1.0 / (1.0 + jnp.exp(-logit_gap))
        other_gate = 1.0 / (1.0 + jnp.exp(logit_gap))
        sent = jnp.zeros((step * slots, width), jnp.float32)
        gate_grads = jnp.zeros((step * slots, 1), jnp.float32)
        for shard in range(shards):
            weights = weights_ref[shard_at(place_ref, shard, shards)]
            pre = mul(rows, weights, 1, 0)
            grads = grads_ref[shard, part, 0].reshape(step * slots, weights.shape[1])
            grads = grads.astype(jnp.float32)
            square = pre * pre
            bent = jnp.tanh(pre * (GELU_ONE + GELU_ONE * GELU_TWO * square))
            share = 0.5 + 0.5 * bent
            act = pre * share
            slope = share + act * (1.0 - share) * (
                2.0 * GELU_ONE + 6.0 * GELU_ONE * GELU_TWO * square
            )
            gate_grads += jnp.sum(act * grads, axis=-1, keepdims=True)
            act_ref[shard, part, 0] = (
                (gate * act).astype(jnp.bfloat16).reshape(step, slots, weights.shape[1])
            )
            grad_pre = (gate * grads * slope).astype(jnp.bfloat16)
            pre_ref[shard, part, 0] = grad_pre.reshape(step, slots, weights.shape[1])
            sent += mul(grad_pre, weights, 1, 1)
        logit_grads = (gate * other_gate * gate_grads * gap).astype(jnp.bfloat16)
        logit_ref[part, 0] = logit_grads.reshape(step, slots, gap.shape[1])
        sent += mul(logit_grads, router_ref[...], 1, 1)
        sent_ref[part] = sent.astype(jnp.bfloat16).reshape(step, slots, width)


def serve(place, rows, act_grads, hot_gap, weights_in, router_wide, which, before, sub=256, tile=512):
    sources, slots, width = rows.shape
    shards = weights_in.shape[0]
    hidden = weights_in.shape[2]
    group = min(sources, max(1, tile // slots))
    wide = pl.BlockSpec((shards, group, 1, slots, hidden), lambda step, at: (0, step, which, 0, 0))
    lanes = pl.BlockSpec((group, 1, slots, hot_gap.shape[3]), lambda step, at: (step, which, 0, 0))
    narrow = pl.BlockSpec((group, slots, width), lambda step, at: (step, 0, 0))
    kept = [] if before is None else list(before)
    return pl.pallas_call(
        functools.partial(expert_kernel, sub=sub),
        grid_spec=pltpu.PrefetchScalarGridSpec(
            num_scalar_prefetch=1,
            grid=(sources // group,),
            in_specs=[narrow, wide, lanes, whole(weights_in.shape), whole(router_wide.shape)]
            + [pl.BlockSpec(memory_space=pl.ANY)] * len(kept),
            out_specs=[narrow, wide, wide, lanes],
        ),
        out_shape=[
            jax.ShapeDtypeStruct(rows.shape, jnp.bfloat16),
            jax.ShapeDtypeStruct(act_grads.shape, jnp.bfloat16),
            jax.ShapeDtypeStruct(act_grads.shape, jnp.bfloat16),
            jax.ShapeDtypeStruct(hot_gap.shape, jnp.bfloat16),
        ],
        input_output_aliases={6 + index: 1 + index for index in range(len(kept))},
        compiler_params=pltpu.CompilerParams(vmem_limit_bytes=VMEM_LIMIT),
        cost_estimate=pl.CostEstimate(
            flops=4 * sources * slots * width * shards * hidden,
            bytes_accessed=6 * sources * slots * shards * hidden,
            transcendentals=sources * slots * shards * hidden,
        ),
        name="expert_middle",
    )(place, rows, act_grads, hot_gap, weights_in, router_wide, *kept)


def act_grads_kernel(place_ref, rows_ref, weights_ref, out_ref):
    shards = weights_ref.shape[0]
    rows = rows_ref[...].reshape(-1, rows_ref.shape[2])
    for shard in range(shards):
        out_ref[shard] = mul(rows, weights_ref[shard_at(place_ref, shard, shards)], 1, 1).astype(
            jnp.bfloat16
        )


def slot_group(sources, capacity):
    return min(sources, max(1, BLOCK // capacity))


def act_grads_of(place, landed, weights, capacity):
    sources, _, width = landed.shape
    shards, hidden, _ = weights.shape
    group = slot_group(sources, capacity)
    tile = group * capacity
    return pl.pallas_call(
        act_grads_kernel,
        grid_spec=pltpu.PrefetchScalarGridSpec(
            num_scalar_prefetch=1,
            grid=(sources // group,),
            in_specs=[
                pl.BlockSpec((group, capacity, width), lambda step, at: (step, 0, 0)),
                whole(weights.shape),
            ],
            out_specs=pl.BlockSpec((shards, tile, hidden), lambda step, at: (0, step, 0)),
        ),
        out_shape=jax.ShapeDtypeStruct((shards, sources * capacity, hidden), jnp.bfloat16),
        compiler_params=pltpu.CompilerParams(vmem_limit_bytes=VMEM_LIMIT),
        cost_estimate=pl.CostEstimate(
            flops=2 * sources * capacity * width * shards * hidden,
            bytes_accessed=2 * sources * capacity * shards * hidden,
            transcendentals=0,
        ),
        name="act_grads",
    )(place, landed, weights)


def result_kernel(place_ref, act_ref, weights_ref, out_ref):
    shards = weights_ref.shape[0]
    total = mul(act_ref[0], weights_ref[shard_at(place_ref, 0, shards)], 1, 0)
    for shard in range(1, shards):
        total += mul(act_ref[shard], weights_ref[shard_at(place_ref, shard, shards)], 1, 0)
    out_ref[...] = total.astype(jnp.bfloat16)


def result_of(place, act, weights):
    shards, rows, hidden = act.shape
    width = weights.shape[2]
    return pl.pallas_call(
        result_kernel,
        grid_spec=pltpu.PrefetchScalarGridSpec(
            num_scalar_prefetch=1,
            grid=(rows // BLOCK,),
            in_specs=[
                pl.BlockSpec((shards, BLOCK, hidden), lambda step, at: (0, step, 0)),
                whole(weights.shape),
            ],
            out_specs=pl.BlockSpec((BLOCK, width), lambda step, at: (step, 0)),
        ),
        out_shape=jax.ShapeDtypeStruct((rows, width), jnp.bfloat16),
        compiler_params=pltpu.CompilerParams(vmem_limit_bytes=VMEM_LIMIT),
        cost_estimate=pl.CostEstimate(
            flops=2 * rows * width * shards * hidden,
            bytes_accessed=2 * rows * shards * hidden,
            transcendentals=0,
        ),
        name="expert_result",
    )(place, act, weights)


def out_weights_kernel(act_ref, landed_ref, out_ref):
    capacity = act_ref.shape[1] // landed_ref.shape[0]
    rows = landed_ref[:, :capacity].reshape(act_ref.shape[1], landed_ref.shape[2])
    out_ref[0] = mul(act_ref[0], rows, 0, 0).astype(jnp.bfloat16)


def out_weights_of(act, landed):
    shards, rows, hidden = act.shape
    width = landed.shape[2]
    return pl.pallas_call(
        out_weights_kernel,
        grid=(shards,),
        in_specs=[
            pl.BlockSpec((1, rows, hidden), lambda step: (step, 0, 0)),
            whole(landed.shape),
        ],
        out_specs=pl.BlockSpec((1, hidden, width), lambda step: (step, 0, 0)),
        out_shape=jax.ShapeDtypeStruct((shards, hidden, width), jnp.bfloat16),
        compiler_params=pltpu.CompilerParams(vmem_limit_bytes=VMEM_LIMIT),
        cost_estimate=pl.CostEstimate(
            flops=2 * rows * width * shards * hidden,
            bytes_accessed=2 * rows * shards * hidden,
            transcendentals=0,
        ),
        name="out_weights",
    )(act, landed)


def in_weights_kernel(first_ref, last_ref, grads_ref, logits_ref, out_ref, router_ref):
    sources, slots, width = first_ref.shape
    first = first_ref[...].reshape(sources * slots, width)
    last = last_ref[...].reshape(sources * slots, width)
    hidden = grads_ref.shape[4]
    out_ref[0] = (
        mul(first, grads_ref[0, :, 0].reshape(sources * slots, hidden), 0, 0)
        + mul(last, grads_ref[0, :, 1].reshape(sources * slots, hidden), 0, 0)
    ).astype(jnp.bfloat16)

    @pl.when(pl.program_id(0) == 0)
    def _():
        lanes = logits_ref.shape[3]
        router_ref[...] = mul(
            first, logits_ref[:, 0].reshape(sources * slots, lanes), 0, 0
        ) + mul(last, logits_ref[:, 1].reshape(sources * slots, lanes), 0, 0)


def in_weights_of(first, last, grads, logit_grads):
    shards, sources, _, slots, hidden = grads.shape
    width = first.shape[2]
    lanes = logit_grads.shape[3]
    return pl.pallas_call(
        in_weights_kernel,
        grid=(shards,),
        in_specs=[
            whole(first.shape),
            whole(last.shape),
            pl.BlockSpec((1,) + grads.shape[1:], lambda step: (step, 0, 0, 0, 0)),
            whole(logit_grads.shape),
        ],
        out_specs=[
            pl.BlockSpec((1, width, hidden), lambda step: (step, 0, 0)),
            whole((width, lanes)),
        ],
        out_shape=[
            jax.ShapeDtypeStruct((shards, width, hidden), jnp.bfloat16),
            jax.ShapeDtypeStruct((width, lanes), jnp.float32),
        ],
        compiler_params=pltpu.CompilerParams(vmem_limit_bytes=VMEM_LIMIT),
        cost_estimate=pl.CostEstimate(
            flops=4 * sources * slots * width * shards * hidden,
            bytes_accessed=4 * sources * slots * shards * hidden,
            transcendentals=0,
        ),
        name="in_weights",
    )(first, last, grads, logit_grads)


def rms_norm(values, gain):
    return values * lax.rsqrt(jnp.mean(values * values, axis=-1, keepdims=True) + EPSILON) * gain


def exchange(pieces):
    return lax.all_to_all(pieces, "expert", split_axis=0, concat_axis=0, tiled=True)


def halved(pieces, axis_name, bit):
    half = pieces.shape[0] // 2
    return pieces[:half], swap(pieces[half:].astype(jnp.bfloat16), axis_name, bit)


def joined(keep, got):
    return keep.astype(jnp.float32) + got.astype(jnp.float32)


def spread_sum(pieces, axis_name):
    for bit in range(bit_count(axis_name)):
        pieces = joined(*halved(pieces, axis_name, bit))
    return pieces[0]


def collect(piece, axis_name):
    pieces = piece[None]
    for bit in reversed(range(1, bit_count(axis_name))):
        pieces = jnp.concatenate([pieces, swap(pieces, axis_name, bit)], axis=0)
    return pieces, swap(pieces, axis_name, 0)


def swap(value, axis_name, bit):
    count = lax.axis_size(axis_name)
    return lax.ppermute(value, axis_name, [(i, i ^ (1 << bit)) for i in range(count)])


def own_bit(axis_name, bit):
    return (lax.axis_index(axis_name) >> bit) & 1


def scatter_sum(pieces, axis_name, order):
    count = (pieces.shape[0] - 1).bit_length()
    bits = sorted(order, reverse=True)
    if count > len(bits):
        bits = list(range(count))[::-1]
    total = pieces.reshape((2,) * count + pieces.shape[1:])
    for bit in order:
        dim = bits.index(bit)
        bits.remove(bit)
        mine = own_bit(axis_name, bit)
        keep = lax.dynamic_index_in_dim(total, mine, dim, keepdims=False)
        send = lax.dynamic_index_in_dim(total, 1 - mine, dim, keepdims=False)
        got = swap(send.astype(jnp.bfloat16), axis_name, bit)
        total = keep.astype(jnp.float32) + got.astype(jnp.float32)
    return total


def gather(value, axis_name, order, done=()):
    bits = list(done)
    for bit in order:
        value = value.reshape((2,) * len(bits) + value.shape[value.ndim - 2 :])
        bits = sorted(bits + [bit], reverse=True)
        dim = bits.index(bit)
        got = swap(value, axis_name, bit)
        first = own_bit(axis_name, bit) == 0
        value = jnp.stack([jnp.where(first, value, got), jnp.where(first, got, value)], axis=dim)
    return value


def butterfly(value, axis_name):
    for bit in range(bit_count(axis_name)):
        value = value + swap(value, axis_name, bit)
    return value


def bit_count(axis_name):
    return (lax.axis_size(axis_name) - 1).bit_length()


def scatter_rows(rows, axis_name):
    bits = list(range(bit_count(axis_name)))
    parts = lax.axis_size(axis_name)
    orders = [bits[turn:] + bits[:turn] for turn in (0, 1)]
    owned = [
        scatter_sum(half.reshape((parts, -1) + rows.shape[1:]), axis_name, order).astype(jnp.bfloat16)
        for half, order in zip(jnp.split(rows, 2, axis=0), orders)
    ]
    return owned, orders


def gather_rows(begun, orders, axis_name):
    halves = [
        gather(part, axis_name, order[::-1][1:], order[::-1][:1])
        for part, order in zip(begun, orders)
    ]
    return jnp.concatenate([half.reshape(-1, half.shape[-1]) for half in halves], axis=0)


def local(
    tokens,
    lengths,
    routes,
    norm1_gain,
    attn_qkv,
    attn_out,
    rel_bias,
    norm2_gain,
    router,
    expert_in,
    expert_out,
    out_grad,
):
    n_tensor = lax.axis_size("tensor")
    tensor_index = lax.axis_index("tensor")
    width = tokens.shape[1]
    own_rows = routes.shape[0]
    inner = attn_out.shape[0]
    head_count, bucket_count = rel_bias.shape
    expert_count = router.shape[1]
    capacity = max(2, 4 * own_rows // expert_count)

    route_hot = (routes[:, :, None] == jnp.arange(expert_count, dtype=jnp.int32)).astype(jnp.int32)
    counts = jnp.sum(route_hot, axis=1)
    before = jnp.cumsum(counts, axis=0) - counts
    slot_rank = jnp.sum(route_hot * before[:, None, :], axis=-1)
    expert_index = lax.axis_index("expert")
    slot_index = routes * capacity + slot_rank
    half_slots = capacity // 2

    def named(slot_ids):
        match = slot_index[:, :, None] == slot_ids[None, None, :]
        return (match[:, 0] | match[:, 1]).astype(jnp.bfloat16)

    slot_ids = jnp.arange(expert_count * capacity, dtype=jnp.int32)
    split_ids = slot_ids.reshape(expert_count, 2, half_slots)
    extra = jnp.full((expert_count, SPARE), -1, jnp.int32)
    long_ids = jnp.concatenate([slot_ids.reshape(expert_count, capacity), extra], axis=1)
    grad_slots = mul(named(long_ids.reshape(-1)), out_grad, 0, 0).astype(jnp.bfloat16)
    other_ids = jnp.sum(
        jnp.where(
            slot_index[:, :, None] == slot_ids[None, None, :], routes[:, ::-1, None] + 1, 0
        ),
        axis=(0, 1),
    ).astype(jnp.bfloat16)
    grad_slots = lax.dynamic_update_slice(
        grad_slots.reshape(expert_count, capacity + SPARE, width),
        other_ids.reshape(expert_count, 1, capacity),
        (0, capacity, 0),
    )
    landed = exchange(grad_slots)
    tokens, _ = lax.optimization_barrier((tokens, grad_slots))
    place = tensor_index.astype(jnp.int32)[None]
    halves = [named(split_ids[:, which].reshape(-1)) for which in range(2)]
    dispatch = named(slot_ids)

    qkv_flat = attn_qkv.transpose(1, 2, 0).reshape(3 * inner, width)
    branch, projected, mixed, log_total = attend(
        place, tokens, lengths, norm1_gain, qkv_flat, attn_out, rel_bias
    )
    branch = spread_sum(branch.reshape(n_tensor, own_rows, width), "tensor")
    own_tokens = lax.dynamic_slice_in_dim(tokens, tensor_index * own_rows, own_rows, 0)
    resid = own_tokens.astype(jnp.float32) + branch
    normed_two, norm2_pull = jax.vjp(rms_norm, resid, norm2_gain)
    hidden_two = normed_two.astype(jnp.bfloat16)
    outgoing = [mul(half, hidden_two, 0, 0).astype(jnp.bfloat16) for half in halves]
    outgoing, landed, expert_in = lax.optimization_barrier((outgoing, landed, expert_in))
    outgoing = [rows.reshape(expert_count, half_slots, width) for rows in outgoing]
    first_rows = exchange(outgoing[0])
    other_here = landed[:, capacity, :capacity].reshape(-1).astype(jnp.int32)
    weights_out = lax.all_gather(expert_out[0], "tensor")
    weights_in = lax.all_gather(expert_in[0], "tensor")
    act_grads = act_grads_of(place, landed, weights_out, capacity)
    shards, _, hidden = act_grads.shape
    act_grads = act_grads.reshape(shards, expert_count, 2, half_slots, hidden)
    lanes = jnp.arange(LANES, dtype=jnp.int32)
    hot_gap = (
        (lanes == expert_index).astype(jnp.int32)[None, :]
        - (other_here[:, None] == lanes[None, :] + 1).astype(jnp.int32)
    ).astype(jnp.bfloat16)
    hot_gap = hot_gap.reshape(expert_count, 2, half_slots, LANES)
    router_wide = jnp.pad(router, ((0, 0), (0, LANES - expert_count)))
    first_rows, act_grads, hot_gap, weights_in, last = lax.optimization_barrier(
        (first_rows, act_grads, hot_gap, weights_in, outgoing[1])
    )
    last_rows = exchange(last)
    sent_one, *kept = serve(place, first_rows, act_grads, hot_gap, weights_in, router_wide, 0, None)
    grad_sent_one = exchange(sent_one)
    sent_two, act, grad_pre, logit_grads = serve(
        place, last_rows, act_grads, hot_gap, weights_in, router_wide, 1, kept
    )
    act = act.reshape(shards, -1, hidden)
    grad_w_out = out_weights_of(act, landed)
    sent_two, grad_w_out, grad_pre = lax.optimization_barrier((sent_two, grad_w_out, grad_pre))
    grad_sent_two = exchange(sent_two)
    grad_w_out = spread_sum(grad_w_out, "tensor")
    grad_w_in, router_part = in_weights_of(first_rows, last_rows, grad_pre, logit_grads)
    router_part = router_part[:, :expert_count]
    act, grad_w_in = lax.optimization_barrier((act, grad_w_in))
    result = result_of(place, act, weights_out)
    grad_sent_one, grad_sent_two, result, dispatch, grad_w_out = lax.optimization_barrier(
        (grad_sent_one, grad_sent_two, result, dispatch, grad_w_out)
    )
    grad_in = out_grad.astype(jnp.float32)
    grad_hidden_two = mul(halves[0], grad_sent_one.reshape(-1, width), 1, 0) + mul(
        halves[1], grad_sent_two.reshape(-1, width), 1, 0
    )
    grad_resid_norm, gain_two_part = norm2_pull(grad_hidden_two)
    grad_resid = grad_in + grad_resid_norm
    grad_sharp = grad_resid.astype(jnp.bfloat16)
    grad_sharp, result = lax.optimization_barrier((grad_sharp, result))
    came_back = exchange(result.reshape(expert_count, capacity, width)).reshape(-1, width)
    near_grad, away_grad = collect(grad_sharp, "tensor")
    tensor_bits = bit_count("tensor")
    for bit in range(tensor_bits - 1):
        grad_w_in = joined(*halved(grad_w_in, "tensor", bit))
    near_grad, away_grad, grad_w_in = lax.optimization_barrier((near_grad, away_grad, grad_w_in))
    grad_w_in, grad_w_in_got = halved(grad_w_in, "tensor", tensor_bits - 1)

    tokens_part, qkv_part, out_part, gain_one_part, bias_part = attend_back(
        place, tokens, lengths, norm1_gain, qkv_flat, attn_out, rel_bias,
        projected, mixed, log_total, near_grad, away_grad,
    )
    tokens_part, qkv_part, out_part, gain_one_part, bias_part, came_back, grad_w_in_got = (
        lax.optimization_barrier(
            (tokens_part, qkv_part, out_part, gain_one_part, bias_part, came_back, grad_w_in_got)
        )
    )
    tokens_shared = lax.psum_scatter(tokens_part, "tensor", scatter_dimension=0, tiled=True)
    weights_part = jnp.concatenate([qkv_part, out_part], axis=0).astype(jnp.bfloat16)
    bias_slots = lax.dynamic_update_slice_in_dim(
        jnp.zeros((n_tensor * head_count, bucket_count), jnp.float32),
        bias_part,
        tensor_index * head_count,
        0,
    )
    small = jnp.concatenate(
        [gain_one_part, gain_two_part, router_part.T.reshape(-1), bias_slots.reshape(-1)]
    )
    small = butterfly(small, "tensor")
    owned, orders = scatter_rows(weights_part, "expert")
    owned, small = lax.optimization_barrier((owned, small))
    small = butterfly(small, "expert")
    begun = [gather(own, "expert", order[::-1][:1]) for own, order in zip(owned, orders)]
    begun, came_back, grad_w_in = lax.optimization_barrier((begun, came_back, grad_w_in))
    weights_total = gather_rows(begun, orders, "expert").astype(jnp.float32)
    output = resid + jnp.dot(dispatch, came_back, preferred_element_type=jnp.float32)
    grad_tokens = grad_resid + tokens_shared.astype(jnp.float32)
    grad_w_in = joined(grad_w_in, grad_w_in_got)
    count = 2 + expert_count
    columns = lax.dynamic_slice_in_dim(
        small[: count * width].reshape(count, width),
        tensor_index * (width // n_tensor),
        width // n_tensor,
        1,
    )
    bias_total = lax.dynamic_slice_in_dim(
        small[count * width :].reshape(n_tensor * head_count, bucket_count),
        tensor_index * head_count,
        head_count,
        0,
    )
    return (
        output,
        grad_tokens,
        columns[0],
        weights_total[: 3 * inner].reshape(3, inner, width).transpose(2, 0, 1),
        weights_total[3 * inner :],
        bias_total,
        columns[1],
        columns[2:].T,
        grad_w_in,
        grad_w_out[None],
    )


def solution(mesh):
    return jax.shard_map(
        local,
        mesh=mesh,
        in_specs=(
            P("expert", None),
            P("expert", None),
            P(("expert", "tensor"), None),
            P(),
            P(None, None, "tensor"),
            P("tensor", None),
            P("tensor", None),
            P(),
            P(),
            P("expert", None, "tensor"),
            P("expert", "tensor", None),
            P(("expert", "tensor"), None),
        ),
        out_specs=(
            P(("expert", "tensor"), None),
            P(("expert", "tensor"), None),
            P("tensor"),
            P(None, None, "tensor"),
            P("tensor", None),
            P("tensor", None),
            P("tensor"),
            P("tensor", None),
            P("expert", None, "tensor"),
            P("expert", "tensor", None),
        ),
        check_vma=False,
    )
```

```python
import functools

import jax
import jax.numpy as jnp
from jax import lax
from jax.experimental import pallas as pl
from jax.experimental.pallas import tpu as pltpu
from jax.sharding import PartitionSpec as P

BLOCK = 512
HALF = 256
EPSILON = 1e-06
BLOCKED = -1e30
VMEM_LIMIT = 48 * 2**20
LANES = 128
SPARE = 16
EXTRA = 64


def mul(left, right, left_dim, right_dim):
    return lax.dot_general(
        left,
        right,
        (((left_dim,), (right_dim,)), ((), ())),
        preferred_element_type=jnp.float32,
    )


def spread_bias(bias_ref, spread_ref, head_count):
    for head in range(head_count):
        line = jnp.broadcast_to(bias_ref[head : head + 1, :], (2 * HALF, 2 * HALF))
        rolled = pltpu.roll(line, 0, 1, stride=1, stride_axis=0)
        spread_ref[head] = rolled[:, :HALF]


def fold_bias(total):
    line = jnp.concatenate([total, jnp.zeros_like(total)], axis=1)
    rows = lax.broadcasted_iota(jnp.int32, line.shape, 0)
    step = 1
    while step < 2 * HALF:
        line = jnp.where((rows & step) != 0, pltpu.roll(line, 2 * HALF - step, 1), line)
        step *= 2
    return jnp.sum(line, axis=0, keepdims=True)


def window_masks(lengths_ref, block_index, half, slots):
    query_pos = (
        lax.broadcasted_iota(jnp.int32, (1, HALF), 1) + block_index * BLOCK + half * HALF
    )
    start = jnp.zeros_like(query_pos)
    end = jnp.int32(0)
    for slot in range(slots):
        end = end + lengths_ref[0, slot]
        start = jnp.where(query_pos >= end, end, start)
    first_key = (block_index - 1) * BLOCK + half * HALF
    far_pos = lax.broadcasted_iota(jnp.int32, (HALF, 1), 0) + first_key
    near_pos = lax.broadcasted_iota(jnp.int32, (2 * HALF, 1), 0) + first_key + HALF
    return far_pos >= start, (near_pos >= start) & (near_pos <= query_pos)


def forward_kernel(
    place_ref, lengths_ref, tokens_ref, gain_ref, qkv_ref, out_ref, bias_ref,
    branch_ref, proj_ref, mixed_ref, log_ref,
    keys_ref, values_ref, spread_ref,
    *, head_count, head_dim, slots,
):
    block_index = pl.program_id(0)
    inner = head_count * head_dim

    @pl.when(block_index == 0)
    def _():
        keys_ref[:, :BLOCK] = jnp.zeros_like(keys_ref[:, :BLOCK])
        values_ref[:, :BLOCK] = jnp.zeros_like(values_ref[:, :BLOCK])
        spread_bias(bias_ref, spread_ref, head_count)

    @pl.when(block_index > 0)
    def _():
        keys_ref[:, :BLOCK] = keys_ref[:, BLOCK:]
        values_ref[:, :BLOCK] = values_ref[:, BLOCK:]

    widened = tokens_ref[...].astype(jnp.float32)
    inverse = lax.rsqrt(jnp.mean(widened * widened, axis=-1, keepdims=True) + EPSILON)
    hidden = (widened * inverse * gain_ref[...]).astype(jnp.bfloat16)
    projected = mul(qkv_ref[...], hidden, 1, 1)
    proj_ref[...] = projected.astype(jnp.bfloat16)
    for head in range(head_count):
        low = inner + head * head_dim
        keys_ref[head, BLOCK:, :] = projected[low : low + head_dim].T.astype(jnp.bfloat16)
    values_ref[:, BLOCK:] = proj_ref[2 * inner :, :]
    scale = head_dim**-0.5
    for half in range(BLOCK // HALF):
        far_mask, near_mask = window_masks(lengths_ref, block_index, half, slots)
        cols = slice(half * HALF, (half + 1) * HALF)
        window = slice(half * HALF, (half + 3) * HALF)
        for head in range(head_count):
            rows = slice(head * head_dim, (head + 1) * head_dim)
            query = proj_ref[rows, cols] * jnp.bfloat16(scale)
            scores = mul(keys_ref[head, window, :], query, 1, 0)
            far = jnp.where(far_mask, scores[:HALF], BLOCKED)
            near = jnp.where(near_mask, scores[HALF:] + spread_ref[head], BLOCKED)
            peak = jnp.maximum(
                jnp.max(far, axis=0, keepdims=True), jnp.max(near, axis=0, keepdims=True)
            )
            far = jnp.exp(far - peak)
            near = jnp.exp(near - peak)
            total = jnp.sum(far, axis=0, keepdims=True) + jnp.sum(near, axis=0, keepdims=True)
            share = 1.0 / total
            weights = jnp.concatenate(
                [(far * share).astype(jnp.bfloat16), (near * share).astype(jnp.bfloat16)], axis=0
            )
            mixed_ref[rows, cols] = mul(values_ref[rows, window], weights, 1, 0).astype(
                jnp.bfloat16
            )
            log_ref[head : head + 1, cols] = peak + jnp.log(total)
    branch_ref[...] = mul(mixed_ref[...], out_ref[...], 0, 0).astype(jnp.bfloat16)


def backward_kernel(
    place_ref, lengths_ref, tokens_ref, gain_ref, qkv_ref, out_ref, bias_ref,
    proj_ref, before_ref, mixed_ref, log_ref, near_grad_ref, away_grad_ref,
    small_ref, gain_two_ref, part_ref, packed_ref,
    spread_ref, near_ref, far_ref, carry_ref, pieces_ref, qkv_grad_ref, out_grad_ref, gain_grad_ref,
    *, head_count, head_dim, slots, block_count, placed,
):
    step = pl.program_id(0)
    block_index = block_count - 1 - step
    inner = head_count * head_dim

    @pl.when(step == 0)
    def _():
        spread_bias(bias_ref, spread_ref, head_count)
        near_ref[...] = jnp.zeros_like(near_ref)
        far_ref[...] = jnp.zeros_like(far_ref)
        carry_ref[...] = jnp.zeros_like(carry_ref)
        qkv_grad_ref[...] = jnp.zeros_like(qkv_grad_ref)
        out_grad_ref[...] = jnp.zeros_like(out_grad_ref)
        gain_grad_ref[...] = jnp.zeros_like(gain_grad_ref)

    @pl.when(step > 0)
    def _():
        carry_ref[:, BLOCK:] = carry_ref[:, :BLOCK]
        carry_ref[:, :BLOCK] = jnp.zeros_like(carry_ref[:, :BLOCK])

    close = placed(block_index, place_ref) < block_count // 2
    grad_branch = jnp.where(close, near_grad_ref[0], away_grad_ref[0])
    out_grad_ref[...] += mul(mixed_ref[...], grad_branch, 1, 0)
    grad_mixed = mul(out_ref[...], grad_branch, 1, 1).astype(jnp.bfloat16)
    scale = head_dim**-0.5
    for head in range(head_count):
        rows = slice(head * head_dim, (head + 1) * head_dim)
        key_rows = slice(inner + head * head_dim, inner + (head + 1) * head_dim)
        value_rows = slice(2 * inner + head * head_dim, 2 * inner + (head + 1) * head_dim)
        keys_flat = jnp.concatenate([before_ref[key_rows, :], proj_ref[key_rows, :]], axis=1)
        values_flat = jnp.concatenate([before_ref[value_rows, :], proj_ref[value_rows, :]], axis=1)
        keys = keys_flat.astype(jnp.float32).T.astype(jnp.bfloat16)
        values = values_flat.astype(jnp.float32).T.astype(jnp.bfloat16)
        for half in range(BLOCK // HALF):
            far_mask, near_mask = window_masks(lengths_ref, block_index, half, slots)
            cols = slice(half * HALF, (half + 1) * HALF)
            window = slice(half * HALF, (half + 3) * HALF)
            query = proj_ref[rows, cols] * jnp.bfloat16(scale)
            scores = mul(keys[window], query, 1, 0)
            log_total = log_ref[head : head + 1, cols]
            far = jnp.where(far_mask, jnp.exp(scores[:HALF] - log_total), 0.0)
            near = jnp.where(
                near_mask, jnp.exp(scores[HALF:] + spread_ref[head] - log_total), 0.0
            )
            probs = jnp.concatenate([far, near], axis=0)
            grad_out = grad_mixed[rows, cols]
            grad_probs = mul(values[window], grad_out, 1, 0)
            row_inner = jnp.sum(probs * grad_probs, axis=0, keepdims=True)
            grad_scores = (probs * (grad_probs - row_inner)).astype(jnp.bfloat16)
            rounded = grad_scores.astype(jnp.float32)
            near_ref[head] += rounded[HALF:]
            far_ref[head : head + 1] += jnp.sum(rounded[:HALF], axis=0, keepdims=True)
            pieces_ref[rows, cols] = (
                mul(keys_flat[:, window], grad_scores, 1, 0) * scale
            ).astype(jnp.bfloat16)
            carry_ref[rows, window] += mul(query, grad_scores, 1, 1)
            carry_ref[key_rows, window] += mul(grad_out, probs.astype(jnp.bfloat16), 1, 1)
    pieces_ref[inner:, :] = carry_ref[:, BLOCK:].astype(jnp.bfloat16)
    widened = tokens_ref[...].astype(jnp.float32)
    inverse = lax.rsqrt(jnp.mean(widened * widened, axis=-1, keepdims=True) + EPSILON)
    normed = widened * inverse
    hidden = (normed * gain_ref[...]).astype(jnp.bfloat16)
    pieces = pieces_ref[...]
    qkv_grad_ref[...] += mul(pieces, hidden, 1, 0)
    grad_hidden = mul(pieces, qkv_ref[...], 0, 0)
    gain_grad_ref[...] += jnp.sum(
        (grad_hidden * normed).reshape(BLOCK // 8, 8, normed.shape[1]), axis=0
    )
    gained = grad_hidden * gain_ref[...]
    part_ref[...] = (
        inverse * (gained - normed * jnp.mean(gained * normed, axis=-1, keepdims=True))
    ).astype(jnp.bfloat16)

    @pl.when(step == block_count - 1)
    def _():
        width = gain_grad_ref.shape[1]
        packed_ref[: 3 * inner, :] = qkv_grad_ref[...].astype(jnp.bfloat16)
        packed_ref[3 * inner : 4 * inner, :] = out_grad_ref[...].astype(jnp.bfloat16)
        lines = []
        for head in range(head_count):
            total = fold_bias(near_ref[head])
            near = total[:, HALF : HALF + LANES]
            lane = lax.broadcasted_iota(jnp.int32, near.shape, 1)
            inside = jnp.where(lane < LANES - 1, near, 0.0)
            rest = (
                jnp.sum(total, axis=1, keepdims=True)
                - jnp.sum(inside, axis=1, keepdims=True)
                + jnp.sum(far_ref[head : head + 1], axis=1, keepdims=True)
            )
            lines.append(jnp.where(lane < LANES - 1, near, rest))
        lines.append(jnp.zeros((1, width - head_count * LANES), jnp.float32))
        bias_row = jnp.concatenate(lines, axis=1)
        gain_row = jnp.sum(gain_grad_ref[...], axis=0, keepdims=True)
        rows = lax.broadcasted_iota(jnp.int32, small_ref.shape, 0)
        gain_two_row = jnp.sum(gain_two_ref[...], axis=0, keepdims=True)
        small = jnp.where(rows == 0, gain_row, jnp.where(rows == 1, bias_row, small_ref[...]))
        small = jnp.where(rows == 2, gain_two_row, small)
        packed_ref[4 * inner :, :] = small.astype(jnp.bfloat16)


def whole(shape):
    return pl.BlockSpec(shape, lambda *steps: (0,) * len(shape))


def reversed_bits(value, count):
    result = value * 0
    for bit in range(count):
        result = result + ((value >> bit) & 1) * 2 ** (count - 1 - bit)
    return result


def bias_line(rel_bias):
    head_count, bucket_count = rel_bias.shape
    line = rel_bias - rel_bias[:, bucket_count - 1 :]
    line = jnp.concatenate(
        [
            jnp.zeros((head_count, HALF), jnp.float32),
            line,
            jnp.zeros((head_count, HALF - bucket_count), jnp.float32),
        ],
        axis=1,
    )
    return jnp.concatenate([line, jnp.zeros((8 - head_count, 2 * HALF), jnp.float32)], axis=0)


def attend(place, tokens, lengths, gain, qkv_flat, attn_out, rel_bias):
    rows, width = tokens.shape
    inner = attn_out.shape[0]
    head_count = rel_bias.shape[0]
    head_dim = inner // head_count
    block_count = rows // BLOCK
    bits = (block_count - 1).bit_length()

    def placed(block, at):
        return reversed_bits(block ^ at[0], bits)

    return pl.pallas_call(
        functools.partial(
            forward_kernel, head_count=head_count, head_dim=head_dim, slots=lengths.shape[1]
        ),
        grid_spec=pltpu.PrefetchScalarGridSpec(
            num_scalar_prefetch=1,
            grid=(block_count,),
            in_specs=[
                pl.BlockSpec(memory_space=pltpu.SMEM),
                pl.BlockSpec((BLOCK, width), lambda step, at: (step, 0)),
                whole((1, width)),
                whole(qkv_flat.shape),
                whole(attn_out.shape),
                whole((8, 2 * HALF)),
            ],
            out_specs=[
                pl.BlockSpec((BLOCK, width), lambda step, at: (placed(step, at), 0)),
                pl.BlockSpec((3 * inner, BLOCK), lambda step, at: (0, step)),
                pl.BlockSpec((inner, BLOCK), lambda step, at: (0, step)),
                pl.BlockSpec((8, BLOCK), lambda step, at: (0, step)),
            ],
            scratch_shapes=[
                pltpu.VMEM((head_count, 2 * BLOCK, head_dim), jnp.bfloat16),
                pltpu.VMEM((inner, 2 * BLOCK), jnp.bfloat16),
                pltpu.VMEM((head_count, 2 * HALF, HALF), jnp.float32),
            ],
        ),
        out_shape=[
            jax.ShapeDtypeStruct((rows, width), jnp.bfloat16),
            jax.ShapeDtypeStruct((3 * inner, rows), jnp.bfloat16),
            jax.ShapeDtypeStruct((inner, rows), jnp.bfloat16),
            jax.ShapeDtypeStruct((8, rows), jnp.float32),
        ],
        compiler_params=pltpu.CompilerParams(vmem_limit_bytes=VMEM_LIMIT),
        cost_estimate=pl.CostEstimate(
            flops=2 * rows * width * inner * 4 + 4 * rows * 768 * inner,
            bytes_accessed=10 * rows * width,
            transcendentals=rows * 768 * head_count,
        ),
        name="attend_forward",
    )(place, lengths, tokens, gain[None, :], qkv_flat, attn_out, bias_line(rel_bias))


def attend_back(
    place, tokens, lengths, gain, qkv_flat, attn_out, rel_bias, projected, mixed, log_total, near_grad,
    away_grad, small, gain_two,
):
    rows, width = tokens.shape
    inner = attn_out.shape[0]
    head_count, bucket_count = rel_bias.shape
    head_dim = inner // head_count
    block_count = rows // BLOCK
    last = block_count - 1
    bits = last.bit_length()

    def placed(block, at):
        return reversed_bits(block ^ at[0], bits)

    return pl.pallas_call(
        functools.partial(
            backward_kernel,
            head_count=head_count,
            head_dim=head_dim,
            slots=lengths.shape[1],
            block_count=block_count,
            placed=placed,
        ),
        grid_spec=pltpu.PrefetchScalarGridSpec(
            num_scalar_prefetch=1,
            grid=(block_count,),
            in_specs=[
                pl.BlockSpec(memory_space=pltpu.SMEM),
                pl.BlockSpec((BLOCK, width), lambda step, at: (last - step, 0)),
                whole((1, width)),
                whole(qkv_flat.shape),
                whole(attn_out.shape),
                whole((8, 2 * HALF)),
                pl.BlockSpec((3 * inner, BLOCK), lambda step, at: (0, last - step)),
                pl.BlockSpec(
                    (3 * inner, BLOCK), lambda step, at: (0, jnp.maximum(last - step - 1, 0))
                ),
                pl.BlockSpec((inner, BLOCK), lambda step, at: (0, last - step)),
                pl.BlockSpec((8, BLOCK), lambda step, at: (0, last - step)),
                pl.BlockSpec(
                    (1, BLOCK, width),
                    lambda step, at: (
                        jnp.minimum(placed(last - step, at), block_count // 2 - 1), 0, 0
                    ),
                ),
                pl.BlockSpec(
                    (1, BLOCK, width),
                    lambda step, at: (
                        jnp.maximum(placed(last - step, at) - block_count // 2, 0), 0, 0
                    ),
                ),
                whole(small.shape),
                whole(gain_two.shape),
            ],
            out_specs=[
                pl.BlockSpec((BLOCK, width), lambda step, at: (last - step, 0)),
                whole((4 * inner + small.shape[0], width)),
            ],
            scratch_shapes=[
                pltpu.VMEM((head_count, 2 * HALF, HALF), jnp.float32),
                pltpu.VMEM((head_count, 2 * HALF, HALF), jnp.float32),
                pltpu.VMEM((8, HALF), jnp.float32),
                pltpu.VMEM((2 * inner, 2 * BLOCK), jnp.float32),
                pltpu.VMEM((3 * inner, BLOCK), jnp.bfloat16),
                pltpu.VMEM((3 * inner, width), jnp.float32),
                pltpu.VMEM((inner, width), jnp.float32),
                pltpu.VMEM((8, width), jnp.float32),
            ],
        ),
        out_shape=[
            jax.ShapeDtypeStruct((rows, width), jnp.bfloat16),
            jax.ShapeDtypeStruct((4 * inner + small.shape[0], width), jnp.bfloat16),
        ],
        compiler_params=pltpu.CompilerParams(vmem_limit_bytes=VMEM_LIMIT),
        cost_estimate=pl.CostEstimate(
            flops=2 * rows * width * inner * 8 + 10 * rows * 768 * inner,
            bytes_accessed=14 * rows * width,
            transcendentals=rows * 768 * head_count,
        ),
        name="attend_backward",
    )(
        place, lengths, tokens, gain[None, :], qkv_flat, attn_out, bias_line(rel_bias),
        projected, projected, mixed, log_total, near_grad, away_grad,
        small, gain_two,
    )


GELU_ONE = 0.7978845608028654
GELU_TWO = 0.044715


def shard_at(place_ref, position, shards):
    offset = 0
    bits = (shards - 1).bit_length()
    for bit in range(bits):
        offset += ((position >> bit) & 1) * 2 ** (bits - 1 - bit)
    return place_ref[0] ^ offset


def expert_kernel(
    place_ref, rows_ref, grads_ref, gap_ref, weights_ref, router_ref, *rest, sub
):
    sent_ref, act_ref, pre_ref, logit_ref = rest[-4:]
    shards = weights_ref.shape[0]
    sources, slots, width = rows_ref.shape
    step = max(1, sub // slots)

    @pl.loop(0, sources // step)
    def _(index):
        part = pl.ds(index * step, step)
        rows = rows_ref[part].reshape(step * slots, width)
        gap = gap_ref[part, 0].reshape(step * slots, gap_ref.shape[3]).astype(jnp.float32)
        logits = mul(rows, router_ref[...], 1, 0)
        logit_gap = jnp.sum(gap * logits, axis=-1, keepdims=True)
        gate = 1.0 / (1.0 + jnp.exp(-logit_gap))
        other_gate = 1.0 / (1.0 + jnp.exp(logit_gap))
        sent = jnp.zeros((step * slots, width), jnp.float32)
        gate_grads = jnp.zeros((step * slots, 1), jnp.float32)
        for shard in range(shards):
            weights = weights_ref[shard_at(place_ref, shard, shards)]
            pre = mul(rows, weights, 1, 0)
            grads = grads_ref[shard, part, 0].reshape(step * slots, weights.shape[1])
            grads = grads.astype(jnp.float32)
            square = pre * pre
            bent = jnp.tanh(pre * (GELU_ONE + GELU_ONE * GELU_TWO * square))
            share = 0.5 + 0.5 * bent
            act = pre * share
            slope = share + act * (1.0 - share) * (
                2.0 * GELU_ONE + 6.0 * GELU_ONE * GELU_TWO * square
            )
            gate_grads += jnp.sum(act * grads, axis=-1, keepdims=True)
            act_ref[shard, part, 0] = (
                (gate * act).astype(jnp.bfloat16).reshape(step, slots, weights.shape[1])
            )
            grad_pre = (gate * grads * slope).astype(jnp.bfloat16)
            pre_ref[shard, part, 0] = grad_pre.reshape(step, slots, weights.shape[1])
            sent += mul(grad_pre, weights, 1, 1)
        logit_grads = (gate * other_gate * gate_grads * gap).astype(jnp.bfloat16)
        logit_ref[part, 0] = logit_grads.reshape(step, slots, gap.shape[1])
        sent += mul(logit_grads, router_ref[...], 1, 1)
        sent_ref[part] = sent.astype(jnp.bfloat16).reshape(step, slots, width)


def serve(place, rows, act_grads, hot_gap, weights_in, router_wide, which, before, sub=256, tile=512):
    sources, slots, width = rows.shape
    shards = weights_in.shape[0]
    hidden = weights_in.shape[2]
    group = min(sources, max(1, tile // slots))
    wide = pl.BlockSpec((shards, group, 1, slots, hidden), lambda step, at: (0, step, which, 0, 0))
    lanes = pl.BlockSpec((group, 1, slots, hot_gap.shape[3]), lambda step, at: (step, which, 0, 0))
    narrow = pl.BlockSpec((group, slots, width), lambda step, at: (step, 0, 0))
    kept = [] if before is None else list(before)
    return pl.pallas_call(
        functools.partial(expert_kernel, sub=sub),
        grid_spec=pltpu.PrefetchScalarGridSpec(
            num_scalar_prefetch=1,
            grid=(sources // group,),
            in_specs=[narrow, wide, lanes, whole(weights_in.shape), whole(router_wide.shape)]
            + [pl.BlockSpec(memory_space=pl.ANY)] * len(kept),
            out_specs=[narrow, wide, wide, lanes],
        ),
        out_shape=[
            jax.ShapeDtypeStruct(rows.shape, jnp.bfloat16),
            jax.ShapeDtypeStruct(act_grads.shape, jnp.bfloat16),
            jax.ShapeDtypeStruct(act_grads.shape, jnp.bfloat16),
            jax.ShapeDtypeStruct(hot_gap.shape, jnp.bfloat16),
        ],
        input_output_aliases={6 + index: 1 + index for index in range(len(kept))},
        compiler_params=pltpu.CompilerParams(vmem_limit_bytes=VMEM_LIMIT),
        cost_estimate=pl.CostEstimate(
            flops=4 * sources * slots * width * shards * hidden,
            bytes_accessed=6 * sources * slots * shards * hidden,
            transcendentals=sources * slots * shards * hidden,
        ),
        name="expert_middle",
    )(place, rows, act_grads, hot_gap, weights_in, router_wide, *kept)


def act_grads_kernel(place_ref, rows_ref, weights_ref, out_ref):
    shards = weights_ref.shape[0]
    rows = rows_ref[...].reshape(-1, rows_ref.shape[2])
    for shard in range(shards):
        out_ref[shard] = mul(rows, weights_ref[shard_at(place_ref, shard, shards)], 1, 1).astype(
            jnp.bfloat16
        )


def slot_group(sources, capacity):
    return min(sources, max(1, BLOCK // capacity))


def act_grads_of(place, landed, weights, capacity):
    sources, _, width = landed.shape
    shards, hidden, _ = weights.shape
    group = slot_group(sources, capacity)
    tile = group * capacity
    return pl.pallas_call(
        act_grads_kernel,
        grid_spec=pltpu.PrefetchScalarGridSpec(
            num_scalar_prefetch=1,
            grid=(sources // group,),
            in_specs=[
                pl.BlockSpec((group, capacity, width), lambda step, at: (step, 0, 0)),
                whole(weights.shape),
            ],
            out_specs=pl.BlockSpec((shards, tile, hidden), lambda step, at: (0, step, 0)),
        ),
        out_shape=jax.ShapeDtypeStruct((shards, sources * capacity, hidden), jnp.bfloat16),
        compiler_params=pltpu.CompilerParams(vmem_limit_bytes=VMEM_LIMIT),
        cost_estimate=pl.CostEstimate(
            flops=2 * sources * capacity * width * shards * hidden,
            bytes_accessed=2 * sources * capacity * shards * hidden,
            transcendentals=0,
        ),
        name="act_grads",
    )(place, landed, weights)


def result_kernel(place_ref, act_ref, weights_ref, out_ref):
    shards = weights_ref.shape[0]
    total = mul(act_ref[0], weights_ref[shard_at(place_ref, 0, shards)], 1, 0)
    for shard in range(1, shards):
        total += mul(act_ref[shard], weights_ref[shard_at(place_ref, shard, shards)], 1, 0)
    out_ref[...] = total.astype(jnp.bfloat16)


def result_of(place, act, weights):
    shards, rows, hidden = act.shape
    width = weights.shape[2]
    return pl.pallas_call(
        result_kernel,
        grid_spec=pltpu.PrefetchScalarGridSpec(
            num_scalar_prefetch=1,
            grid=(rows // BLOCK,),
            in_specs=[
                pl.BlockSpec((shards, BLOCK, hidden), lambda step, at: (0, step, 0)),
                whole(weights.shape),
            ],
            out_specs=pl.BlockSpec((BLOCK, width), lambda step, at: (step, 0)),
        ),
        out_shape=jax.ShapeDtypeStruct((rows, width), jnp.bfloat16),
        compiler_params=pltpu.CompilerParams(vmem_limit_bytes=VMEM_LIMIT),
        cost_estimate=pl.CostEstimate(flops=0, bytes_accessed=0, transcendentals=0),
        name="expert_result",
    )(place, act, weights)


def store_half(value, send_ref, keep_ref):
    half = pl.num_programs(0) // 2

    @pl.when(pl.program_id(0) < half)
    def _():
        send_ref[0] = value

    @pl.when(pl.program_id(0) >= half)
    def _():
        keep_ref[0] = value


def half_specs(shards, rows, columns):
    half = shards // 2
    shape = jax.ShapeDtypeStruct((half, rows, columns), jnp.bfloat16)
    specs = [
        pl.BlockSpec((1, rows, columns), lambda step: (jnp.minimum(step, half - 1), 0, 0)),
        pl.BlockSpec((1, rows, columns), lambda step: (jnp.maximum(step - half, 0), 0, 0)),
    ]
    return specs, [shape, shape]


def send_first(step, shards):
    return (step + shards // 2) % shards


def out_weights_kernel(act_ref, landed_ref, send_ref, keep_ref):
    capacity = act_ref.shape[1] // landed_ref.shape[0]
    rows = landed_ref[:, :capacity].reshape(act_ref.shape[1], landed_ref.shape[2])
    store_half(mul(act_ref[0], rows, 0, 0).astype(jnp.bfloat16), send_ref, keep_ref)


def out_weights_of(act, landed):
    shards, rows, hidden = act.shape
    width = landed.shape[2]
    specs, shapes = half_specs(shards, hidden, width)
    return pl.pallas_call(
        out_weights_kernel,
        grid=(shards,),
        in_specs=[
            pl.BlockSpec((1, rows, hidden), lambda step: (send_first(step, shards), 0, 0)),
            whole(landed.shape),
        ],
        out_specs=specs,
        out_shape=shapes,
        compiler_params=pltpu.CompilerParams(vmem_limit_bytes=VMEM_LIMIT),
        cost_estimate=pl.CostEstimate(flops=0, bytes_accessed=0, transcendentals=0),
        name="out_weights",
    )(act, landed)


def in_weights_kernel(
    first_ref, last_ref, grads_ref, logits_ref, send_ref, keep_ref, router_ref
):
    sources, slots, width = first_ref.shape
    first = first_ref[...].reshape(sources * slots, width)
    last = last_ref[...].reshape(sources * slots, width)
    hidden = grads_ref.shape[4]
    total = mul(first, grads_ref[0, :, 0].reshape(sources * slots, hidden), 0, 0) + mul(
        last, grads_ref[0, :, 1].reshape(sources * slots, hidden), 0, 0
    )
    store_half(total.astype(jnp.bfloat16), send_ref, keep_ref)

    @pl.when(pl.program_id(0) == 0)
    def _():
        lanes = logits_ref.shape[3]
        router_ref[...] = mul(
            first, logits_ref[:, 0].reshape(sources * slots, lanes), 0, 0
        ) + mul(last, logits_ref[:, 1].reshape(sources * slots, lanes), 0, 0)


def in_weights_of(first, last, grads, logit_grads):
    shards, sources, _, slots, hidden = grads.shape
    width = first.shape[2]
    lanes = logit_grads.shape[3]
    specs, shapes = half_specs(shards, width, hidden)
    return pl.pallas_call(
        in_weights_kernel,
        grid=(shards,),
        in_specs=[
            whole(first.shape),
            whole(last.shape),
            pl.BlockSpec(
                (1,) + grads.shape[1:], lambda step: (send_first(step, shards), 0, 0, 0, 0)
            ),
            whole(logit_grads.shape),
        ],
        out_specs=specs + [whole((width, lanes))],
        out_shape=shapes + [jax.ShapeDtypeStruct((width, lanes), jnp.float32)],
        compiler_params=pltpu.CompilerParams(vmem_limit_bytes=VMEM_LIMIT),
        cost_estimate=pl.CostEstimate(flops=0, bytes_accessed=0, transcendentals=0),
        name="in_weights",
    )(first, last, grads, logit_grads)


def place_kernel(routes_ref, grad_ref, slots_ref, index_ref, *, capacity, spare):
    expert = pl.program_id(0)
    experts = pl.num_programs(0)
    tokens = routes_ref.shape[1]
    lanes = lax.broadcasted_iota(jnp.int32, (LANES, tokens), 0)
    hot = [(routes_ref[choice : choice + 1, :] == lanes) for choice in range(2)]

    @pl.when(expert == 0)
    def _():
        counts = (hot[0] | hot[1]).astype(jnp.bfloat16)
        earlier = (
            lax.broadcasted_iota(jnp.int32, (tokens, tokens), 0)
            < lax.broadcasted_iota(jnp.int32, (tokens, tokens), 1)
        ).astype(jnp.bfloat16)
        before = mul(counts, earlier, 1, 0)
        for choice in range(2):
            rank = jnp.sum(jnp.where(hot[choice], before, 0.0), axis=0, keepdims=True)
            index_ref[choice : choice + 1, :] = (
                routes_ref[choice : choice + 1, :] * capacity + rank.astype(jnp.int32)
            )

    slot = lax.broadcasted_iota(jnp.int32, (capacity, tokens), 0) + expert * capacity
    named = [(index_ref[choice : choice + 1, :] == slot) for choice in range(2)]
    spread = (named[0] | named[1]).astype(jnp.bfloat16)
    slots_ref[0, :capacity] = mul(spread, grad_ref[...], 1, 0).astype(jnp.bfloat16)
    others = [
        jnp.broadcast_to(routes_ref[1 - choice : 2 - choice, :] + 1, (spare, tokens))
        .astype(jnp.float32)
        .astype(jnp.bfloat16)
        for choice in range(2)
    ]
    ids = mul(others[0], named[0].astype(jnp.bfloat16), 1, 1) + mul(
        others[1], named[1].astype(jnp.bfloat16), 1, 1
    )
    width = slots_ref.shape[2]
    padded = jnp.concatenate([ids, jnp.zeros((spare, width - capacity), jnp.float32)], axis=1)
    slots_ref[0, capacity:] = padded.astype(jnp.bfloat16)


def place_rows(routes, out_grad, experts, capacity):
    tokens, width = out_grad.shape
    return pl.pallas_call(
        functools.partial(place_kernel, capacity=capacity, spare=SPARE),
        grid=(experts,),
        in_specs=[whole((2, tokens)), whole((tokens, width))],
        out_specs=[
            pl.BlockSpec((1, capacity + SPARE, width), lambda step: (step, 0, 0)),
            whole((8, tokens)),
        ],
        out_shape=[
            jax.ShapeDtypeStruct((experts, capacity + SPARE, width), jnp.bfloat16),
            jax.ShapeDtypeStruct((8, tokens), jnp.int32),
        ],
        compiler_params=pltpu.CompilerParams(vmem_limit_bytes=VMEM_LIMIT),
        cost_estimate=pl.CostEstimate(
            flops=2 * experts * capacity * tokens * width,
            bytes_accessed=2 * experts * capacity * width,
            transcendentals=0,
        ),
        name="place_rows",
    )(routes.T, out_grad)


def combine_kernel(
    first_ref, first_rows_ref, last_ref, last_rows_ref, resid_ref, gain_ref, grad_ref,
    out_ref, sharp_ref, gain_grad_ref,
):
    grad_hidden = mul(first_ref[...], first_rows_ref[...], 1, 0) + mul(
        last_ref[...], last_rows_ref[...], 1, 0
    )
    resid = resid_ref[...]
    inverse = lax.rsqrt(jnp.mean(resid * resid, axis=-1, keepdims=True) + EPSILON)
    normed = resid * inverse

    @pl.when(pl.program_id(0) == 0)
    def _():
        gain_grad_ref[...] = jnp.zeros_like(gain_grad_ref)

    rows, width = resid.shape
    gain_grad_ref[...] += jnp.sum((grad_hidden * normed).reshape(rows // 8, 8, width), axis=0)
    gained = grad_hidden * gain_ref[...]
    total = grad_ref[...].astype(jnp.float32) + inverse * (
        gained - normed * jnp.mean(gained * normed, axis=-1, keepdims=True)
    )
    out_ref[...] = total
    sharp_ref[...] = total.astype(jnp.bfloat16)


def combine(first, first_rows, last, last_rows, resid, gain, out_grad):
    rows, width = resid.shape
    slots = first_rows.shape[0]
    tile = pl.BlockSpec((HALF, width), lambda step: (step, 0))
    named = pl.BlockSpec((HALF, slots), lambda step: (step, 0))
    total, sharp, gain_grad = pl.pallas_call(
        combine_kernel,
        grid=(rows // HALF,),
        in_specs=[
            named, whole((slots, width)), named, whole((slots, width)), tile, whole((1, width)), tile,
        ],
        out_specs=[tile, tile, whole((8, width))],
        out_shape=[
            jax.ShapeDtypeStruct((rows, width), jnp.float32),
            jax.ShapeDtypeStruct((rows, width), jnp.bfloat16),
            jax.ShapeDtypeStruct((8, width), jnp.float32),
        ],
        compiler_params=pltpu.CompilerParams(vmem_limit_bytes=VMEM_LIMIT),
        cost_estimate=pl.CostEstimate(
            flops=4 * rows * slots * width,
            bytes_accessed=4 * slots * width + 12 * rows * width,
            transcendentals=rows,
        ),
        name="combine",
    )(first, first_rows, last, last_rows, resid, gain[None, :], out_grad)
    return total, sharp, gain_grad


def rms_norm(values, gain):
    return values * lax.rsqrt(jnp.mean(values * values, axis=-1, keepdims=True) + EPSILON) * gain


def exchange(pieces):
    return lax.all_to_all(pieces, "expert", split_axis=0, concat_axis=0, tiled=True)


def halved(pieces, axis_name, bit):
    half = pieces.shape[0] // 2
    return pieces[:half], swap(pieces[half:].astype(jnp.bfloat16), axis_name, bit)


def joined(keep, got):
    return keep.astype(jnp.float32) + got.astype(jnp.float32)


def joined_low(keep, got):
    return joined(keep, got).astype(jnp.bfloat16)


def spread_sum(pieces, axis_name):
    for bit in range(bit_count(axis_name)):
        pieces = joined(*halved(pieces, axis_name, bit))
    return pieces[0]


def spread_rest(pieces, axis_name):
    for bit in range(1, bit_count(axis_name)):
        pieces = joined(*halved(pieces, axis_name, bit))
    return pieces[0]


def collect(piece, axis_name):
    pieces = piece[None]
    for bit in reversed(range(1, bit_count(axis_name))):
        pieces = jnp.concatenate([pieces, swap(pieces, axis_name, bit)], axis=0)
    return pieces


def swap(value, axis_name, bit):
    count = lax.axis_size(axis_name)
    return lax.ppermute(value, axis_name, [(i, i ^ (1 << bit)) for i in range(count)])


def own_bit(axis_name, bit):
    return (lax.axis_index(axis_name) >> bit) & 1


def bit_groups(axis_name):
    bits = list(range(bit_count(axis_name)))
    return [tuple(bits[:1])] + [tuple(bits[low : low + 2]) for low in range(1, len(bits), 2)]


def send_over(value, axis_name, group, offset):
    mask = sum(((offset >> place) & 1) << bit for place, bit in enumerate(group))
    count = lax.axis_size(axis_name)
    return lax.ppermute(value, axis_name, [(i, i ^ mask) for i in range(count)])


def group_sum(value, axis_name):
    for group in bit_groups(axis_name):
        parts = [send_over(value, axis_name, group, m) for m in range(1, 2 ** len(group))]
        value = sum(parts, value)
    return value


def scatter_sum(pieces, axis_name, order):
    bits = list(range(bit_count(axis_name)))[::-1]
    total = pieces.reshape((2,) * len(bits) + pieces.shape[1:])
    for group in order:
        parts = []
        for offset in range(2 ** len(group)):
            part, left = total, list(bits)
            for place, bit in enumerate(group):
                dim = left.index(bit)
                left.remove(bit)
                index = own_bit(axis_name, bit) ^ ((offset >> place) & 1)
                part = lax.dynamic_index_in_dim(part, index, dim, keepdims=False)
            if offset:
                part = send_over(part.astype(jnp.bfloat16), axis_name, group, offset)
            parts.append(part.astype(jnp.float32))
        total = sum(parts[1:], parts[0])
        bits = left
    return total


def gather(value, axis_name, order, done=()):
    bits = list(done)
    for group in order:
        value = value.reshape((2,) * len(bits) + value.shape[value.ndim - 2 :])
        size = 2 ** len(group)
        parts = [value] + [send_over(value, axis_name, group, m) for m in range(1, size)]
        for place, bit in enumerate(group):
            flip = own_bit(axis_name, bit) == 1
            parts = [jnp.where(flip, parts[m ^ (1 << place)], parts[m]) for m in range(size)]
        stacked = jnp.stack(parts).reshape((2,) * len(group) + value.shape)
        now = sorted(group, reverse=True) + bits
        bits = sorted(now, reverse=True)
        order_of = [now.index(bit) for bit in bits]
        value = stacked.transpose(order_of + list(range(len(bits), stacked.ndim)))
    return value


def bit_count(axis_name):
    return (lax.axis_size(axis_name) - 1).bit_length()


def scatter_rows(rows, axis_name):
    groups = bit_groups(axis_name)
    parts = lax.axis_size(axis_name)
    middle = rows.shape[0] // EXTRA // 2 * EXTRA
    orders = [groups[turn:] + groups[:turn] for turn in (0, 1)]
    owned = [
        scatter_sum(half.reshape((parts, -1) + rows.shape[1:]), axis_name, order).astype(
            jnp.bfloat16
        )
        for half, order in zip((rows[:middle], rows[middle:]), orders)
    ]
    return owned, orders


def gather_rows(begun, orders, axis_name):
    halves = []
    for part, order in zip(begun, orders):
        done = sorted(order[-1], reverse=True)
        halves.append(gather(part, axis_name, order[::-1][1:], done))
    return jnp.concatenate([half.reshape(-1, half.shape[-1]) for half in halves], axis=0)


def local(
    tokens,
    lengths,
    routes,
    norm1_gain,
    attn_qkv,
    attn_out,
    rel_bias,
    norm2_gain,
    router,
    expert_in,
    expert_out,
    out_grad,
):
    n_tensor = lax.axis_size("tensor")
    tensor_index = lax.axis_index("tensor")
    width = tokens.shape[1]
    own_rows = routes.shape[0]
    inner = attn_out.shape[0]
    head_count, bucket_count = rel_bias.shape
    expert_count = router.shape[1]
    capacity = max(2, 4 * own_rows // expert_count)

    expert_index = lax.axis_index("expert")
    grad_slots, slot_index = place_rows(routes, out_grad, expert_count, capacity)
    slot_index = slot_index[:2].T
    half_slots = capacity // 2

    def named(slot_ids):
        match = slot_index[:, :, None] == slot_ids[None, None, :]
        return (match[:, 0] | match[:, 1]).astype(jnp.bfloat16)

    slot_ids = jnp.arange(expert_count * capacity, dtype=jnp.int32)
    split_ids = slot_ids.reshape(expert_count, 2, half_slots)
    landed = exchange(grad_slots)
    tokens, _ = lax.optimization_barrier((tokens, grad_slots))
    place = tensor_index.astype(jnp.int32)[None]
    halves = [named(split_ids[:, which].reshape(-1)) for which in range(2)]
    dispatch = named(slot_ids)

    qkv_flat = attn_qkv.transpose(1, 2, 0).reshape(3 * inner, width)
    branch, projected, mixed, log_total = attend(
        place, tokens, lengths, norm1_gain, qkv_flat, attn_out, rel_bias
    )
    branch = spread_sum(branch.reshape(n_tensor, own_rows, width), "tensor")
    own_tokens = lax.dynamic_slice_in_dim(tokens, tensor_index * own_rows, own_rows, 0)
    resid = own_tokens.astype(jnp.float32) + branch
    hidden_two = rms_norm(resid, norm2_gain).astype(jnp.bfloat16)
    outgoing = [mul(half, hidden_two, 0, 0).astype(jnp.bfloat16) for half in halves]
    outgoing, landed, expert_in = lax.optimization_barrier((outgoing, landed, expert_in))
    outgoing = [rows.reshape(expert_count, half_slots, width) for rows in outgoing]
    first_rows = exchange(outgoing[0])
    other_here = landed[:, capacity, :capacity].reshape(-1).astype(jnp.int32)
    weights_out = lax.all_gather(expert_out[0], "tensor")
    weights_in = lax.all_gather(expert_in[0], "tensor")
    act_grads = act_grads_of(place, landed, weights_out, capacity)
    shards, _, hidden = act_grads.shape
    act_grads = act_grads.reshape(shards, expert_count, 2, half_slots, hidden)
    lanes = jnp.arange(LANES, dtype=jnp.int32)
    hot_gap = (
        (lanes == expert_index).astype(jnp.int32)[None, :]
        - (other_here[:, None] == lanes[None, :] + 1).astype(jnp.int32)
    ).astype(jnp.bfloat16)
    hot_gap = hot_gap.reshape(expert_count, 2, half_slots, LANES)
    router_wide = jnp.pad(router, ((0, 0), (0, LANES - expert_count)))
    first_rows, act_grads, hot_gap, weights_in, last = lax.optimization_barrier(
        (first_rows, act_grads, hot_gap, weights_in, outgoing[1])
    )
    last_rows = exchange(last)
    sent_one, *kept = serve(place, first_rows, act_grads, hot_gap, weights_in, router_wide, 0, None)
    grad_sent_one = exchange(sent_one)
    sent_two, act, grad_pre, logit_grads = serve(
        place, last_rows, act_grads, hot_gap, weights_in, router_wide, 1, kept
    )
    act = act.reshape(shards, -1, hidden)
    out_send, out_keep = out_weights_of(act, landed)
    sent_two, out_send, out_keep, grad_pre = lax.optimization_barrier(
        (sent_two, out_send, out_keep, grad_pre)
    )
    grad_sent_two = exchange(sent_two)
    out_half = joined_low(out_keep, swap(out_send, "tensor", 0))
    out_half, grad_pre = lax.optimization_barrier((out_half, grad_pre))
    grad_w_out = spread_rest(out_half, "tensor")
    in_send, in_keep, router_part = in_weights_of(first_rows, last_rows, grad_pre, logit_grads)
    router_part = router_part[:, :expert_count]
    count = 2 + expert_count
    extra = -(-(count + 1) // EXTRA) * EXTRA - count - 1
    blank = jnp.zeros((1, width), jnp.float32)
    small = jnp.concatenate(
        [blank, blank, blank, router_part.T, jnp.zeros((extra, width), jnp.float32)], axis=0
    )
    act, in_send, in_keep, small = lax.optimization_barrier((act, in_send, in_keep, small))
    in_got = swap(in_send, "tensor", 0)
    result = result_of(place, act, weights_out)
    grad_sent_one, grad_sent_two, result, dispatch, grad_w_out = lax.optimization_barrier(
        (grad_sent_one, grad_sent_two, result, dispatch, grad_w_out)
    )
    grad_resid, grad_sharp, gain_two_part = combine(
        halves[0],
        grad_sent_one.reshape(-1, width),
        halves[1],
        grad_sent_two.reshape(-1, width),
        resid,
        norm2_gain,
        out_grad,
    )
    came_back = exchange(result.reshape(expert_count, capacity, width)).reshape(-1, width)
    tensor_bits = bit_count("tensor")
    grad_w_in = joined_low(in_keep, in_got)
    for bit in range(1, tensor_bits - 1):
        grad_w_in = joined_low(*halved(grad_w_in, "tensor", bit))
    near_grad = collect(grad_sharp, "tensor")
    near_grad, grad_w_in = lax.optimization_barrier((near_grad, grad_w_in))
    away_grad = swap(near_grad, "tensor", 0)
    grad_w_in, grad_w_in_got = halved(grad_w_in, "tensor", tensor_bits - 1)

    tokens_part, weights_part = attend_back(
        place, tokens, lengths, norm1_gain, qkv_flat, attn_out, rel_bias,
        projected, mixed, log_total, near_grad, away_grad, small, gain_two_part,
    )
    tokens_part, weights_part, came_back, grad_w_in_got = lax.optimization_barrier(
        (tokens_part, weights_part, came_back, grad_w_in_got)
    )
    tokens_shared = lax.psum_scatter(tokens_part, "tensor", scatter_dimension=0, tiled=True)
    owned, orders = scatter_rows(weights_part, "expert")
    owned = lax.optimization_barrier(owned)
    begun = [gather(own, "expert", order[::-1][:1]) for own, order in zip(owned, orders)]
    begun, came_back, grad_w_in, tokens_shared = lax.optimization_barrier(
        (begun, came_back, grad_w_in, tokens_shared)
    )
    weights_total = gather_rows(begun, orders, "expert").astype(jnp.float32)
    output = resid + jnp.dot(dispatch, came_back, preferred_element_type=jnp.float32)
    grad_tokens = grad_resid + tokens_shared.astype(jnp.float32)
    grad_w_in = joined(grad_w_in, grad_w_in_got)
    low = 4 * inner
    bias_total = weights_total[low + 1, : rel_bias.size].reshape(rel_bias.shape)
    small = weights_total[low : low + count + 1]
    small = group_sum(jnp.concatenate([small[:1], small[2:]], axis=0), "tensor")
    columns = lax.dynamic_slice_in_dim(
        small, tensor_index * (width // n_tensor), width // n_tensor, 1
    )
    return (
        output,
        grad_tokens,
        columns[0],
        weights_total[: 3 * inner].reshape(3, inner, width).transpose(2, 0, 1),
        weights_total[3 * inner : 4 * inner],
        bias_total,
        columns[1],
        columns[2:].T,
        grad_w_in,
        grad_w_out[None],
    )


def solution(mesh):
    return jax.shard_map(
        local,
        mesh=mesh,
        in_specs=(
            P("expert", None),
            P("expert", None),
            P(("expert", "tensor"), None),
            P(),
            P(None, None, "tensor"),
            P("tensor", None),
            P("tensor", None),
            P(),
            P(),
            P("expert", None, "tensor"),
            P("expert", "tensor", None),
            P(("expert", "tensor"), None),
        ),
        out_specs=(
            P(("expert", "tensor"), None),
            P(("expert", "tensor"), None),
            P("tensor"),
            P(None, None, "tensor"),
            P("tensor", None),
            P("tensor", None),
            P("tensor"),
            P("tensor", None),
            P("expert", None, "tensor"),
            P("expert", "tensor", None),
        ),
        check_vma=False,
    )
```

```python
import functools

import jax
import jax.numpy as jnp
from jax import lax
from jax.experimental import pallas as pl
from jax.experimental.pallas import tpu as pltpu
from jax.sharding import PartitionSpec as P

BLOCK = 512
HALF = 256
EPSILON = 1e-06
BLOCKED = -1e30
VMEM_LIMIT = 48 * 2**20
LANES = 128
SPARE = 16
EXTRA = 64


def mul(left, right, left_dim, right_dim):
    return lax.dot_general(
        left,
        right,
        (((left_dim,), (right_dim,)), ((), ())),
        preferred_element_type=jnp.float32,
    )


def spread_bias(bias_ref, spread_ref, head_count):
    for head in range(head_count):
        line = jnp.broadcast_to(bias_ref[head : head + 1, :], (2 * HALF, 2 * HALF))
        rolled = pltpu.roll(line, 0, 1, stride=1, stride_axis=0)
        spread_ref[head] = rolled[:, :HALF]


def fold_bias(total):
    line = jnp.concatenate([total, jnp.zeros_like(total)], axis=1)
    rows = lax.broadcasted_iota(jnp.int32, line.shape, 0)
    step = 1
    while step < 2 * HALF:
        line = jnp.where((rows & step) != 0, pltpu.roll(line, 2 * HALF - step, 1), line)
        step *= 2
    return jnp.sum(line, axis=0, keepdims=True)


def window_masks(lengths_ref, block_index, half, slots):
    query_pos = (
        lax.broadcasted_iota(jnp.int32, (1, HALF), 1) + block_index * BLOCK + half * HALF
    )
    start = jnp.zeros_like(query_pos)
    end = jnp.int32(0)
    for slot in range(slots):
        end = end + lengths_ref[0, slot]
        start = jnp.where(query_pos >= end, end, start)
    first_key = (block_index - 1) * BLOCK + half * HALF
    far_pos = lax.broadcasted_iota(jnp.int32, (HALF, 1), 0) + first_key
    near_pos = lax.broadcasted_iota(jnp.int32, (2 * HALF, 1), 0) + first_key + HALF
    return far_pos >= start, (near_pos >= start) & (near_pos <= query_pos)


def forward_kernel(
    place_ref, lengths_ref, tokens_ref, gain_ref, qkv_ref, out_ref, bias_ref,
    branch_ref, proj_ref, mixed_ref, log_ref,
    keys_ref, values_ref, spread_ref,
    *, head_count, head_dim, slots,
):
    block_index = pl.program_id(0)
    inner = head_count * head_dim

    @pl.when(block_index == 0)
    def _():
        keys_ref[:, :BLOCK] = jnp.zeros_like(keys_ref[:, :BLOCK])
        values_ref[:, :BLOCK] = jnp.zeros_like(values_ref[:, :BLOCK])
        spread_bias(bias_ref, spread_ref, head_count)

    @pl.when(block_index > 0)
    def _():
        keys_ref[:, :BLOCK] = keys_ref[:, BLOCK:]
        values_ref[:, :BLOCK] = values_ref[:, BLOCK:]

    widened = tokens_ref[...].astype(jnp.float32)
    inverse = lax.rsqrt(jnp.mean(widened * widened, axis=-1, keepdims=True) + EPSILON)
    hidden = (widened * inverse * gain_ref[...]).astype(jnp.bfloat16)
    projected = mul(qkv_ref[...], hidden, 1, 1)
    proj_ref[...] = projected.astype(jnp.bfloat16)
    for head in range(head_count):
        low = inner + head * head_dim
        keys_ref[head, BLOCK:, :] = projected[low : low + head_dim].T.astype(jnp.bfloat16)
    values_ref[:, BLOCK:] = proj_ref[2 * inner :, :]
    scale = head_dim**-0.5
    for half in range(BLOCK // HALF):
        far_mask, near_mask = window_masks(lengths_ref, block_index, half, slots)
        cols = slice(half * HALF, (half + 1) * HALF)
        window = slice(half * HALF, (half + 3) * HALF)
        for head in range(head_count):
            rows = slice(head * head_dim, (head + 1) * head_dim)
            query = proj_ref[rows, cols] * jnp.bfloat16(scale)
            scores = mul(keys_ref[head, window, :], query, 1, 0)
            far = jnp.where(far_mask, scores[:HALF], BLOCKED)
            near = jnp.where(near_mask, scores[HALF:] + spread_ref[head], BLOCKED)
            peak = jnp.maximum(
                jnp.max(far, axis=0, keepdims=True), jnp.max(near, axis=0, keepdims=True)
            )
            far = jnp.exp(far - peak)
            near = jnp.exp(near - peak)
            total = jnp.sum(far, axis=0, keepdims=True) + jnp.sum(near, axis=0, keepdims=True)
            share = 1.0 / total
            weights = jnp.concatenate(
                [(far * share).astype(jnp.bfloat16), (near * share).astype(jnp.bfloat16)], axis=0
            )
            mixed_ref[rows, cols] = mul(values_ref[rows, window], weights, 1, 0).astype(
                jnp.bfloat16
            )
            log_ref[head : head + 1, cols] = peak + jnp.log(total)
    branch_ref[...] = mul(mixed_ref[...], out_ref[...], 0, 0).astype(jnp.bfloat16)


def backward_kernel(
    place_ref, lengths_ref, tokens_ref, gain_ref, qkv_ref, out_ref, bias_ref,
    proj_ref, before_ref, mixed_ref, log_ref, near_grad_ref, away_grad_ref,
    small_ref, gain_two_ref, part_ref, packed_ref,
    spread_ref, near_ref, far_ref, carry_ref, pieces_ref, qkv_grad_ref, out_grad_ref, gain_grad_ref,
    *, head_count, head_dim, slots, block_count, placed,
):
    step = pl.program_id(0)
    block_index = block_count - 1 - step
    inner = head_count * head_dim

    @pl.when(step == 0)
    def _():
        spread_bias(bias_ref, spread_ref, head_count)
        near_ref[...] = jnp.zeros_like(near_ref)
        far_ref[...] = jnp.zeros_like(far_ref)
        carry_ref[...] = jnp.zeros_like(carry_ref)
        qkv_grad_ref[...] = jnp.zeros_like(qkv_grad_ref)
        out_grad_ref[...] = jnp.zeros_like(out_grad_ref)
        gain_grad_ref[...] = jnp.zeros_like(gain_grad_ref)

    @pl.when(step > 0)
    def _():
        carry_ref[:, BLOCK:] = carry_ref[:, :BLOCK]
        carry_ref[:, :BLOCK] = jnp.zeros_like(carry_ref[:, :BLOCK])

    close = placed(block_index, place_ref) < block_count // 2
    grad_branch = jnp.where(close, near_grad_ref[0], away_grad_ref[0])
    out_grad_ref[...] += mul(mixed_ref[...], grad_branch, 1, 0)
    grad_mixed = mul(out_ref[...], grad_branch, 1, 1).astype(jnp.bfloat16)
    scale = head_dim**-0.5
    for head in range(head_count):
        rows = slice(head * head_dim, (head + 1) * head_dim)
        key_rows = slice(inner + head * head_dim, inner + (head + 1) * head_dim)
        value_rows = slice(2 * inner + head * head_dim, 2 * inner + (head + 1) * head_dim)
        keys_flat = jnp.concatenate([before_ref[key_rows, :], proj_ref[key_rows, :]], axis=1)
        values_flat = jnp.concatenate([before_ref[value_rows, :], proj_ref[value_rows, :]], axis=1)
        keys = keys_flat.astype(jnp.float32).T.astype(jnp.bfloat16)
        values = values_flat.astype(jnp.float32).T.astype(jnp.bfloat16)
        for half in range(BLOCK // HALF):
            far_mask, near_mask = window_masks(lengths_ref, block_index, half, slots)
            cols = slice(half * HALF, (half + 1) * HALF)
            window = slice(half * HALF, (half + 3) * HALF)
            query = proj_ref[rows, cols] * jnp.bfloat16(scale)
            scores = mul(keys[window], query, 1, 0)
            log_total = log_ref[head : head + 1, cols]
            far = jnp.where(far_mask, jnp.exp(scores[:HALF] - log_total), 0.0)
            near = jnp.where(
                near_mask, jnp.exp(scores[HALF:] + spread_ref[head] - log_total), 0.0
            )
            probs = jnp.concatenate([far, near], axis=0)
            grad_out = grad_mixed[rows, cols]
            grad_probs = mul(values[window], grad_out, 1, 0)
            row_inner = jnp.sum(probs * grad_probs, axis=0, keepdims=True)
            grad_scores = (probs * (grad_probs - row_inner)).astype(jnp.bfloat16)
            rounded = grad_scores.astype(jnp.float32)
            near_ref[head] += rounded[HALF:]
            far_ref[head : head + 1] += jnp.sum(rounded[:HALF], axis=0, keepdims=True)
            pieces_ref[rows, cols] = (
                mul(keys_flat[:, window], grad_scores, 1, 0) * scale
            ).astype(jnp.bfloat16)
            carry_ref[rows, window] += mul(query, grad_scores, 1, 1)
            carry_ref[key_rows, window] += mul(grad_out, probs.astype(jnp.bfloat16), 1, 1)
    pieces_ref[inner:, :] = carry_ref[:, BLOCK:].astype(jnp.bfloat16)
    widened = tokens_ref[...].astype(jnp.float32)
    inverse = lax.rsqrt(jnp.mean(widened * widened, axis=-1, keepdims=True) + EPSILON)
    normed = widened * inverse
    hidden = (normed * gain_ref[...]).astype(jnp.bfloat16)
    pieces = pieces_ref[...]
    qkv_grad_ref[...] += mul(pieces, hidden, 1, 0)
    grad_hidden = mul(pieces, qkv_ref[...], 0, 0)
    gain_grad_ref[...] += jnp.sum(
        (grad_hidden * normed).reshape(BLOCK // 8, 8, normed.shape[1]), axis=0
    )
    gained = grad_hidden * gain_ref[...]
    part_ref[...] = (
        inverse * (gained - normed * jnp.mean(gained * normed, axis=-1, keepdims=True))
    ).astype(jnp.bfloat16)

    @pl.when(step == block_count - 1)
    def _():
        width = gain_grad_ref.shape[1]
        packed_ref[: 3 * inner, :] = qkv_grad_ref[...].astype(jnp.bfloat16)
        packed_ref[3 * inner : 4 * inner, :] = out_grad_ref[...].astype(jnp.bfloat16)
        lines = []
        for head in range(head_count):
            total = fold_bias(near_ref[head])
            near = total[:, HALF : HALF + LANES]
            lane = lax.broadcasted_iota(jnp.int32, near.shape, 1)
            inside = jnp.where(lane < LANES - 1, near, 0.0)
            rest = (
                jnp.sum(total, axis=1, keepdims=True)
                - jnp.sum(inside, axis=1, keepdims=True)
                + jnp.sum(far_ref[head : head + 1], axis=1, keepdims=True)
            )
            lines.append(jnp.where(lane < LANES - 1, near, rest))
        lines.append(jnp.zeros((1, width - head_count * LANES), jnp.float32))
        bias_row = jnp.concatenate(lines, axis=1)
        gain_row = jnp.sum(gain_grad_ref[...], axis=0, keepdims=True)
        rows = lax.broadcasted_iota(jnp.int32, small_ref.shape, 0)
        gain_two_row = jnp.sum(gain_two_ref[...], axis=0, keepdims=True)
        small = jnp.where(rows == 0, gain_row, jnp.where(rows == 1, bias_row, small_ref[...]))
        small = jnp.where(rows == 2, gain_two_row, small)
        packed_ref[4 * inner :, :] = small.astype(jnp.bfloat16)


def whole(shape):
    return pl.BlockSpec(shape, lambda *steps: (0,) * len(shape))


def reversed_bits(value, count):
    result = value * 0
    for bit in range(count):
        result = result + ((value >> bit) & 1) * 2 ** (count - 1 - bit)
    return result


def bias_line(rel_bias):
    head_count, bucket_count = rel_bias.shape
    line = rel_bias - rel_bias[:, bucket_count - 1 :]
    line = jnp.concatenate(
        [
            jnp.zeros((head_count, HALF), jnp.float32),
            line,
            jnp.zeros((head_count, HALF - bucket_count), jnp.float32),
        ],
        axis=1,
    )
    return jnp.concatenate([line, jnp.zeros((8 - head_count, 2 * HALF), jnp.float32)], axis=0)


def attend(place, tokens, lengths, gain, qkv_flat, attn_out, rel_bias):
    rows, width = tokens.shape
    inner = attn_out.shape[0]
    head_count = rel_bias.shape[0]
    head_dim = inner // head_count
    block_count = rows // BLOCK
    bits = (block_count - 1).bit_length()

    def placed(block, at):
        return reversed_bits(block ^ at[0], bits)

    return pl.pallas_call(
        functools.partial(
            forward_kernel, head_count=head_count, head_dim=head_dim, slots=lengths.shape[1]
        ),
        grid_spec=pltpu.PrefetchScalarGridSpec(
            num_scalar_prefetch=1,
            grid=(block_count,),
            in_specs=[
                pl.BlockSpec(memory_space=pltpu.SMEM),
                pl.BlockSpec((BLOCK, width), lambda step, at: (step, 0)),
                whole((1, width)),
                whole(qkv_flat.shape),
                whole(attn_out.shape),
                whole((8, 2 * HALF)),
            ],
            out_specs=[
                pl.BlockSpec((BLOCK, width), lambda step, at: (placed(step, at), 0)),
                pl.BlockSpec((3 * inner, BLOCK), lambda step, at: (0, step)),
                pl.BlockSpec((inner, BLOCK), lambda step, at: (0, step)),
                pl.BlockSpec((8, BLOCK), lambda step, at: (0, step)),
            ],
            scratch_shapes=[
                pltpu.VMEM((head_count, 2 * BLOCK, head_dim), jnp.bfloat16),
                pltpu.VMEM((inner, 2 * BLOCK), jnp.bfloat16),
                pltpu.VMEM((head_count, 2 * HALF, HALF), jnp.float32),
            ],
        ),
        out_shape=[
            jax.ShapeDtypeStruct((rows, width), jnp.bfloat16),
            jax.ShapeDtypeStruct((3 * inner, rows), jnp.bfloat16),
            jax.ShapeDtypeStruct((inner, rows), jnp.bfloat16),
            jax.ShapeDtypeStruct((8, rows), jnp.float32),
        ],
        compiler_params=pltpu.CompilerParams(vmem_limit_bytes=VMEM_LIMIT),
        cost_estimate=pl.CostEstimate(
            flops=2 * rows * width * inner * 4 + 4 * rows * 768 * inner,
            bytes_accessed=10 * rows * width,
            transcendentals=rows * 768 * head_count,
        ),
        name="attend_forward",
    )(place, lengths, tokens, gain[None, :], qkv_flat, attn_out, bias_line(rel_bias))


def attend_back(
    place, tokens, lengths, gain, qkv_flat, attn_out, rel_bias, projected, mixed, log_total, near_grad,
    away_grad, small, gain_two,
):
    rows, width = tokens.shape
    inner = attn_out.shape[0]
    head_count, bucket_count = rel_bias.shape
    head_dim = inner // head_count
    block_count = rows // BLOCK
    last = block_count - 1
    bits = last.bit_length()

    def placed(block, at):
        return reversed_bits(block ^ at[0], bits)

    return pl.pallas_call(
        functools.partial(
            backward_kernel,
            head_count=head_count,
            head_dim=head_dim,
            slots=lengths.shape[1],
            block_count=block_count,
            placed=placed,
        ),
        grid_spec=pltpu.PrefetchScalarGridSpec(
            num_scalar_prefetch=1,
            grid=(block_count,),
            in_specs=[
                pl.BlockSpec(memory_space=pltpu.SMEM),
                pl.BlockSpec((BLOCK, width), lambda step, at: (last - step, 0)),
                whole((1, width)),
                whole(qkv_flat.shape),
                whole(attn_out.shape),
                whole((8, 2 * HALF)),
                pl.BlockSpec((3 * inner, BLOCK), lambda step, at: (0, last - step)),
                pl.BlockSpec(
                    (3 * inner, BLOCK), lambda step, at: (0, jnp.maximum(last - step - 1, 0))
                ),
                pl.BlockSpec((inner, BLOCK), lambda step, at: (0, last - step)),
                pl.BlockSpec((8, BLOCK), lambda step, at: (0, last - step)),
                pl.BlockSpec(
                    (1, BLOCK, width),
                    lambda step, at: (
                        jnp.minimum(placed(last - step, at), block_count // 2 - 1), 0, 0
                    ),
                ),
                pl.BlockSpec(
                    (1, BLOCK, width),
                    lambda step, at: (
                        jnp.maximum(placed(last - step, at) - block_count // 2, 0), 0, 0
                    ),
                ),
                whole(small.shape),
                whole(gain_two.shape),
            ],
            out_specs=[
                pl.BlockSpec((BLOCK, width), lambda step, at: (last - step, 0)),
                whole((4 * inner + small.shape[0], width)),
            ],
            scratch_shapes=[
                pltpu.VMEM((head_count, 2 * HALF, HALF), jnp.float32),
                pltpu.VMEM((head_count, 2 * HALF, HALF), jnp.float32),
                pltpu.VMEM((8, HALF), jnp.float32),
                pltpu.VMEM((2 * inner, 2 * BLOCK), jnp.float32),
                pltpu.VMEM((3 * inner, BLOCK), jnp.bfloat16),
                pltpu.VMEM((3 * inner, width), jnp.float32),
                pltpu.VMEM((inner, width), jnp.float32),
                pltpu.VMEM((8, width), jnp.float32),
            ],
        ),
        out_shape=[
            jax.ShapeDtypeStruct((rows, width), jnp.bfloat16),
            jax.ShapeDtypeStruct((4 * inner + small.shape[0], width), jnp.bfloat16),
        ],
        compiler_params=pltpu.CompilerParams(vmem_limit_bytes=VMEM_LIMIT),
        cost_estimate=pl.CostEstimate(
            flops=2 * rows * width * inner * 8 + 10 * rows * 768 * inner,
            bytes_accessed=14 * rows * width,
            transcendentals=rows * 768 * head_count,
        ),
        name="attend_backward",
    )(
        place, lengths, tokens, gain[None, :], qkv_flat, attn_out, bias_line(rel_bias),
        projected, projected, mixed, log_total, near_grad, away_grad,
        small, gain_two,
    )


GELU_ONE = 0.7978845608028654
GELU_TWO = 0.044715


def shard_at(place_ref, position, shards):
    offset = 0
    bits = (shards - 1).bit_length()
    for bit in range(bits):
        offset += ((position >> bit) & 1) * 2 ** (bits - 1 - bit)
    return place_ref[0] ^ offset


def expert_kernel(
    place_ref, rows_ref, grads_ref, gap_ref, weights_ref, router_ref, *rest, sub
):
    sent_ref, act_ref, pre_ref, logit_ref = rest[-4:]
    shards = weights_ref.shape[0]
    sources, slots, width = rows_ref.shape
    step = max(1, sub // slots)

    @pl.loop(0, sources // step)
    def _(index):
        part = pl.ds(index * step, step)
        rows = rows_ref[part].reshape(step * slots, width)
        gap = gap_ref[part, 0].reshape(step * slots, gap_ref.shape[3]).astype(jnp.float32)
        logits = mul(rows, router_ref[...], 1, 0)
        logit_gap = jnp.sum(gap * logits, axis=-1, keepdims=True)
        gate = 1.0 / (1.0 + jnp.exp(-logit_gap))
        other_gate = 1.0 / (1.0 + jnp.exp(logit_gap))
        sent = jnp.zeros((step * slots, width), jnp.float32)
        gate_grads = jnp.zeros((step * slots, 1), jnp.float32)
        for shard in range(shards):
            weights = weights_ref[shard_at(place_ref, shard, shards)]
            pre = mul(rows, weights, 1, 0)
            grads = grads_ref[shard, part, 0].reshape(step * slots, weights.shape[1])
            grads = grads.astype(jnp.float32)
            square = pre * pre
            bent = jnp.tanh(pre * (GELU_ONE + GELU_ONE * GELU_TWO * square))
            share = 0.5 + 0.5 * bent
            act = pre * share
            slope = share + act * (1.0 - share) * (
                2.0 * GELU_ONE + 6.0 * GELU_ONE * GELU_TWO * square
            )
            gate_grads += jnp.sum(act * grads, axis=-1, keepdims=True)
            act_ref[shard, part, 0] = (
                (gate * act).astype(jnp.bfloat16).reshape(step, slots, weights.shape[1])
            )
            grad_pre = (gate * grads * slope).astype(jnp.bfloat16)
            pre_ref[shard, part, 0] = grad_pre.reshape(step, slots, weights.shape[1])
            sent += mul(grad_pre, weights, 1, 1)
        logit_grads = (gate * other_gate * gate_grads * gap).astype(jnp.bfloat16)
        logit_ref[part, 0] = logit_grads.reshape(step, slots, gap.shape[1])
        sent += mul(logit_grads, router_ref[...], 1, 1)
        sent_ref[part] = sent.astype(jnp.bfloat16).reshape(step, slots, width)


def serve(place, rows, act_grads, hot_gap, weights_in, router_wide, which, before, sub=256, tile=512):
    sources, slots, width = rows.shape
    shards = weights_in.shape[0]
    hidden = weights_in.shape[2]
    group = min(sources, max(1, tile // slots))
    wide = pl.BlockSpec((shards, group, 1, slots, hidden), lambda step, at: (0, step, which, 0, 0))
    lanes = pl.BlockSpec((group, 1, slots, hot_gap.shape[3]), lambda step, at: (step, which, 0, 0))
    narrow = pl.BlockSpec((group, slots, width), lambda step, at: (step, 0, 0))
    kept = [] if before is None else list(before)
    return pl.pallas_call(
        functools.partial(expert_kernel, sub=sub),
        grid_spec=pltpu.PrefetchScalarGridSpec(
            num_scalar_prefetch=1,
            grid=(sources // group,),
            in_specs=[narrow, wide, lanes, whole(weights_in.shape), whole(router_wide.shape)]
            + [pl.BlockSpec(memory_space=pl.ANY)] * len(kept),
            out_specs=[narrow, wide, wide, lanes],
        ),
        out_shape=[
            jax.ShapeDtypeStruct(rows.shape, jnp.bfloat16),
            jax.ShapeDtypeStruct(act_grads.shape, jnp.bfloat16),
            jax.ShapeDtypeStruct(act_grads.shape, jnp.bfloat16),
            jax.ShapeDtypeStruct(hot_gap.shape, jnp.bfloat16),
        ],
        input_output_aliases={6 + index: 1 + index for index in range(len(kept))},
        compiler_params=pltpu.CompilerParams(vmem_limit_bytes=VMEM_LIMIT),
        cost_estimate=pl.CostEstimate(
            flops=4 * sources * slots * width * shards * hidden,
            bytes_accessed=6 * sources * slots * shards * hidden,
            transcendentals=sources * slots * shards * hidden,
        ),
        name="expert_middle",
    )(place, rows, act_grads, hot_gap, weights_in, router_wide, *kept)


def act_grads_kernel(place_ref, rows_ref, weights_ref, out_ref):
    shards = weights_ref.shape[0]
    rows = rows_ref[...].reshape(-1, rows_ref.shape[2])
    for shard in range(shards):
        out_ref[shard] = mul(rows, weights_ref[shard_at(place_ref, shard, shards)], 1, 1).astype(
            jnp.bfloat16
        )


def slot_group(sources, capacity):
    return min(sources, max(1, BLOCK // capacity))


def act_grads_of(place, landed, weights, capacity):
    sources, _, width = landed.shape
    shards, hidden, _ = weights.shape
    group = slot_group(sources, capacity)
    tile = group * capacity
    return pl.pallas_call(
        act_grads_kernel,
        grid_spec=pltpu.PrefetchScalarGridSpec(
            num_scalar_prefetch=1,
            grid=(sources // group,),
            in_specs=[
                pl.BlockSpec((group, capacity, width), lambda step, at: (step, 0, 0)),
                whole(weights.shape),
            ],
            out_specs=pl.BlockSpec((shards, tile, hidden), lambda step, at: (0, step, 0)),
        ),
        out_shape=jax.ShapeDtypeStruct((shards, sources * capacity, hidden), jnp.bfloat16),
        compiler_params=pltpu.CompilerParams(vmem_limit_bytes=VMEM_LIMIT),
        cost_estimate=pl.CostEstimate(
            flops=2 * sources * capacity * width * shards * hidden,
            bytes_accessed=2 * sources * capacity * shards * hidden,
            transcendentals=0,
        ),
        name="act_grads",
    )(place, landed, weights)


def result_kernel(place_ref, act_ref, weights_ref, out_ref):
    shards = weights_ref.shape[0]
    total = mul(act_ref[0], weights_ref[shard_at(place_ref, 0, shards)], 1, 0)
    for shard in range(1, shards):
        total += mul(act_ref[shard], weights_ref[shard_at(place_ref, shard, shards)], 1, 0)
    out_ref[...] = total.astype(jnp.bfloat16)


def result_of(place, act, weights):
    shards, rows, hidden = act.shape
    width = weights.shape[2]
    return pl.pallas_call(
        result_kernel,
        grid_spec=pltpu.PrefetchScalarGridSpec(
            num_scalar_prefetch=1,
            grid=(rows // BLOCK,),
            in_specs=[
                pl.BlockSpec((shards, BLOCK, hidden), lambda step, at: (0, step, 0)),
                whole(weights.shape),
            ],
            out_specs=pl.BlockSpec((BLOCK, width), lambda step, at: (step, 0)),
        ),
        out_shape=jax.ShapeDtypeStruct((rows, width), jnp.bfloat16),
        compiler_params=pltpu.CompilerParams(vmem_limit_bytes=VMEM_LIMIT),
        cost_estimate=pl.CostEstimate(flops=0, bytes_accessed=0, transcendentals=0),
        name="expert_result",
    )(place, act, weights)


def store_half(value, send_ref, keep_ref):
    half = pl.num_programs(0) // 2

    @pl.when(pl.program_id(0) < half)
    def _():
        send_ref[0] = value

    @pl.when(pl.program_id(0) >= half)
    def _():
        keep_ref[0] = value


def half_specs(shards, rows, columns):
    half = shards // 2
    shape = jax.ShapeDtypeStruct((half, rows, columns), jnp.bfloat16)
    specs = [
        pl.BlockSpec((1, rows, columns), lambda step: (jnp.minimum(step, half - 1), 0, 0)),
        pl.BlockSpec((1, rows, columns), lambda step: (jnp.maximum(step - half, 0), 0, 0)),
    ]
    return specs, [shape, shape]


def send_first(step, shards):
    return (step + shards // 2) % shards


def out_weights_kernel(act_ref, landed_ref, send_ref, keep_ref):
    capacity = act_ref.shape[1] // landed_ref.shape[0]
    rows = landed_ref[:, :capacity].reshape(act_ref.shape[1], landed_ref.shape[2])
    store_half(mul(act_ref[0], rows, 0, 0).astype(jnp.bfloat16), send_ref, keep_ref)


def out_weights_of(act, landed):
    shards, rows, hidden = act.shape
    width = landed.shape[2]
    specs, shapes = half_specs(shards, hidden, width)
    return pl.pallas_call(
        out_weights_kernel,
        grid=(shards,),
        in_specs=[
            pl.BlockSpec((1, rows, hidden), lambda step: (send_first(step, shards), 0, 0)),
            whole(landed.shape),
        ],
        out_specs=specs,
        out_shape=shapes,
        compiler_params=pltpu.CompilerParams(vmem_limit_bytes=VMEM_LIMIT),
        cost_estimate=pl.CostEstimate(flops=0, bytes_accessed=0, transcendentals=0),
        name="out_weights",
    )(act, landed)


def in_weights_kernel(
    first_ref, last_ref, grads_ref, logits_ref, send_ref, keep_ref, router_ref
):
    sources, slots, width = first_ref.shape
    first = first_ref[...].reshape(sources * slots, width)
    last = last_ref[...].reshape(sources * slots, width)
    hidden = grads_ref.shape[4]
    total = mul(first, grads_ref[0, :, 0].reshape(sources * slots, hidden), 0, 0) + mul(
        last, grads_ref[0, :, 1].reshape(sources * slots, hidden), 0, 0
    )
    store_half(total.astype(jnp.bfloat16), send_ref, keep_ref)

    @pl.when(pl.program_id(0) == 0)
    def _():
        lanes = logits_ref.shape[3]
        router_ref[...] = mul(
            first, logits_ref[:, 0].reshape(sources * slots, lanes), 0, 0
        ) + mul(last, logits_ref[:, 1].reshape(sources * slots, lanes), 0, 0)


def in_weights_of(first, last, grads, logit_grads):
    shards, sources, _, slots, hidden = grads.shape
    width = first.shape[2]
    lanes = logit_grads.shape[3]
    specs, shapes = half_specs(shards, width, hidden)
    return pl.pallas_call(
        in_weights_kernel,
        grid=(shards,),
        in_specs=[
            whole(first.shape),
            whole(last.shape),
            pl.BlockSpec(
                (1,) + grads.shape[1:], lambda step: (send_first(step, shards), 0, 0, 0, 0)
            ),
            whole(logit_grads.shape),
        ],
        out_specs=specs + [whole((width, lanes))],
        out_shape=shapes + [jax.ShapeDtypeStruct((width, lanes), jnp.float32)],
        compiler_params=pltpu.CompilerParams(vmem_limit_bytes=VMEM_LIMIT),
        cost_estimate=pl.CostEstimate(flops=0, bytes_accessed=0, transcendentals=0),
        name="in_weights",
    )(first, last, grads, logit_grads)


def place_kernel(routes_ref, grad_ref, slots_ref, index_ref, *, capacity, spare):
    expert = pl.program_id(0)
    experts = pl.num_programs(0)
    tokens = routes_ref.shape[1]
    lanes = lax.broadcasted_iota(jnp.int32, (LANES, tokens), 0)
    hot = [(routes_ref[choice : choice + 1, :] == lanes) for choice in range(2)]

    @pl.when(expert == 0)
    def _():
        counts = (hot[0] | hot[1]).astype(jnp.bfloat16)
        earlier = (
            lax.broadcasted_iota(jnp.int32, (tokens, tokens), 0)
            < lax.broadcasted_iota(jnp.int32, (tokens, tokens), 1)
        ).astype(jnp.bfloat16)
        before = mul(counts, earlier, 1, 0)
        for choice in range(2):
            rank = jnp.sum(jnp.where(hot[choice], before, 0.0), axis=0, keepdims=True)
            index_ref[choice : choice + 1, :] = (
                routes_ref[choice : choice + 1, :] * capacity + rank.astype(jnp.int32)
            )

    slot = lax.broadcasted_iota(jnp.int32, (capacity, tokens), 0) + expert * capacity
    named = [(index_ref[choice : choice + 1, :] == slot) for choice in range(2)]
    spread = (named[0] | named[1]).astype(jnp.bfloat16)
    slots_ref[0, :capacity] = mul(spread, grad_ref[...], 1, 0).astype(jnp.bfloat16)
    others = [
        jnp.broadcast_to(routes_ref[1 - choice : 2 - choice, :] + 1, (spare, tokens))
        .astype(jnp.float32)
        .astype(jnp.bfloat16)
        for choice in range(2)
    ]
    ids = mul(others[0], named[0].astype(jnp.bfloat16), 1, 1) + mul(
        others[1], named[1].astype(jnp.bfloat16), 1, 1
    )
    width = slots_ref.shape[2]
    padded = jnp.concatenate([ids, jnp.zeros((spare, width - capacity), jnp.float32)], axis=1)
    slots_ref[0, capacity:] = padded.astype(jnp.bfloat16)


def place_rows(routes, out_grad, experts, capacity):
    tokens, width = out_grad.shape
    return pl.pallas_call(
        functools.partial(place_kernel, capacity=capacity, spare=SPARE),
        grid=(experts,),
        in_specs=[whole((2, tokens)), whole((tokens, width))],
        out_specs=[
            pl.BlockSpec((1, capacity + SPARE, width), lambda step: (step, 0, 0)),
            whole((8, tokens)),
        ],
        out_shape=[
            jax.ShapeDtypeStruct((experts, capacity + SPARE, width), jnp.bfloat16),
            jax.ShapeDtypeStruct((8, tokens), jnp.int32),
        ],
        compiler_params=pltpu.CompilerParams(vmem_limit_bytes=VMEM_LIMIT),
        cost_estimate=pl.CostEstimate(
            flops=2 * experts * capacity * tokens * width,
            bytes_accessed=2 * experts * capacity * width,
            transcendentals=0,
        ),
        name="place_rows",
    )(routes.T, out_grad)


def combine_kernel(
    first_ref, first_rows_ref, last_ref, last_rows_ref, resid_ref, gain_ref, grad_ref,
    out_ref, sharp_ref, gain_grad_ref,
):
    grad_hidden = mul(first_ref[...], first_rows_ref[...], 1, 0) + mul(
        last_ref[...], last_rows_ref[...], 1, 0
    )
    resid = resid_ref[...]
    inverse = lax.rsqrt(jnp.mean(resid * resid, axis=-1, keepdims=True) + EPSILON)
    normed = resid * inverse

    @pl.when(pl.program_id(0) == 0)
    def _():
        gain_grad_ref[...] = jnp.zeros_like(gain_grad_ref)

    rows, width = resid.shape
    gain_grad_ref[...] += jnp.sum((grad_hidden * normed).reshape(rows // 8, 8, width), axis=0)
    gained = grad_hidden * gain_ref[...]
    total = grad_ref[...].astype(jnp.float32) + inverse * (
        gained - normed * jnp.mean(gained * normed, axis=-1, keepdims=True)
    )
    out_ref[...] = total
    sharp_ref[...] = total.astype(jnp.bfloat16)


def combine(first, first_rows, last, last_rows, resid, gain, out_grad):
    rows, width = resid.shape
    slots = first_rows.shape[0]
    tile = pl.BlockSpec((HALF, width), lambda step: (step, 0))
    named = pl.BlockSpec((HALF, slots), lambda step: (step, 0))
    total, sharp, gain_grad = pl.pallas_call(
        combine_kernel,
        grid=(rows // HALF,),
        in_specs=[
            named, whole((slots, width)), named, whole((slots, width)), tile, whole((1, width)), tile,
        ],
        out_specs=[tile, tile, whole((8, width))],
        out_shape=[
            jax.ShapeDtypeStruct((rows, width), jnp.float32),
            jax.ShapeDtypeStruct((rows, width), jnp.bfloat16),
            jax.ShapeDtypeStruct((8, width), jnp.float32),
        ],
        compiler_params=pltpu.CompilerParams(vmem_limit_bytes=VMEM_LIMIT),
        cost_estimate=pl.CostEstimate(
            flops=4 * rows * slots * width,
            bytes_accessed=4 * slots * width + 12 * rows * width,
            transcendentals=rows,
        ),
        name="combine",
    )(first, first_rows, last, last_rows, resid, gain[None, :], out_grad)
    return total, sharp, gain_grad


def rms_norm(values, gain):
    return values * lax.rsqrt(jnp.mean(values * values, axis=-1, keepdims=True) + EPSILON) * gain


def exchange(pieces):
    return lax.all_to_all(pieces, "expert", split_axis=0, concat_axis=0, tiled=True)


def halved(pieces, axis_name, bit):
    half = pieces.shape[0] // 2
    return pieces[:half], swap(pieces[half:].astype(jnp.bfloat16), axis_name, bit)


def joined(keep, got):
    return keep.astype(jnp.float32) + got.astype(jnp.float32)


def joined_low(keep, got):
    return joined(keep, got).astype(jnp.bfloat16)


def spread_sum(pieces, axis_name):
    for bit in range(bit_count(axis_name)):
        pieces = joined(*halved(pieces, axis_name, bit))
    return pieces[0]


def spread_rest(pieces, axis_name):
    for bit in range(1, bit_count(axis_name)):
        pieces = joined(*halved(pieces, axis_name, bit))
    return pieces[0]


def collect(piece, axis_name):
    pieces = piece[None]
    for bit in reversed(range(1, bit_count(axis_name))):
        pieces = jnp.concatenate([pieces, swap(pieces, axis_name, bit)], axis=0)
    return pieces


def swap(value, axis_name, bit):
    count = lax.axis_size(axis_name)
    return lax.ppermute(value, axis_name, [(i, i ^ (1 << bit)) for i in range(count)])


def own_bit(axis_name, bit):
    return (lax.axis_index(axis_name) >> bit) & 1


def bit_groups(axis_name):
    bits = list(range(bit_count(axis_name)))
    return [tuple(bits[:1])] + [tuple(bits[low : low + 2]) for low in range(1, len(bits), 2)]


def send_over(value, axis_name, group, offset):
    mask = sum(((offset >> place) & 1) << bit for place, bit in enumerate(group))
    count = lax.axis_size(axis_name)
    return lax.ppermute(value, axis_name, [(i, i ^ mask) for i in range(count)])


def group_sum(value, axis_name):
    for group in bit_groups(axis_name):
        parts = [send_over(value, axis_name, group, m) for m in range(1, 2 ** len(group))]
        value = sum(parts, value)
    return value


def scatter_sum(pieces, axis_name, order):
    bits = list(range(bit_count(axis_name)))[::-1]
    total = pieces.reshape((2,) * len(bits) + pieces.shape[1:])
    for group in order:
        parts = []
        for offset in range(2 ** len(group)):
            part, left = total, list(bits)
            for place, bit in enumerate(group):
                dim = left.index(bit)
                left.remove(bit)
                index = own_bit(axis_name, bit) ^ ((offset >> place) & 1)
                part = lax.dynamic_index_in_dim(part, index, dim, keepdims=False)
            if offset:
                part = send_over(part.astype(jnp.bfloat16), axis_name, group, offset)
            parts.append(part.astype(jnp.float32))
        total = sum(parts[1:], parts[0])
        bits = left
    return total


def gather(value, axis_name, order, done=()):
    bits = list(done)
    for group in order:
        value = value.reshape((2,) * len(bits) + value.shape[value.ndim - 2 :])
        size = 2 ** len(group)
        parts = [value] + [send_over(value, axis_name, group, m) for m in range(1, size)]
        for place, bit in enumerate(group):
            flip = own_bit(axis_name, bit) == 1
            parts = [jnp.where(flip, parts[m ^ (1 << place)], parts[m]) for m in range(size)]
        stacked = jnp.stack(parts).reshape((2,) * len(group) + value.shape)
        now = sorted(group, reverse=True) + bits
        bits = sorted(now, reverse=True)
        order_of = [now.index(bit) for bit in bits]
        value = stacked.transpose(order_of + list(range(len(bits), stacked.ndim)))
    return value


def bit_count(axis_name):
    return (lax.axis_size(axis_name) - 1).bit_length()


def scatter_rows(rows, axis_name):
    groups = bit_groups(axis_name)
    parts = lax.axis_size(axis_name)
    middle = rows.shape[0] // EXTRA // 2 * EXTRA
    orders = [groups[turn:] + groups[:turn] for turn in (0, 1)]
    owned = [
        scatter_sum(half.reshape((parts, -1) + rows.shape[1:]), axis_name, order).astype(
            jnp.bfloat16
        )
        for half, order in zip((rows[:middle], rows[middle:]), orders)
    ]
    return owned, orders


def gather_rows(begun, orders, axis_name):
    halves = []
    for part, order in zip(begun, orders):
        done = sorted(order[-1], reverse=True)
        halves.append(gather(part, axis_name, order[::-1][1:], done))
    return jnp.concatenate([half.reshape(-1, half.shape[-1]) for half in halves], axis=0)


def local(
    tokens,
    lengths,
    routes,
    norm1_gain,
    attn_qkv,
    attn_out,
    rel_bias,
    norm2_gain,
    router,
    expert_in,
    expert_out,
    out_grad,
):
    n_tensor = lax.axis_size("tensor")
    tensor_index = lax.axis_index("tensor")
    width = tokens.shape[1]
    own_rows = routes.shape[0]
    inner = attn_out.shape[0]
    head_count, bucket_count = rel_bias.shape
    expert_count = router.shape[1]
    capacity = max(2, 4 * own_rows // expert_count)

    expert_index = lax.axis_index("expert")
    grad_slots, slot_index = place_rows(routes, out_grad, expert_count, capacity)
    slot_index = slot_index[:2].T
    half_slots = capacity // 2

    def named(slot_ids):
        match = slot_index[:, :, None] == slot_ids[None, None, :]
        return (match[:, 0] | match[:, 1]).astype(jnp.bfloat16)

    slot_ids = jnp.arange(expert_count * capacity, dtype=jnp.int32)
    split_ids = slot_ids.reshape(expert_count, 2, half_slots)
    landed = exchange(grad_slots)
    tokens, _ = lax.optimization_barrier((tokens, grad_slots))
    place = tensor_index.astype(jnp.int32)[None]
    halves = [named(split_ids[:, which].reshape(-1)) for which in range(2)]
    dispatch = named(slot_ids)

    qkv_flat = attn_qkv.transpose(1, 2, 0).reshape(3 * inner, width)
    branch, projected, mixed, log_total = attend(
        place, tokens, lengths, norm1_gain, qkv_flat, attn_out, rel_bias
    )
    branch = spread_sum(branch.reshape(n_tensor, own_rows, width), "tensor")
    own_tokens = lax.dynamic_slice_in_dim(tokens, tensor_index * own_rows, own_rows, 0)
    resid = own_tokens.astype(jnp.float32) + branch
    hidden_two = rms_norm(resid, norm2_gain).astype(jnp.bfloat16)
    outgoing = [mul(half, hidden_two, 0, 0).astype(jnp.bfloat16) for half in halves]
    outgoing, landed, expert_in = lax.optimization_barrier((outgoing, landed, expert_in))
    outgoing = [rows.reshape(expert_count, half_slots, width) for rows in outgoing]
    first_rows = exchange(outgoing[0])
    other_here = landed[:, capacity, :capacity].reshape(-1).astype(jnp.int32)
    weights_out = lax.all_gather(expert_out[0], "tensor")
    weights_in = lax.all_gather(expert_in[0], "tensor")
    act_grads = act_grads_of(place, landed, weights_out, capacity)
    shards, _, hidden = act_grads.shape
    act_grads = act_grads.reshape(shards, expert_count, 2, half_slots, hidden)
    lanes = jnp.arange(LANES, dtype=jnp.int32)
    hot_gap = (
        (lanes == expert_index).astype(jnp.int32)[None, :]
        - (other_here[:, None] == lanes[None, :] + 1).astype(jnp.int32)
    ).astype(jnp.bfloat16)
    hot_gap = hot_gap.reshape(expert_count, 2, half_slots, LANES)
    router_wide = jnp.pad(router, ((0, 0), (0, LANES - expert_count)))
    first_rows, act_grads, hot_gap, weights_in, last, dispatch, halves = lax.optimization_barrier(
        (first_rows, act_grads, hot_gap, weights_in, outgoing[1], dispatch, halves)
    )
    last_rows = exchange(last)
    sent_one, *kept = serve(place, first_rows, act_grads, hot_gap, weights_in, router_wide, 0, None)
    grad_sent_one = exchange(sent_one)
    sent_two, act, grad_pre, logit_grads = serve(
        place, last_rows, act_grads, hot_gap, weights_in, router_wide, 1, kept
    )
    act = act.reshape(shards, -1, hidden)
    out_send, out_keep = out_weights_of(act, landed)
    sent_two, out_send, out_keep, grad_pre = lax.optimization_barrier(
        (sent_two, out_send, out_keep, grad_pre)
    )
    grad_sent_two = exchange(sent_two)
    out_half = joined_low(out_keep, swap(out_send, "tensor", 0))
    out_half, grad_pre = lax.optimization_barrier((out_half, grad_pre))
    for bit in range(1, bit_count("tensor") - 1):
        out_half = joined_low(*halved(out_half, "tensor", bit))
    out_half, out_got = halved(out_half, "tensor", bit_count("tensor") - 1)
    in_send, in_keep, router_part = in_weights_of(first_rows, last_rows, grad_pre, logit_grads)
    router_part = router_part[:, :expert_count]
    count = 2 + expert_count
    extra = -(-(count + 1) // EXTRA) * EXTRA - count - 1
    blank = jnp.zeros((1, width), jnp.float32)
    small = jnp.concatenate(
        [blank, blank, blank, router_part.T, jnp.zeros((extra, width), jnp.float32)], axis=0
    )
    act, in_send, in_keep, small = lax.optimization_barrier((act, in_send, in_keep, small))
    in_got = swap(in_send, "tensor", 0)
    result = result_of(place, act, weights_out)
    grad_sent_one, grad_sent_two, result, out_half, out_got = lax.optimization_barrier(
        (grad_sent_one, grad_sent_two, result, out_half, out_got)
    )
    grad_resid, grad_sharp, gain_two_part = combine(
        halves[0],
        grad_sent_one.reshape(-1, width),
        halves[1],
        grad_sent_two.reshape(-1, width),
        resid,
        norm2_gain,
        out_grad,
    )
    came_back = exchange(result.reshape(expert_count, capacity, width)).reshape(-1, width)
    tensor_bits = bit_count("tensor")
    grad_w_in = joined_low(in_keep, in_got)
    for bit in range(1, tensor_bits - 1):
        grad_w_in = joined_low(*halved(grad_w_in, "tensor", bit))
    near_grad = collect(grad_sharp, "tensor")
    near_grad, grad_w_in = lax.optimization_barrier((near_grad, grad_w_in))
    away_grad = swap(near_grad, "tensor", 0)
    grad_w_in, grad_w_in_got = halved(grad_w_in, "tensor", tensor_bits - 1)

    tokens_part, weights_part = attend_back(
        place, tokens, lengths, norm1_gain, qkv_flat, attn_out, rel_bias,
        projected, mixed, log_total, near_grad, away_grad, small, gain_two_part,
    )
    tokens_part, weights_part, came_back, grad_w_in_got = lax.optimization_barrier(
        (tokens_part, weights_part, came_back, grad_w_in_got)
    )
    tokens_shared = lax.psum_scatter(tokens_part, "tensor", scatter_dimension=0, tiled=True)
    owned, orders = scatter_rows(weights_part, "expert")
    owned = lax.optimization_barrier(owned)
    begun = [gather(own, "expert", order[::-1][:1]) for own, order in zip(owned, orders)]
    begun, came_back, grad_w_in, tokens_shared, out_half = lax.optimization_barrier(
        (begun, came_back, grad_w_in, tokens_shared, out_half)
    )
    grad_w_out = joined(out_half, out_got)
    weights_total = gather_rows(begun, orders, "expert").astype(jnp.float32)
    output = resid + jnp.dot(dispatch, came_back, preferred_element_type=jnp.float32)
    grad_tokens = grad_resid + tokens_shared.astype(jnp.float32)
    grad_w_in = joined(grad_w_in, grad_w_in_got)
    low = 4 * inner
    bias_total = weights_total[low + 1, : rel_bias.size].reshape(rel_bias.shape)
    small = weights_total[low : low + count + 1]
    small = group_sum(jnp.concatenate([small[:1], small[2:]], axis=0), "tensor")
    columns = lax.dynamic_slice_in_dim(
        small, tensor_index * (width // n_tensor), width // n_tensor, 1
    )
    return (
        output,
        grad_tokens,
        columns[0],
        weights_total[: 3 * inner].reshape(3, inner, width).transpose(2, 0, 1),
        weights_total[3 * inner : 4 * inner],
        bias_total,
        columns[1],
        columns[2:].T,
        grad_w_in,
        grad_w_out,
    )


def solution(mesh):
    return jax.shard_map(
        local,
        mesh=mesh,
        in_specs=(
            P("expert", None),
            P("expert", None),
            P(("expert", "tensor"), None),
            P(),
            P(None, None, "tensor"),
            P("tensor", None),
            P("tensor", None),
            P(),
            P(),
            P("expert", None, "tensor"),
            P("expert", "tensor", None),
            P(("expert", "tensor"), None),
        ),
        out_specs=(
            P(("expert", "tensor"), None),
            P(("expert", "tensor"), None),
            P("tensor"),
            P(None, None, "tensor"),
            P("tensor", None),
            P("tensor", None),
            P("tensor"),
            P("tensor", None),
            P("expert", None, "tensor"),
            P("expert", "tensor", None),
        ),
        check_vma=False,
    )
```

```python
import functools

import jax
import jax.numpy as jnp
from jax import lax
from jax.experimental import pallas as pl
from jax.experimental.pallas import tpu as pltpu
from jax.sharding import PartitionSpec as P

BLOCK = 512
HALF = 256
EPSILON = 1e-06
BLOCKED = -1e30
VMEM_LIMIT = 48 * 2**20
LANES = 128
SPARE = 16
EXTRA = 64


def mul(left, right, left_dim, right_dim):
    return lax.dot_general(
        left,
        right,
        (((left_dim,), (right_dim,)), ((), ())),
        preferred_element_type=jnp.float32,
    )


def spread_bias(bias_ref, spread_ref, head_count):
    for head in range(head_count):
        line = jnp.broadcast_to(bias_ref[head : head + 1, :], (2 * HALF, 2 * HALF))
        rolled = pltpu.roll(line, 0, 1, stride=1, stride_axis=0)
        spread_ref[head] = rolled[:, :HALF]


def fold_bias(total):
    line = jnp.concatenate([total, jnp.zeros_like(total)], axis=1)
    rows = lax.broadcasted_iota(jnp.int32, line.shape, 0)
    step = 1
    while step < 2 * HALF:
        line = jnp.where((rows & step) != 0, pltpu.roll(line, 2 * HALF - step, 1), line)
        step *= 2
    return jnp.sum(line, axis=0, keepdims=True)


def window_masks(lengths_ref, block_index, half, slots):
    query_pos = (
        lax.broadcasted_iota(jnp.int32, (1, HALF), 1) + block_index * BLOCK + half * HALF
    )
    start = jnp.zeros_like(query_pos)
    end = jnp.int32(0)
    for slot in range(slots):
        end = end + lengths_ref[0, slot]
        start = jnp.where(query_pos >= end, end, start)
    first_key = (block_index - 1) * BLOCK + half * HALF
    far_pos = lax.broadcasted_iota(jnp.int32, (HALF, 1), 0) + first_key
    near_pos = lax.broadcasted_iota(jnp.int32, (2 * HALF, 1), 0) + first_key + HALF
    return far_pos >= start, (near_pos >= start) & (near_pos <= query_pos)


def forward_kernel(
    place_ref, lengths_ref, tokens_ref, gain_ref, qkv_ref, out_ref, bias_ref,
    branch_ref, proj_ref, mixed_ref, log_ref,
    keys_ref, values_ref, spread_ref,
    *, head_count, head_dim, slots,
):
    block_index = pl.program_id(0)
    inner = head_count * head_dim

    @pl.when(block_index == 0)
    def _():
        keys_ref[:, :BLOCK] = jnp.zeros_like(keys_ref[:, :BLOCK])
        values_ref[:, :BLOCK] = jnp.zeros_like(values_ref[:, :BLOCK])
        spread_bias(bias_ref, spread_ref, head_count)

    @pl.when(block_index > 0)
    def _():
        keys_ref[:, :BLOCK] = keys_ref[:, BLOCK:]
        values_ref[:, :BLOCK] = values_ref[:, BLOCK:]

    widened = tokens_ref[...].astype(jnp.float32)
    inverse = lax.rsqrt(jnp.mean(widened * widened, axis=-1, keepdims=True) + EPSILON)
    hidden = (widened * inverse * gain_ref[...]).astype(jnp.bfloat16)
    projected = mul(qkv_ref[...], hidden, 1, 1)
    proj_ref[...] = projected.astype(jnp.bfloat16)
    for head in range(head_count):
        low = inner + head * head_dim
        keys_ref[head, BLOCK:, :] = projected[low : low + head_dim].T.astype(jnp.bfloat16)
    values_ref[:, BLOCK:] = proj_ref[2 * inner :, :]
    scale = head_dim**-0.5
    for half in range(BLOCK // HALF):
        far_mask, near_mask = window_masks(lengths_ref, block_index, half, slots)
        cols = slice(half * HALF, (half + 1) * HALF)
        window = slice(half * HALF, (half + 3) * HALF)
        for head in range(head_count):
            rows = slice(head * head_dim, (head + 1) * head_dim)
            query = proj_ref[rows, cols] * jnp.bfloat16(scale)
            scores = mul(keys_ref[head, window, :], query, 1, 0)
            far = jnp.where(far_mask, scores[:HALF], BLOCKED)
            near = jnp.where(near_mask, scores[HALF:] + spread_ref[head], BLOCKED)
            peak = jnp.maximum(
                jnp.max(far, axis=0, keepdims=True), jnp.max(near, axis=0, keepdims=True)
            )
            far = jnp.exp(far - peak)
            near = jnp.exp(near - peak)
            total = jnp.sum(far, axis=0, keepdims=True) + jnp.sum(near, axis=0, keepdims=True)
            share = 1.0 / total
            weights = jnp.concatenate(
                [(far * share).astype(jnp.bfloat16), (near * share).astype(jnp.bfloat16)], axis=0
            )
            mixed_ref[rows, cols] = mul(values_ref[rows, window], weights, 1, 0).astype(
                jnp.bfloat16
            )
            log_ref[head : head + 1, cols] = peak + jnp.log(total)
    branch_ref[...] = mul(mixed_ref[...], out_ref[...], 0, 0).astype(jnp.bfloat16)


def backward_kernel(
    place_ref, lengths_ref, tokens_ref, gain_ref, qkv_ref, out_ref, bias_ref,
    proj_ref, before_ref, mixed_ref, log_ref, near_grad_ref, away_grad_ref,
    small_ref, gain_two_ref, part_ref, packed_ref,
    spread_ref, near_ref, far_ref, carry_ref, pieces_ref, qkv_grad_ref, out_grad_ref, gain_grad_ref,
    *, head_count, head_dim, slots, block_count, placed,
):
    step = pl.program_id(0)
    block_index = block_count - 1 - step
    inner = head_count * head_dim

    @pl.when(step == 0)
    def _():
        spread_bias(bias_ref, spread_ref, head_count)
        near_ref[...] = jnp.zeros_like(near_ref)
        far_ref[...] = jnp.zeros_like(far_ref)
        carry_ref[...] = jnp.zeros_like(carry_ref)
        qkv_grad_ref[...] = jnp.zeros_like(qkv_grad_ref)
        out_grad_ref[...] = jnp.zeros_like(out_grad_ref)
        gain_grad_ref[...] = jnp.zeros_like(gain_grad_ref)

    @pl.when(step > 0)
    def _():
        carry_ref[:, BLOCK:] = carry_ref[:, :BLOCK]
        carry_ref[:, :BLOCK] = jnp.zeros_like(carry_ref[:, :BLOCK])

    close = placed(block_index, place_ref) < block_count // 2
    grad_branch = jnp.where(close, near_grad_ref[0], away_grad_ref[0])
    out_grad_ref[...] += mul(mixed_ref[...], grad_branch, 1, 0)
    grad_mixed = mul(out_ref[...], grad_branch, 1, 1).astype(jnp.bfloat16)
    scale = head_dim**-0.5
    for head in range(head_count):
        rows = slice(head * head_dim, (head + 1) * head_dim)
        key_rows = slice(inner + head * head_dim, inner + (head + 1) * head_dim)
        value_rows = slice(2 * inner + head * head_dim, 2 * inner + (head + 1) * head_dim)
        keys_flat = jnp.concatenate([before_ref[key_rows, :], proj_ref[key_rows, :]], axis=1)
        values_flat = jnp.concatenate([before_ref[value_rows, :], proj_ref[value_rows, :]], axis=1)
        keys = keys_flat.astype(jnp.float32).T.astype(jnp.bfloat16)
        values = values_flat.astype(jnp.float32).T.astype(jnp.bfloat16)
        for half in range(BLOCK // HALF):
            far_mask, near_mask = window_masks(lengths_ref, block_index, half, slots)
            cols = slice(half * HALF, (half + 1) * HALF)
            window = slice(half * HALF, (half + 3) * HALF)
            query = proj_ref[rows, cols] * jnp.bfloat16(scale)
            scores = mul(keys[window], query, 1, 0)
            log_total = log_ref[head : head + 1, cols]
            far = jnp.where(far_mask, jnp.exp(scores[:HALF] - log_total), 0.0)
            near = jnp.where(
                near_mask, jnp.exp(scores[HALF:] + spread_ref[head] - log_total), 0.0
            )
            probs = jnp.concatenate([far, near], axis=0)
            grad_out = grad_mixed[rows, cols]
            grad_probs = mul(values[window], grad_out, 1, 0)
            row_inner = jnp.sum(probs * grad_probs, axis=0, keepdims=True)
            grad_scores = (probs * (grad_probs - row_inner)).astype(jnp.bfloat16)
            rounded = grad_scores.astype(jnp.float32)
            near_ref[head] += rounded[HALF:]
            far_ref[head : head + 1] += jnp.sum(rounded[:HALF], axis=0, keepdims=True)
            pieces_ref[rows, cols] = (
                mul(keys_flat[:, window], grad_scores, 1, 0) * scale
            ).astype(jnp.bfloat16)
            carry_ref[rows, window] += mul(query, grad_scores, 1, 1)
            carry_ref[key_rows, window] += mul(grad_out, probs.astype(jnp.bfloat16), 1, 1)
    pieces_ref[inner:, :] = carry_ref[:, BLOCK:].astype(jnp.bfloat16)
    widened = tokens_ref[...].astype(jnp.float32)
    inverse = lax.rsqrt(jnp.mean(widened * widened, axis=-1, keepdims=True) + EPSILON)
    normed = widened * inverse
    hidden = (normed * gain_ref[...]).astype(jnp.bfloat16)
    pieces = pieces_ref[...]
    qkv_grad_ref[...] += mul(pieces, hidden, 1, 0)
    grad_hidden = mul(pieces, qkv_ref[...], 0, 0)
    gain_grad_ref[...] += jnp.sum(
        (grad_hidden * normed).reshape(BLOCK // 8, 8, normed.shape[1]), axis=0
    )
    gained = grad_hidden * gain_ref[...]
    part_ref[...] = (
        inverse * (gained - normed * jnp.mean(gained * normed, axis=-1, keepdims=True))
    ).astype(jnp.bfloat16)

    @pl.when(step == block_count - 1)
    def _():
        width = gain_grad_ref.shape[1]
        packed_ref[: 3 * inner, :] = qkv_grad_ref[...].astype(jnp.bfloat16)
        packed_ref[3 * inner : 4 * inner, :] = out_grad_ref[...].astype(jnp.bfloat16)
        lines = []
        for head in range(head_count):
            total = fold_bias(near_ref[head])
            near = total[:, HALF : HALF + LANES]
            lane = lax.broadcasted_iota(jnp.int32, near.shape, 1)
            inside = jnp.where(lane < LANES - 1, near, 0.0)
            rest = (
                jnp.sum(total, axis=1, keepdims=True)
                - jnp.sum(inside, axis=1, keepdims=True)
                + jnp.sum(far_ref[head : head + 1], axis=1, keepdims=True)
            )
            lines.append(jnp.where(lane < LANES - 1, near, rest))
        lines.append(jnp.zeros((1, width - head_count * LANES), jnp.float32))
        bias_row = jnp.concatenate(lines, axis=1)
        gain_row = jnp.sum(gain_grad_ref[...], axis=0, keepdims=True)
        rows = lax.broadcasted_iota(jnp.int32, small_ref.shape, 0)
        gain_two_row = jnp.sum(gain_two_ref[...], axis=0, keepdims=True)
        small = jnp.where(rows == 0, gain_row, jnp.where(rows == 1, bias_row, small_ref[...]))
        small = jnp.where(rows == 2, gain_two_row, small)
        packed_ref[4 * inner :, :] = small.astype(jnp.bfloat16)


def whole(shape):
    return pl.BlockSpec(shape, lambda *steps: (0,) * len(shape))


def reversed_bits(value, count):
    result = value * 0
    for bit in range(count):
        result = result + ((value >> bit) & 1) * 2 ** (count - 1 - bit)
    return result


def bias_line(rel_bias):
    head_count, bucket_count = rel_bias.shape
    line = rel_bias - rel_bias[:, bucket_count - 1 :]
    line = jnp.concatenate(
        [
            jnp.zeros((head_count, HALF), jnp.float32),
            line,
            jnp.zeros((head_count, HALF - bucket_count), jnp.float32),
        ],
        axis=1,
    )
    return jnp.concatenate([line, jnp.zeros((8 - head_count, 2 * HALF), jnp.float32)], axis=0)


def attend(place, tokens, lengths, gain, qkv_flat, attn_out, rel_bias):
    rows, width = tokens.shape
    inner = attn_out.shape[0]
    head_count = rel_bias.shape[0]
    head_dim = inner // head_count
    block_count = rows // BLOCK
    bits = (block_count - 1).bit_length()

    def placed(block, at):
        return reversed_bits(block ^ at[0], bits)

    return pl.pallas_call(
        functools.partial(
            forward_kernel, head_count=head_count, head_dim=head_dim, slots=lengths.shape[1]
        ),
        grid_spec=pltpu.PrefetchScalarGridSpec(
            num_scalar_prefetch=1,
            grid=(block_count,),
            in_specs=[
                pl.BlockSpec(memory_space=pltpu.SMEM),
                pl.BlockSpec((BLOCK, width), lambda step, at: (step, 0)),
                whole((1, width)),
                whole(qkv_flat.shape),
                whole(attn_out.shape),
                whole((8, 2 * HALF)),
            ],
            out_specs=[
                pl.BlockSpec((BLOCK, width), lambda step, at: (placed(step, at), 0)),
                pl.BlockSpec((3 * inner, BLOCK), lambda step, at: (0, step)),
                pl.BlockSpec((inner, BLOCK), lambda step, at: (0, step)),
                pl.BlockSpec((8, BLOCK), lambda step, at: (0, step)),
            ],
            scratch_shapes=[
                pltpu.VMEM((head_count, 2 * BLOCK, head_dim), jnp.bfloat16),
                pltpu.VMEM((inner, 2 * BLOCK), jnp.bfloat16),
                pltpu.VMEM((head_count, 2 * HALF, HALF), jnp.float32),
            ],
        ),
        out_shape=[
            jax.ShapeDtypeStruct((rows, width), jnp.bfloat16),
            jax.ShapeDtypeStruct((3 * inner, rows), jnp.bfloat16),
            jax.ShapeDtypeStruct((inner, rows), jnp.bfloat16),
            jax.ShapeDtypeStruct((8, rows), jnp.float32),
        ],
        compiler_params=pltpu.CompilerParams(vmem_limit_bytes=VMEM_LIMIT),
        cost_estimate=pl.CostEstimate(
            flops=2 * rows * width * inner * 4 + 4 * rows * 768 * inner,
            bytes_accessed=10 * rows * width,
            transcendentals=rows * 768 * head_count,
        ),
        name="attend_forward",
    )(place, lengths, tokens, gain[None, :], qkv_flat, attn_out, bias_line(rel_bias))


def attend_back(
    place, tokens, lengths, gain, qkv_flat, attn_out, rel_bias, projected, mixed, log_total, near_grad,
    away_grad, small, gain_two,
):
    rows, width = tokens.shape
    inner = attn_out.shape[0]
    head_count, bucket_count = rel_bias.shape
    head_dim = inner // head_count
    block_count = rows // BLOCK
    last = block_count - 1
    bits = last.bit_length()

    def placed(block, at):
        return reversed_bits(block ^ at[0], bits)

    return pl.pallas_call(
        functools.partial(
            backward_kernel,
            head_count=head_count,
            head_dim=head_dim,
            slots=lengths.shape[1],
            block_count=block_count,
            placed=placed,
        ),
        grid_spec=pltpu.PrefetchScalarGridSpec(
            num_scalar_prefetch=1,
            grid=(block_count,),
            in_specs=[
                pl.BlockSpec(memory_space=pltpu.SMEM),
                pl.BlockSpec((BLOCK, width), lambda step, at: (last - step, 0)),
                whole((1, width)),
                whole(qkv_flat.shape),
                whole(attn_out.shape),
                whole((8, 2 * HALF)),
                pl.BlockSpec((3 * inner, BLOCK), lambda step, at: (0, last - step)),
                pl.BlockSpec(
                    (3 * inner, BLOCK), lambda step, at: (0, jnp.maximum(last - step - 1, 0))
                ),
                pl.BlockSpec((inner, BLOCK), lambda step, at: (0, last - step)),
                pl.BlockSpec((8, BLOCK), lambda step, at: (0, last - step)),
                pl.BlockSpec(
                    (1, BLOCK, width),
                    lambda step, at: (
                        jnp.minimum(placed(last - step, at), block_count // 2 - 1), 0, 0
                    ),
                ),
                pl.BlockSpec(
                    (1, BLOCK, width),
                    lambda step, at: (
                        jnp.maximum(placed(last - step, at) - block_count // 2, 0), 0, 0
                    ),
                ),
                whole(small.shape),
                whole(gain_two.shape),
            ],
            out_specs=[
                pl.BlockSpec((BLOCK, width), lambda step, at: (last - step, 0)),
                whole((4 * inner + small.shape[0], width)),
            ],
            scratch_shapes=[
                pltpu.VMEM((head_count, 2 * HALF, HALF), jnp.float32),
                pltpu.VMEM((head_count, 2 * HALF, HALF), jnp.float32),
                pltpu.VMEM((8, HALF), jnp.float32),
                pltpu.VMEM((2 * inner, 2 * BLOCK), jnp.float32),
                pltpu.VMEM((3 * inner, BLOCK), jnp.bfloat16),
                pltpu.VMEM((3 * inner, width), jnp.float32),
                pltpu.VMEM((inner, width), jnp.float32),
                pltpu.VMEM((8, width), jnp.float32),
            ],
        ),
        out_shape=[
            jax.ShapeDtypeStruct((rows, width), jnp.bfloat16),
            jax.ShapeDtypeStruct((4 * inner + small.shape[0], width), jnp.bfloat16),
        ],
        compiler_params=pltpu.CompilerParams(vmem_limit_bytes=VMEM_LIMIT),
        cost_estimate=pl.CostEstimate(
            flops=2 * rows * width * inner * 8 + 10 * rows * 768 * inner,
            bytes_accessed=14 * rows * width,
            transcendentals=rows * 768 * head_count,
        ),
        name="attend_backward",
    )(
        place, lengths, tokens, gain[None, :], qkv_flat, attn_out, bias_line(rel_bias),
        projected, projected, mixed, log_total, near_grad, away_grad,
        small, gain_two,
    )


GELU_ONE = 0.7978845608028654
GELU_TWO = 0.044715


def shard_at(place_ref, position, shards):
    offset = 0
    bits = (shards - 1).bit_length()
    for bit in range(bits):
        offset += ((position >> bit) & 1) * 2 ** (bits - 1 - bit)
    return place_ref[0] ^ offset


def expert_kernel(
    place_ref, rows_ref, grads_ref, gap_ref, weights_ref, router_ref, *rest, sub
):
    sent_ref, act_ref, pre_ref, logit_ref = rest[-4:]
    shards = weights_ref.shape[0]
    sources, slots, width = rows_ref.shape
    step = max(1, sub // slots)

    @pl.loop(0, sources // step)
    def _(index):
        part = pl.ds(index * step, step)
        rows = rows_ref[part].reshape(step * slots, width)
        gap = gap_ref[part, 0].reshape(step * slots, gap_ref.shape[3]).astype(jnp.float32)
        logits = mul(rows, router_ref[...], 1, 0)
        logit_gap = jnp.sum(gap * logits, axis=-1, keepdims=True)
        gate = 1.0 / (1.0 + jnp.exp(-logit_gap))
        other_gate = 1.0 / (1.0 + jnp.exp(logit_gap))
        sent = jnp.zeros((step * slots, width), jnp.float32)
        gate_grads = jnp.zeros((step * slots, 1), jnp.float32)
        for shard in range(shards):
            weights = weights_ref[shard_at(place_ref, shard, shards)]
            pre = mul(rows, weights, 1, 0)
            grads = grads_ref[shard, part, 0].reshape(step * slots, weights.shape[1])
            grads = grads.astype(jnp.float32)
            square = pre * pre
            bent = jnp.tanh(pre * (GELU_ONE + GELU_ONE * GELU_TWO * square))
            share = 0.5 + 0.5 * bent
            act = pre * share
            slope = share + act * (1.0 - share) * (
                2.0 * GELU_ONE + 6.0 * GELU_ONE * GELU_TWO * square
            )
            gate_grads += jnp.sum(act * grads, axis=-1, keepdims=True)
            act_ref[shard, part, 0] = (
                (gate * act).astype(jnp.bfloat16).reshape(step, slots, weights.shape[1])
            )
            grad_pre = (gate * grads * slope).astype(jnp.bfloat16)
            pre_ref[shard, part, 0] = grad_pre.reshape(step, slots, weights.shape[1])
            sent += mul(grad_pre, weights, 1, 1)
        logit_grads = (gate * other_gate * gate_grads * gap).astype(jnp.bfloat16)
        logit_ref[part, 0] = logit_grads.reshape(step, slots, gap.shape[1])
        sent += mul(logit_grads, router_ref[...], 1, 1)
        sent_ref[part] = sent.astype(jnp.bfloat16).reshape(step, slots, width)


def serve(place, rows, act_grads, hot_gap, weights_in, router_wide, which, before, sub=256, tile=512):
    sources, slots, width = rows.shape
    shards = weights_in.shape[0]
    hidden = weights_in.shape[2]
    group = min(sources, max(1, tile // slots))
    wide = pl.BlockSpec((shards, group, 1, slots, hidden), lambda step, at: (0, step, which, 0, 0))
    lanes = pl.BlockSpec((group, 1, slots, hot_gap.shape[3]), lambda step, at: (step, which, 0, 0))
    narrow = pl.BlockSpec((group, slots, width), lambda step, at: (step, 0, 0))
    kept = [] if before is None else list(before)
    return pl.pallas_call(
        functools.partial(expert_kernel, sub=sub),
        grid_spec=pltpu.PrefetchScalarGridSpec(
            num_scalar_prefetch=1,
            grid=(sources // group,),
            in_specs=[narrow, wide, lanes, whole(weights_in.shape), whole(router_wide.shape)]
            + [pl.BlockSpec(memory_space=pl.ANY)] * len(kept),
            out_specs=[narrow, wide, wide, lanes],
        ),
        out_shape=[
            jax.ShapeDtypeStruct(rows.shape, jnp.bfloat16),
            jax.ShapeDtypeStruct(act_grads.shape, jnp.bfloat16),
            jax.ShapeDtypeStruct(act_grads.shape, jnp.bfloat16),
            jax.ShapeDtypeStruct(hot_gap.shape, jnp.bfloat16),
        ],
        input_output_aliases={6 + index: 1 + index for index in range(len(kept))},
        compiler_params=pltpu.CompilerParams(vmem_limit_bytes=VMEM_LIMIT),
        cost_estimate=pl.CostEstimate(
            flops=4 * sources * slots * width * shards * hidden,
            bytes_accessed=6 * sources * slots * shards * hidden,
            transcendentals=sources * slots * shards * hidden,
        ),
        name="expert_middle",
    )(place, rows, act_grads, hot_gap, weights_in, router_wide, *kept)


def act_grads_kernel(place_ref, rows_ref, weights_ref, out_ref):
    shards = weights_ref.shape[0]
    rows = rows_ref[...].reshape(-1, rows_ref.shape[2])
    for shard in range(shards):
        out_ref[shard] = mul(rows, weights_ref[shard_at(place_ref, shard, shards)], 1, 1).astype(
            jnp.bfloat16
        )


def slot_group(sources, capacity):
    return min(sources, max(1, BLOCK // capacity))


def act_grads_of(place, landed, weights, capacity):
    sources, _, width = landed.shape
    shards, hidden, _ = weights.shape
    group = slot_group(sources, capacity)
    tile = group * capacity
    return pl.pallas_call(
        act_grads_kernel,
        grid_spec=pltpu.PrefetchScalarGridSpec(
            num_scalar_prefetch=1,
            grid=(sources // group,),
            in_specs=[
                pl.BlockSpec((group, capacity, width), lambda step, at: (step, 0, 0)),
                whole(weights.shape),
            ],
            out_specs=pl.BlockSpec((shards, tile, hidden), lambda step, at: (0, step, 0)),
        ),
        out_shape=jax.ShapeDtypeStruct((shards, sources * capacity, hidden), jnp.bfloat16),
        compiler_params=pltpu.CompilerParams(vmem_limit_bytes=VMEM_LIMIT),
        cost_estimate=pl.CostEstimate(
            flops=2 * sources * capacity * width * shards * hidden,
            bytes_accessed=2 * sources * capacity * shards * hidden,
            transcendentals=0,
        ),
        name="act_grads",
    )(place, landed, weights)


def result_kernel(place_ref, act_ref, weights_ref, out_ref):
    shards = weights_ref.shape[0]
    total = mul(act_ref[0], weights_ref[shard_at(place_ref, 0, shards)], 1, 0)
    for shard in range(1, shards):
        total += mul(act_ref[shard], weights_ref[shard_at(place_ref, shard, shards)], 1, 0)
    out_ref[...] = total.astype(jnp.bfloat16)


def result_of(place, act, weights):
    shards, rows, hidden = act.shape
    width = weights.shape[2]
    return pl.pallas_call(
        result_kernel,
        grid_spec=pltpu.PrefetchScalarGridSpec(
            num_scalar_prefetch=1,
            grid=(rows // BLOCK,),
            in_specs=[
                pl.BlockSpec((shards, BLOCK, hidden), lambda step, at: (0, step, 0)),
                whole(weights.shape),
            ],
            out_specs=pl.BlockSpec((BLOCK, width), lambda step, at: (step, 0)),
        ),
        out_shape=jax.ShapeDtypeStruct((rows, width), jnp.bfloat16),
        compiler_params=pltpu.CompilerParams(vmem_limit_bytes=VMEM_LIMIT),
        cost_estimate=pl.CostEstimate(flops=0, bytes_accessed=0, transcendentals=0),
        name="expert_result",
    )(place, act, weights)


def store_half(value, send_ref, keep_ref):
    half = pl.num_programs(0) // 2

    @pl.when(pl.program_id(0) < half)
    def _():
        send_ref[0] = value

    @pl.when(pl.program_id(0) >= half)
    def _():
        keep_ref[0] = value


def half_specs(shards, rows, columns):
    half = shards // 2
    shape = jax.ShapeDtypeStruct((half, rows, columns), jnp.bfloat16)
    specs = [
        pl.BlockSpec((1, rows, columns), lambda step: (jnp.minimum(step, half - 1), 0, 0)),
        pl.BlockSpec((1, rows, columns), lambda step: (jnp.maximum(step - half, 0), 0, 0)),
    ]
    return specs, [shape, shape]


def send_first(step, shards):
    return (step + shards // 2) % shards


def out_weights_kernel(act_ref, landed_ref, send_ref, keep_ref):
    capacity = act_ref.shape[1] // landed_ref.shape[0]
    rows = landed_ref[:, :capacity].reshape(act_ref.shape[1], landed_ref.shape[2])
    store_half(mul(act_ref[0], rows, 0, 0).astype(jnp.bfloat16), send_ref, keep_ref)


def out_weights_of(act, landed):
    shards, rows, hidden = act.shape
    width = landed.shape[2]
    specs, shapes = half_specs(shards, hidden, width)
    return pl.pallas_call(
        out_weights_kernel,
        grid=(shards,),
        in_specs=[
            pl.BlockSpec((1, rows, hidden), lambda step: (send_first(step, shards), 0, 0)),
            whole(landed.shape),
        ],
        out_specs=specs,
        out_shape=shapes,
        compiler_params=pltpu.CompilerParams(vmem_limit_bytes=VMEM_LIMIT),
        cost_estimate=pl.CostEstimate(flops=0, bytes_accessed=0, transcendentals=0),
        name="out_weights",
    )(act, landed)


def in_weights_kernel(
    first_ref, last_ref, grads_ref, logits_ref, send_ref, keep_ref, router_ref
):
    sources, slots, width = first_ref.shape
    first = first_ref[...].reshape(sources * slots, width)
    last = last_ref[...].reshape(sources * slots, width)
    hidden = grads_ref.shape[4]
    total = mul(first, grads_ref[0, :, 0].reshape(sources * slots, hidden), 0, 0) + mul(
        last, grads_ref[0, :, 1].reshape(sources * slots, hidden), 0, 0
    )
    store_half(total.astype(jnp.bfloat16), send_ref, keep_ref)

    @pl.when(pl.program_id(0) == 0)
    def _():
        lanes = logits_ref.shape[3]
        router_ref[...] = mul(
            first, logits_ref[:, 0].reshape(sources * slots, lanes), 0, 0
        ) + mul(last, logits_ref[:, 1].reshape(sources * slots, lanes), 0, 0)


def in_weights_of(first, last, grads, logit_grads):
    shards, sources, _, slots, hidden = grads.shape
    width = first.shape[2]
    lanes = logit_grads.shape[3]
    specs, shapes = half_specs(shards, width, hidden)
    return pl.pallas_call(
        in_weights_kernel,
        grid=(shards,),
        in_specs=[
            whole(first.shape),
            whole(last.shape),
            pl.BlockSpec(
                (1,) + grads.shape[1:], lambda step: (send_first(step, shards), 0, 0, 0, 0)
            ),
            whole(logit_grads.shape),
        ],
        out_specs=specs + [whole((width, lanes))],
        out_shape=shapes + [jax.ShapeDtypeStruct((width, lanes), jnp.float32)],
        compiler_params=pltpu.CompilerParams(vmem_limit_bytes=VMEM_LIMIT),
        cost_estimate=pl.CostEstimate(flops=0, bytes_accessed=0, transcendentals=0),
        name="in_weights",
    )(first, last, grads, logit_grads)


def place_kernel(routes_ref, grad_ref, slots_ref, index_ref, *, capacity, spare):
    expert = pl.program_id(0)
    experts = pl.num_programs(0)
    tokens = routes_ref.shape[1]
    lanes = lax.broadcasted_iota(jnp.int32, (LANES, tokens), 0)
    hot = [(routes_ref[choice : choice + 1, :] == lanes) for choice in range(2)]

    @pl.when(expert == 0)
    def _():
        counts = (hot[0] | hot[1]).astype(jnp.bfloat16)
        earlier = (
            lax.broadcasted_iota(jnp.int32, (tokens, tokens), 0)
            < lax.broadcasted_iota(jnp.int32, (tokens, tokens), 1)
        ).astype(jnp.bfloat16)
        before = mul(counts, earlier, 1, 0)
        for choice in range(2):
            rank = jnp.sum(jnp.where(hot[choice], before, 0.0), axis=0, keepdims=True)
            index_ref[choice : choice + 1, :] = (
                routes_ref[choice : choice + 1, :] * capacity + rank.astype(jnp.int32)
            )

    slot = lax.broadcasted_iota(jnp.int32, (capacity, tokens), 0) + expert * capacity
    named = [(index_ref[choice : choice + 1, :] == slot) for choice in range(2)]
    spread = (named[0] | named[1]).astype(jnp.bfloat16)
    slots_ref[0, :capacity] = mul(spread, grad_ref[...], 1, 0).astype(jnp.bfloat16)
    others = [
        jnp.broadcast_to(routes_ref[1 - choice : 2 - choice, :] + 1, (spare, tokens))
        .astype(jnp.float32)
        .astype(jnp.bfloat16)
        for choice in range(2)
    ]
    ids = mul(others[0], named[0].astype(jnp.bfloat16), 1, 1) + mul(
        others[1], named[1].astype(jnp.bfloat16), 1, 1
    )
    width = slots_ref.shape[2]
    padded = jnp.concatenate([ids, jnp.zeros((spare, width - capacity), jnp.float32)], axis=1)
    slots_ref[0, capacity:] = padded.astype(jnp.bfloat16)


def place_rows(routes, out_grad, experts, capacity):
    tokens, width = out_grad.shape
    return pl.pallas_call(
        functools.partial(place_kernel, capacity=capacity, spare=SPARE),
        grid=(experts,),
        in_specs=[whole((2, tokens)), whole((tokens, width))],
        out_specs=[
            pl.BlockSpec((1, capacity + SPARE, width), lambda step: (step, 0, 0)),
            whole((8, tokens)),
        ],
        out_shape=[
            jax.ShapeDtypeStruct((experts, capacity + SPARE, width), jnp.bfloat16),
            jax.ShapeDtypeStruct((8, tokens), jnp.int32),
        ],
        compiler_params=pltpu.CompilerParams(vmem_limit_bytes=VMEM_LIMIT),
        cost_estimate=pl.CostEstimate(
            flops=2 * experts * capacity * tokens * width,
            bytes_accessed=2 * experts * capacity * width,
            transcendentals=0,
        ),
        name="place_rows",
    )(routes.T, out_grad)


def combine_kernel(
    first_ref, first_rows_ref, last_ref, last_rows_ref, resid_ref, gain_ref, grad_ref,
    out_ref, sharp_ref, gain_grad_ref,
):
    grad_hidden = mul(first_ref[...], first_rows_ref[...], 1, 0) + mul(
        last_ref[...], last_rows_ref[...], 1, 0
    )
    resid = resid_ref[...]
    inverse = lax.rsqrt(jnp.mean(resid * resid, axis=-1, keepdims=True) + EPSILON)
    normed = resid * inverse

    @pl.when(pl.program_id(0) == 0)
    def _():
        gain_grad_ref[...] = jnp.zeros_like(gain_grad_ref)

    rows, width = resid.shape
    gain_grad_ref[...] += jnp.sum((grad_hidden * normed).reshape(rows // 8, 8, width), axis=0)
    gained = grad_hidden * gain_ref[...]
    total = grad_ref[...].astype(jnp.float32) + inverse * (
        gained - normed * jnp.mean(gained * normed, axis=-1, keepdims=True)
    )
    out_ref[...] = total
    sharp_ref[...] = total.astype(jnp.bfloat16)


def combine(first, first_rows, last, last_rows, resid, gain, out_grad):
    rows, width = resid.shape
    slots = first_rows.shape[0]
    tile = pl.BlockSpec((HALF, width), lambda step: (step, 0))
    named = pl.BlockSpec((HALF, slots), lambda step: (step, 0))
    total, sharp, gain_grad = pl.pallas_call(
        combine_kernel,
        grid=(rows // HALF,),
        in_specs=[
            named, whole((slots, width)), named, whole((slots, width)), tile, whole((1, width)), tile,
        ],
        out_specs=[tile, tile, whole((8, width))],
        out_shape=[
            jax.ShapeDtypeStruct((rows, width), jnp.float32),
            jax.ShapeDtypeStruct((rows, width), jnp.bfloat16),
            jax.ShapeDtypeStruct((8, width), jnp.float32),
        ],
        compiler_params=pltpu.CompilerParams(vmem_limit_bytes=VMEM_LIMIT),
        cost_estimate=pl.CostEstimate(
            flops=4 * rows * slots * width,
            bytes_accessed=4 * slots * width + 12 * rows * width,
            transcendentals=rows,
        ),
        name="combine",
    )(first, first_rows, last, last_rows, resid, gain[None, :], out_grad)
    return total, sharp, gain_grad


def rms_norm(values, gain):
    return values * lax.rsqrt(jnp.mean(values * values, axis=-1, keepdims=True) + EPSILON) * gain


def exchange(pieces):
    return lax.all_to_all(pieces, "expert", split_axis=0, concat_axis=0, tiled=True)


def halved(pieces, axis_name, bit):
    half = pieces.shape[0] // 2
    return pieces[:half], swap(pieces[half:].astype(jnp.bfloat16), axis_name, bit)


def joined(keep, got):
    return keep.astype(jnp.float32) + got.astype(jnp.float32)


def joined_low(keep, got):
    return joined(keep, got).astype(jnp.bfloat16)


def spread_sum(pieces, axis_name):
    for bit in range(bit_count(axis_name)):
        pieces = joined(*halved(pieces, axis_name, bit))
    return pieces[0]


def spread_rest(pieces, axis_name):
    for bit in range(1, bit_count(axis_name)):
        pieces = joined(*halved(pieces, axis_name, bit))
    return pieces[0]


def collect(piece, axis_name):
    pieces = piece[None]
    for bit in reversed(range(1, bit_count(axis_name))):
        pieces = jnp.concatenate([pieces, swap(pieces, axis_name, bit)], axis=0)
    return pieces


def swap(value, axis_name, bit):
    count = lax.axis_size(axis_name)
    return lax.ppermute(value, axis_name, [(i, i ^ (1 << bit)) for i in range(count)])


def own_bit(axis_name, bit):
    return (lax.axis_index(axis_name) >> bit) & 1


def bit_groups(axis_name):
    bits = list(range(bit_count(axis_name)))
    return [tuple(bits[:1])] + [tuple(bits[low : low + 2]) for low in range(1, len(bits), 2)]


def send_over(value, axis_name, group, offset):
    mask = sum(((offset >> place) & 1) << bit for place, bit in enumerate(group))
    count = lax.axis_size(axis_name)
    return lax.ppermute(value, axis_name, [(i, i ^ mask) for i in range(count)])


def group_sum(value, axis_name):
    for group in bit_groups(axis_name):
        parts = [send_over(value, axis_name, group, m) for m in range(1, 2 ** len(group))]
        value = sum(parts, value)
    return value


def scatter_sum(pieces, axis_name, order):
    bits = list(range(bit_count(axis_name)))[::-1]
    total = pieces.reshape((2,) * len(bits) + pieces.shape[1:])
    for group in order:
        parts = []
        for offset in range(2 ** len(group)):
            part, left = total, list(bits)
            for place, bit in enumerate(group):
                dim = left.index(bit)
                left.remove(bit)
                index = own_bit(axis_name, bit) ^ ((offset >> place) & 1)
                part = lax.dynamic_index_in_dim(part, index, dim, keepdims=False)
            if offset:
                part = send_over(part.astype(jnp.bfloat16), axis_name, group, offset)
            parts.append(part.astype(jnp.float32))
        total = sum(parts[1:], parts[0])
        bits = left
    return total


def gather(value, axis_name, order, done=()):
    bits = list(done)
    for group in order:
        value = value.reshape((2,) * len(bits) + value.shape[value.ndim - 2 :])
        size = 2 ** len(group)
        parts = [value] + [send_over(value, axis_name, group, m) for m in range(1, size)]
        for place, bit in enumerate(group):
            flip = own_bit(axis_name, bit) == 1
            parts = [jnp.where(flip, parts[m ^ (1 << place)], parts[m]) for m in range(size)]
        stacked = jnp.stack(parts).reshape((2,) * len(group) + value.shape)
        now = sorted(group, reverse=True) + bits
        bits = sorted(now, reverse=True)
        order_of = [now.index(bit) for bit in bits]
        value = stacked.transpose(order_of + list(range(len(bits), stacked.ndim)))
    return value


def bit_count(axis_name):
    return (lax.axis_size(axis_name) - 1).bit_length()


def scatter_rows(rows, axis_name):
    groups = bit_groups(axis_name)
    parts = lax.axis_size(axis_name)
    middle = rows.shape[0] // EXTRA // 2 * EXTRA
    orders = [groups[turn:] + groups[:turn] for turn in (0, 1)]
    owned = [
        scatter_sum(half.reshape((parts, -1) + rows.shape[1:]), axis_name, order).astype(
            jnp.bfloat16
        )
        for half, order in zip((rows[:middle], rows[middle:]), orders)
    ]
    return owned, orders


def gather_rows(begun, orders, axis_name):
    halves = []
    for part, order in zip(begun, orders):
        done = sorted(order[-1], reverse=True)
        halves.append(gather(part, axis_name, order[::-1][1:], done))
    return jnp.concatenate([half.reshape(-1, half.shape[-1]) for half in halves], axis=0)


def local(
    tokens,
    lengths,
    routes,
    norm1_gain,
    attn_qkv,
    attn_out,
    rel_bias,
    norm2_gain,
    router,
    expert_in,
    expert_out,
    out_grad,
):
    n_tensor = lax.axis_size("tensor")
    tensor_index = lax.axis_index("tensor")
    width = tokens.shape[1]
    own_rows = routes.shape[0]
    inner = attn_out.shape[0]
    head_count, bucket_count = rel_bias.shape
    expert_count = router.shape[1]
    capacity = max(2, 4 * own_rows // expert_count)

    expert_index = lax.axis_index("expert")
    grad_slots, slot_index = place_rows(routes, out_grad, expert_count, capacity)
    slot_index = slot_index[:2].T
    half_slots = capacity // 2

    def named(slot_ids):
        match = slot_index[:, :, None] == slot_ids[None, None, :]
        return (match[:, 0] | match[:, 1]).astype(jnp.bfloat16)

    slot_ids = jnp.arange(expert_count * capacity, dtype=jnp.int32)
    split_ids = slot_ids.reshape(expert_count, 2, half_slots)
    landed = exchange(grad_slots)
    tokens, _ = lax.optimization_barrier((tokens, grad_slots))
    place = tensor_index.astype(jnp.int32)[None]
    halves = [named(split_ids[:, which].reshape(-1)) for which in range(2)]
    dispatch = named(slot_ids)

    qkv_flat = attn_qkv.transpose(1, 2, 0).reshape(3 * inner, width)
    branch, projected, mixed, log_total = attend(
        place, tokens, lengths, norm1_gain, qkv_flat, attn_out, rel_bias
    )
    branch = spread_sum(branch.reshape(n_tensor, own_rows, width), "tensor")
    own_tokens = lax.dynamic_slice_in_dim(tokens, tensor_index * own_rows, own_rows, 0)
    resid = own_tokens.astype(jnp.float32) + branch
    hidden_two = rms_norm(resid, norm2_gain).astype(jnp.bfloat16)
    outgoing = [mul(half, hidden_two, 0, 0).astype(jnp.bfloat16) for half in halves]
    outgoing, landed, expert_in = lax.optimization_barrier((outgoing, landed, expert_in))
    outgoing = [rows.reshape(expert_count, half_slots, width) for rows in outgoing]
    first_rows = exchange(outgoing[0])
    other_here = landed[:, capacity, :capacity].reshape(-1).astype(jnp.int32)
    weights_out = lax.all_gather(expert_out[0], "tensor")
    weights_in = lax.all_gather(expert_in[0], "tensor")
    act_grads = act_grads_of(place, landed, weights_out, capacity)
    shards, _, hidden = act_grads.shape
    act_grads = act_grads.reshape(shards, expert_count, 2, half_slots, hidden)
    lanes = jnp.arange(LANES, dtype=jnp.int32)
    hot_gap = (
        (lanes == expert_index).astype(jnp.int32)[None, :]
        - (other_here[:, None] == lanes[None, :] + 1).astype(jnp.int32)
    ).astype(jnp.bfloat16)
    hot_gap = hot_gap.reshape(expert_count, 2, half_slots, LANES)
    router_wide = jnp.pad(router, ((0, 0), (0, LANES - expert_count)))
    first_rows, act_grads, hot_gap, weights_in, last, dispatch, halves = lax.optimization_barrier(
        (first_rows, act_grads, hot_gap, weights_in, outgoing[1], dispatch, halves)
    )
    last_rows = exchange(last)
    sent_one, *kept = serve(place, first_rows, act_grads, hot_gap, weights_in, router_wide, 0, None)
    grad_sent_one = exchange(sent_one)
    sent_two, act, grad_pre, logit_grads = serve(
        place, last_rows, act_grads, hot_gap, weights_in, router_wide, 1, kept
    )
    act = act.reshape(shards, -1, hidden)
    out_send, out_keep = out_weights_of(act, landed)
    sent_two, out_send, out_keep, grad_pre = lax.optimization_barrier(
        (sent_two, out_send, out_keep, grad_pre)
    )
    grad_sent_two = exchange(sent_two)
    out_half = joined_low(out_keep, swap(out_send, "tensor", 0))
    out_half, grad_pre = lax.optimization_barrier((out_half, grad_pre))
    for bit in range(1, bit_count("tensor") - 1):
        out_half = joined_low(*halved(out_half, "tensor", bit))
    out_half, out_got = halved(out_half, "tensor", bit_count("tensor") - 1)
    in_send, in_keep, router_part = in_weights_of(first_rows, last_rows, grad_pre, logit_grads)
    router_part = router_part[:, :expert_count]
    count = 2 + expert_count
    extra = -(-(count + 1) // EXTRA) * EXTRA - count - 1
    blank = jnp.zeros((1, width), jnp.float32)
    small = jnp.concatenate(
        [blank, blank, blank, router_part.T, jnp.zeros((extra, width), jnp.float32)], axis=0
    )
    act, in_send, in_keep, small = lax.optimization_barrier((act, in_send, in_keep, small))
    in_got = swap(in_send, "tensor", 0)
    result = result_of(place, act, weights_out)
    grad_sent_one, grad_sent_two, result, out_half, out_got = lax.optimization_barrier(
        (grad_sent_one, grad_sent_two, result, out_half, out_got)
    )
    grad_resid, grad_sharp, gain_two_part = combine(
        halves[0],
        grad_sent_one.reshape(-1, width),
        halves[1],
        grad_sent_two.reshape(-1, width),
        resid,
        norm2_gain,
        out_grad,
    )
    came_back = exchange(result.reshape(expert_count, capacity, width)).reshape(-1, width)
    tensor_bits = bit_count("tensor")
    grad_w_in = joined_low(in_keep, in_got)
    for bit in range(1, tensor_bits - 1):
        grad_w_in = joined_low(*halved(grad_w_in, "tensor", bit))
    near_grad = collect(grad_sharp, "tensor")
    near_grad, grad_w_in = lax.optimization_barrier((near_grad, grad_w_in))
    away_grad = swap(near_grad, "tensor", 0)
    grad_w_in, grad_w_in_got = halved(grad_w_in, "tensor", tensor_bits - 1)

    tokens_part, weights_part = attend_back(
        place, tokens, lengths, norm1_gain, qkv_flat, attn_out, rel_bias,
        projected, mixed, log_total, near_grad, away_grad, small, gain_two_part,
    )
    tokens_part, weights_part, came_back, grad_w_in_got = lax.optimization_barrier(
        (tokens_part, weights_part, came_back, grad_w_in_got)
    )
    tokens_shared = lax.psum_scatter(tokens_part, "tensor", scatter_dimension=0, tiled=True)
    owned, orders = scatter_rows(weights_part, "expert")
    owned, grad_w_in, out_half = lax.optimization_barrier((owned, grad_w_in, out_half))
    grad_w_in = joined(grad_w_in, grad_w_in_got)
    grad_w_out = joined(out_half, out_got)
    begun = [gather(own, "expert", order[::-1][:1]) for own, order in zip(owned, orders)]
    begun, came_back, grad_w_in, tokens_shared, grad_w_out = lax.optimization_barrier(
        (begun, came_back, grad_w_in, tokens_shared, grad_w_out)
    )
    weights_total = gather_rows(begun, orders, "expert").astype(jnp.float32)
    output = resid + jnp.dot(dispatch, came_back, preferred_element_type=jnp.float32)
    grad_tokens = grad_resid + tokens_shared.astype(jnp.float32)
    low = 4 * inner
    bias_total = weights_total[low + 1, : rel_bias.size].reshape(rel_bias.shape)
    small = weights_total[low : low + count + 1]
    small = group_sum(jnp.concatenate([small[:1], small[2:]], axis=0), "tensor")
    columns = lax.dynamic_slice_in_dim(
        small, tensor_index * (width // n_tensor), width // n_tensor, 1
    )
    return (
        output,
        grad_tokens,
        columns[0],
        weights_total[: 3 * inner].reshape(3, inner, width).transpose(2, 0, 1),
        weights_total[3 * inner : 4 * inner],
        bias_total,
        columns[1],
        columns[2:].T,
        grad_w_in,
        grad_w_out,
    )


def solution(mesh):
    return jax.shard_map(
        local,
        mesh=mesh,
        in_specs=(
            P("expert", None),
            P("expert", None),
            P(("expert", "tensor"), None),
            P(),
            P(None, None, "tensor"),
            P("tensor", None),
            P("tensor", None),
            P(),
            P(),
            P("expert", None, "tensor"),
            P("expert", "tensor", None),
            P(("expert", "tensor"), None),
        ),
        out_specs=(
            P(("expert", "tensor"), None),
            P(("expert", "tensor"), None),
            P("tensor"),
            P(None, None, "tensor"),
            P("tensor", None),
            P("tensor", None),
            P("tensor"),
            P("tensor", None),
            P("expert", None, "tensor"),
            P("expert", "tensor", None),
        ),
        check_vma=False,
    )
```
